128 devices in a mesh: dp: 8 (over y, z_lo), ctx: 16 (over z_hi, x, core).
Axes of the slice: x: 4, y: 4, z: 4 (z_hi: 2, z_lo: 2; z = z_hi * 2 + z_lo), core: 2. Of those that a mesh axis runs over, the one named last changes fastest.
Arguments:
- tokens: bfloat16 [24576, 1536], P(('dp', 'ctx')), may hold values from -6 to 6
- segments: int32 [24576], P('dp'), may hold values from 0 to 4, as said below
- routes: int32 [24576, 2], P(('dp', 'ctx')), may hold values from 0 to 15, all different within a row; in each aligned block of 192 rows (0 to 191, 192 to 383, ...) at most 36 rows name the same one
- gain_attn: bfloat16 [1536], P(('dp', 'ctx')), may hold values from 0.25 to 1.75
- w_query: bfloat16 [1536, 1536], P(('dp', 'ctx')), may hold values from -0.21875 to 0.21875
- key_weight: bfloat16 [1536, 512], P(('dp', 'ctx')), may hold values from -0.15625 to 0.15625
- value_weight: bfloat16 [1536, 512], P(('dp', 'ctx')), may hold values from -0.15625 to 0.15625
- w_out: bfloat16 [1536, 1536], P(('dp', 'ctx')), may hold values from -1.75 to 1.75
- w_router: bfloat16 [1536, 16], P(('dp', 'ctx')), may hold values from -0.109375 to 0.109375
- gain_ffn: bfloat16 [1536], P(('dp', 'ctx')), may hold values from 0.25 to 1.75
- w_gate: bfloat16 [16, 1536, 1024], P('ctx', 'dp'), may hold values from -0.15625 to 0.15625
- w_up: bfloat16 [16, 1536, 1024], P('ctx', 'dp'), may hold values from -0.15625 to 0.15625
- w_down: bfloat16 [16, 1024, 1536], P('ctx', 'dp'), may hold values from -0.375 to 0.375
- cotangent: bfloat16 [24576, 1536], P(('dp', 'ctx')), may hold values from -24 to 24
Outputs:
- mixed: bfloat16 [24576, 1536], P(('dp', 'ctx'))
- grad_input: bfloat16 [24576, 1536], P(('dp', 'ctx'))
- grad_gain_attn: float32 [1536], P(('dp', 'ctx'))
- grad_query: float32 [1536, 1536], P(('dp', 'ctx'))
- grad_key: float32 [1536, 512], P(('dp', 'ctx'))
- grad_value: float32 [1536, 512], P(('dp', 'ctx'))
- grad_out_proj: float32 [1536, 1536], P(('dp', 'ctx'))
- grad_router: float32 [1536, 16], P(('dp', 'ctx'))
- grad_gain_ffn: float32 [1536], P(('dp', 'ctx'))
- grad_gate: float32 [16, 1536, 1024], P('ctx', 'dp')
- grad_up: float32 [16, 1536, 1024], P('ctx', 'dp')
- grad_down: float32 [16, 1024, 1536], P('ctx', 'dp')
The draws below stay inside these ranges and needn't reach their ends.
Inputs may be any that keep to these rules, and one draw needn't show every extreme that they name: `segments`: within each sequence of 3072 tokens (one per index of dp) the ids never fall and each id marks one document; every sequence packs five documents, the first two and last two of them of at least 204 tokens each, and the middle one of 1728 to 1920 tokens. `routes`: each row names 2 different experts; among the rows of one device no expert is named by more than 36 rows, a bound that some block reaches.
All inputs are finite; a program needn't handle non-finite values.
Results may differ from the reference program's by a relative error of at most 0.018.
Values may be sent and summed in bfloat16 or wider, within the bound.
A program may use at most 192 MiB of HBM per device.

```python
import math
import jax
import jax.numpy as jnp
import numpy as np
from jax import lax

MODEL_WIDTH = 1536
QUERY_HEAD_COUNT = 24
KEY_VALUE_HEADS = 8
HEAD_SIZE = 64
FF = 1024
TOP = 2
TOK_DEV = 192
EXPERTS = 16
SEQ_LEN = 3072
TOKENS = 24576
CAP = 36


def draw_segments(key, part):
    key = jax.random.fold_in(key, 7)
    sequences = TOKENS // SEQ_LEN
    shortest = max(1, SEQ_LEN // 15)
    long_lo = SEQ_LEN // 2 + TOK_DEV
    long_hi = SEQ_LEN * 5 // 8
    first_key, second_key, third_key, fourth_key = jax.random.split(key, 4)
    long_len = jax.random.randint(first_key, (sequences, 1), long_lo, long_hi + 1)
    start = 2 * shortest + jax.random.randint(second_key, (sequences, 1), 0, SEQ_LEN - long_len - 4 * shortest + 1)
    finish = start + long_len
    front_cut = jax.random.randint(third_key, (sequences, 1), shortest, start - shortest + 1)
    back_cut = finish + jax.random.randint(fourth_key, (sequences, 1), shortest, SEQ_LEN - finish - shortest + 1)
    positions = jnp.arange(SEQ_LEN, dtype=jnp.int32)[None, :]
    seg_ids = (positions >= front_cut).astype(jnp.int32) + (positions >= start).astype(jnp.int32) + (positions >= finish).astype(jnp.int32) + (positions >= back_cut).astype(jnp.int32)
    return seg_ids.reshape(-1).astype(jnp.int32)


def with_spikes(array, rng, source, target, parts, factor):
    owner, partner = [(jnp.arange(array.shape[position]) // (array.shape[position] // parts)).reshape([-1 if axis == position else 1 for axis in range(array.ndim)]) for position in (source, target)]
    chosen = jax.random.permutation(rng, parts)[partner]
    strong = (owner == chosen) | (owner == (partner + parts // 2) % parts)
    return jnp.where(strong, factor * array, array)


def level_of(own_key, extent, cuts, least, top_value):
    def one(position, shards_of):
        draws = jax.random.uniform(jax.random.fold_in(jax.random.fold_in(own_key, 6), position), (shards_of,), jnp.float32, least / len(cuts), top_value / len(cuts))
        return jnp.repeat(jnp.exp(draws), extent[position] // shards_of).reshape((-1,) + (1,) * (len(extent) - position - 1))

    level = one(*cuts[0])
    for cut in cuts[1:]:
        level = level * one(*cut)
    return level


def routed_block(key, own, number, rows, amount, top, most, skew):
    sequence = jax.random.permutation(key, amount)
    crowded, usual = portions_of(amount, rows * top, most, skew, True), portions_of(amount, rows * top, most, skew, False)
    places = jnp.arange(amount)

    def named(sizes, offset_by):
        used = int((sizes > 0).sum())
        fixed = max(1, used // 4)
        shifted = fixed + (places - fixed + offset_by * (used - fixed)) % max(1, amount - fixed)
        return jnp.zeros((amount,), jnp.int32).at[sequence[jnp.where(places < fixed, places, shifted)]].set(jnp.asarray(sizes, jnp.int32))

    sizes = jnp.where(number % 4 == 0, named(crowded, number // 4), named(usual, number - number // 4 - 1))
    mixed = jax.random.permutation(jax.random.fold_in(own, 3), amount)
    donor, sink = mixed[0:amount // 2 * 2:2], mixed[1:amount // 2 * 2:2]
    margin = jnp.minimum(sizes[donor] - 1, most - sizes[sink]) // 2
    margin = jnp.where((donor == sequence[0]) | (sink == sequence[0]) | (sizes[sink] == 0), 0, jnp.maximum(margin, 0))
    shifted = jax.random.randint(jax.random.fold_in(own, 4), (amount // 2,), 0, 1 << 20) % (margin + 1)
    sizes = sizes.at[donor].add(-shifted).at[sink].add(shifted)
    items = jnp.searchsorted(jnp.cumsum(sizes), jnp.arange(rows * top), side="right").astype(jnp.int32)
    table = items.reshape(top, rows).T
    table = table[jax.random.permutation(jax.random.fold_in(own, 1), rows)]
    offset_by = jax.random.randint(jax.random.fold_in(own, 2), (rows, 1), 0, top)
    return jnp.take_along_axis(table, (jnp.arange(top)[None, :] + offset_by) % top, axis=1)


def portions_of(count, total, reach, lean, full):
    portions = [(1 << 20) // math.isqrt(grade ** lean) + 1 for grade in range(1, count + 1)]
    largest = reach if full else min(reach, max(-(-total // count), total * portions[0] // sum(portions)))
    least = 1 if total - largest >= count - 1 else 0
    counts, rest = [largest] + [least] * (count - 1), total - largest - least * (count - 1)
    while rest > 0:
        candidates = [i for i in range(1, count) if counts[i] < largest] or [i for i in range(1, count) if counts[i] < reach]
        mass, left = sum([portions[i] for i in candidates]), rest
        for i in candidates:
            addition = min(reach - counts[i], max(1, left * portions[i] // mass), rest)
            counts[i] = counts[i] + addition
            rest = rest - addition
    return np.array(counts)


def scatter_about(stream_key, shape, scale, limit, pieces=(), kind=jnp.bfloat16):
    values = jax.random.normal(stream_key, shape, jnp.float32) * scale
    if len(pieces) > 0:
        values = level_of(stream_key, shape, pieces, -0.22, 0.18) * values
    return jnp.clip(values, min=-limit, max=limit).astype(kind)


def gaussian_with(stream_key, shape, deviation, limit, pieces, heavy, kind=jnp.bfloat16):
    drawn = deviation * jax.random.normal(stream_key, shape, jnp.float32)
    if pieces:
        drawn = drawn * level_of(stream_key, shape, pieces, -0.22, 0.18)
    return jnp.clip(with_spikes(drawn, jax.random.fold_in(stream_key, 3), *heavy), -limit, limit).astype(kind)


def setup_inputs(seed: int = 0) -> dict:
    splits = jax.random.split(jax.random.key(seed), 15)
    tokens = scatter_about(splits[0], (TOKENS, MODEL_WIDTH), 1.0, 6.0, ((0, 128),))
    segments = draw_segments(jax.random.fold_in(splits[14], 71), 0)
    routes_keys = jax.random.split(jax.random.fold_in(splits[2], 1), TOKENS // TOK_DEV)
    routes_turns = jax.random.permutation(jax.random.fold_in(splits[2], 3), TOKENS // TOK_DEV)
    routes = jax.vmap(lambda own, number: routed_block(jax.random.fold_in(splits[2], 2), own, number, TOK_DEV, EXPERTS, TOP, CAP, 1))(routes_keys, routes_turns).reshape((TOKENS, TOP))
    gain_attn = jnp.clip(1.0 + 0.15 * jax.random.normal(splits[3], (MODEL_WIDTH,), jnp.float32), 0.25, 1.75).astype(jnp.bfloat16)
    w_query = scatter_about(splits[4], (MODEL_WIDTH, QUERY_HEAD_COUNT * HEAD_SIZE), (MODEL_WIDTH // 2) ** -0.5, 0.21875, ((0, 128),))
    key_weight = scatter_about(splits[5], (MODEL_WIDTH, KEY_VALUE_HEADS * HEAD_SIZE), MODEL_WIDTH ** -0.5, 0.15625, ((0, 128),))
    value_weight = scatter_about(splits[6], (MODEL_WIDTH, KEY_VALUE_HEADS * HEAD_SIZE), MODEL_WIDTH ** -0.5, 0.15625, ((0, 128),))
    w_out = scatter_about(splits[7], (MODEL_WIDTH, QUERY_HEAD_COUNT * HEAD_SIZE), (max(1, MODEL_WIDTH // 128)) ** -0.5, 1.75, ((0, 128),))
    w_router = scatter_about(splits[8], (MODEL_WIDTH, EXPERTS), (2 * MODEL_WIDTH) ** -0.5, 0.109375, ((0, 128),))
    gain_ffn = jnp.clip(1.0 + 0.15 * jax.random.normal(splits[9], (MODEL_WIDTH,), jnp.float32), 0.25, 1.75).astype(jnp.bfloat16)
    w_gate = scatter_about(splits[10], (EXPERTS, MODEL_WIDTH, FF), MODEL_WIDTH ** -0.5, 0.15625, ((0, 16), (1, 8)))
    w_up = scatter_about(splits[11], (EXPERTS, MODEL_WIDTH, FF), MODEL_WIDTH ** -0.5, 0.15625, ((0, 16), (1, 8)))
    w_down = scatter_about(splits[12], (EXPERTS, FF, MODEL_WIDTH), (FF // 4) ** -0.5, 0.375, ((0, 16), (1, 8)))
    cotangent = gaussian_with(splits[13], (TOKENS, MODEL_WIDTH), 1.0, 24.0, ((0, 128),), (0, 1, 128, 5.5))
    return {"tokens": tokens, "segments": segments, "routes": routes, "gain_attn": gain_attn, "w_query": w_query, "key_weight": key_weight, "value_weight": value_weight, "w_out": w_out, "w_router": w_router, "gain_ffn": gain_ffn, "w_gate": w_gate, "w_up": w_up, "w_down": w_down, "cotangent": cotangent}


EPSILON = 1e-06
NEGATIVE = -1e+30
PRECISE = lax.Precision.HIGHEST

@jax.custom_vjp
def low(v):
    return lax.optimization_barrier(v.astype(jnp.bfloat16)).astype(jnp.float32)

@jax.custom_vjp
def low_back(v):
    return v

def low_keep(v):
    return (low(v), None)

def low_pass(kept, grad):
    return (grad,)

def back_keep(v):
    return (v, None)

def back_low(kept, grad):
    return (low(grad),)
low.defvjp(low_keep, low_pass)
low_back.defvjp(back_keep, back_low)

def inverse_rms(values):
    return lax.rsqrt(lax.optimization_barrier(jnp.mean(values * values, axis=-1, keepdims=True)) + EPSILON)

def attend_block(query_block, heads_of_keys, heads_of_values, query_pos, query_seg, key_pos, key_seg):
    scores = jnp.einsum('qhgd,khd->hgqk', query_block, heads_of_keys, precision=PRECISE) * HEAD_SIZE ** (-0.5)
    scores = low_back(scores)
    allowed = (key_pos[None, :] <= query_pos[:, None]) & (key_seg[None, :] == query_seg[:, None])
    scores = jnp.where(allowed, scores, NEGATIVE)
    highest = lax.optimization_barrier(jnp.max(scores, axis=-1, keepdims=True))
    log_total = highest + jnp.log(lax.optimization_barrier(jnp.sum(jnp.exp(scores - highest), axis=-1, keepdims=True)))
    weights = jnp.exp(scores - log_total)
    return jnp.einsum('hgqk,khd->qhgd', low(weights), heads_of_values, precision=PRECISE)

def dispatch_rows(route_ids, experts):
    sequence_rows = route_ids.shape[0]
    blocks = sequence_rows // TOK_DEV
    flat_ids = route_ids.reshape(blocks, TOK_DEV * TOP)
    onehot = (flat_ids[:, :, None] == jnp.arange(experts, dtype=jnp.int32)[None, None, :]).astype(jnp.int32)
    earlier = (jnp.cumsum(onehot, axis=1) - 1).astype(jnp.int32)
    slot_ids = lax.optimization_barrier(jnp.sum(onehot * earlier, axis=-1)).astype(jnp.int32)
    block_ids = jnp.arange(blocks, dtype=jnp.int32)[:, None]
    targets = flat_ids * (blocks * CAP) + block_ids * CAP + slot_ids
    return targets.astype(jnp.int32).reshape(sequence_rows, TOP)

def sequence_block(residual, seg_ids, route_ids, params):
    gain_one, query_proj, key_proj, value_proj, out_proj, router_proj, gain_two, gate_proj, up_proj, down_proj = params
    sequence_rows = residual.shape[0]
    query_group_size = QUERY_HEAD_COUNT // KEY_VALUE_HEADS
    normed = low(residual * inverse_rms(residual) * gain_one)
    rows_of_queries = low_back(low(jnp.dot(normed, query_proj, precision=PRECISE)))
    rows_of_keys = low_back(low(jnp.dot(normed, key_proj, precision=PRECISE)))
    rows_of_values = low_back(low(jnp.dot(normed, value_proj, precision=PRECISE)))
    positions = jnp.arange(sequence_rows, dtype=jnp.int32)
    rows_per_block = math.gcd(sequence_rows, 512)
    blocks_of_queries = rows_of_queries.reshape(sequence_rows // rows_per_block, rows_per_block, KEY_VALUE_HEADS, query_group_size, HEAD_SIZE)
    heads_of_keys = rows_of_keys.reshape(sequence_rows, KEY_VALUE_HEADS, HEAD_SIZE)
    heads_of_values = rows_of_values.reshape(sequence_rows, KEY_VALUE_HEADS, HEAD_SIZE)

    def one_block(element):
        query_block, block_pos, block_seg = element
        return attend_block(query_block, heads_of_keys, heads_of_values, block_pos, block_seg, positions, seg_ids)
    attended = lax.map(jax.checkpoint(one_block), (blocks_of_queries, positions.reshape(-1, rows_per_block), seg_ids.reshape(-1, rows_per_block)))
    attended = low_back(low(attended.reshape(sequence_rows, QUERY_HEAD_COUNT * HEAD_SIZE)))
    branch = low_back(jnp.dot(attended, out_proj.T, precision=PRECISE))
    hidden_one = residual + branch
    normed_two = low(hidden_one * inverse_rms(hidden_one) * gain_two)
    logits = low_back(jnp.dot(normed_two, router_proj, precision=PRECISE))
    experts = router_proj.shape[1]
    picked = (route_ids[:, :, None] == jnp.arange(experts, dtype=jnp.int32)[None, None, :]).astype(jnp.float32)
    chosen = lax.optimization_barrier(jnp.sum(picked * logits[:, None, :], axis=-1))
    gate_weights = jax.nn.softmax(chosen, axis=-1)
    targets = dispatch_rows(route_ids, experts).reshape(-1)
    copies = low_back(jnp.broadcast_to(normed_two[:, None, :], (sequence_rows, TOP, MODEL_WIDTH)))
    buffer = jnp.zeros((experts * (sequence_rows // TOK_DEV) * CAP, MODEL_WIDTH), jnp.float32).at[targets].add(copies.reshape(-1, MODEL_WIDTH))
    expert_in = buffer.reshape(experts, -1, MODEL_WIDTH)
    gate_pre = low_back(jnp.einsum('end,edf->enf', expert_in, gate_proj, precision=PRECISE))
    up_pre = low_back(jnp.einsum('end,edf->enf', expert_in, up_proj, precision=PRECISE))
    hidden = low(jax.nn.silu(gate_pre) * up_pre)
    expert_out = low_back(low(jnp.einsum('enf,efd->end', hidden, down_proj, precision=PRECISE)))
    returned = expert_out.reshape(-1, MODEL_WIDTH)[targets].reshape(sequence_rows, TOP, MODEL_WIDTH)
    return hidden_one + lax.optimization_barrier(jnp.sum(gate_weights[:, :, None] * returned, axis=1))

def reference(tokens, segments, routes, gain_attn, w_query, key_weight, value_weight, w_out, w_router, gain_ffn, w_gate, w_up, w_down, cotangent):
    sequences = tokens.shape[0] // SEQ_LEN
    residual = tokens.astype(jnp.float32).reshape(sequences, SEQ_LEN, MODEL_WIDTH)
    seg_ids = segments.reshape(sequences, SEQ_LEN)
    route_ids = routes.reshape(sequences, SEQ_LEN, TOP)
    params = tuple((weight.astype(jnp.float32) for weight in (gain_attn, w_query, key_weight, value_weight, w_out, w_router, gain_ffn, w_gate, w_up, w_down)))

    def forward(residual_all, params_all):

        def one_sequence(unused, element):
            residual_seq, seg_seq, route_seq = element
            return (unused, sequence_block(residual_seq, seg_seq, route_seq, params_all))
        _, outputs = lax.scan(one_sequence, jnp.zeros((), jnp.float32), (residual_all, seg_ids, route_ids))
        return outputs
    outputs, pullback = jax.vjp(forward, residual, params)
    grad_residual, grad_params = pullback(cotangent.astype(jnp.float32).reshape(sequences, SEQ_LEN, MODEL_WIDTH))
    mixed = outputs.reshape(-1, MODEL_WIDTH).astype(jnp.bfloat16)
    grad_input = grad_residual.reshape(-1, MODEL_WIDTH).astype(jnp.bfloat16)
    return (mixed, grad_input, grad_params[0], grad_params[1], grad_params[2], grad_params[3], grad_params[4], grad_params[5], grad_params[6], grad_params[7], grad_params[8], grad_params[9])
```

```python
import math

import jax
import jax.numpy as jnp
from jax import lax
from jax.experimental import pallas as pl
from jax.experimental.pallas import tpu as pltpu
from jax.sharding import PartitionSpec as P

QUERY_HEAD_COUNT = 24
KEY_VALUE_HEADS = 8
HEAD_SIZE = 64
TOP = 2


EPSILON = 1e-06
NEGATIVE = -1e30


def inverse_rms(values):
    return lax.rsqrt(jnp.mean(values * values, axis=-1, keepdims=True) + EPSILON)


def norm_backward(grad_normed, values, inverse, gain):
    unit_rows = values * inverse
    grad_unit = grad_normed * gain
    grad_values = inverse * (
        grad_unit - unit_rows * jnp.mean(grad_unit * unit_rows, axis=-1, keepdims=True)
    )
    return (grad_values, jnp.sum(grad_normed * unit_rows, axis=0))


def contract_rows(left, right):
    return lax.dot_general(
        left, right, (((0,), (0,)), ((), ())), preferred_element_type=jnp.float32
    )


def contract_cols(left, right):
    return lax.dot_general(
        left, right, (((1,), (1,)), ((), ())), preferred_element_type=jnp.float32
    )


def allowed_pairs(query_pos, query_seg, block_pos, block_seg):
    return (block_pos[None, :] <= query_pos[:, None]) & (block_seg[None, :] == query_seg[:, None])


def block_scores(heads_of_queries, key_block, allowed, factor):
    scores = (
        jnp.einsum(
            "qhgd,khd->hgqk", heads_of_queries, key_block, preferred_element_type=jnp.float32
        )
        * factor
    )
    return jnp.where(allowed, scores, NEGATIVE)


def attend_forward(
    heads_of_queries, key_blocks, value_blocks, key_pos, key_seg, query_pos, query_seg, factor
):
    stat_shape = (
        heads_of_queries.shape[1],
        heads_of_queries.shape[2],
        heads_of_queries.shape[0],
        1,
    )

    def running_step(running, element):
        highest, total = running
        key_block, block_pos, block_seg = element
        scores = block_scores(
            heads_of_queries,
            key_block,
            allowed_pairs(query_pos, query_seg, block_pos, block_seg),
            factor,
        )
        new_high = jnp.maximum(highest, jnp.max(scores, axis=-1, keepdims=True))
        total = total * jnp.exp(highest - new_high) + jnp.sum(
            jnp.exp(scores - new_high), axis=-1, keepdims=True
        )
        return ((new_high, total), None)

    start_state = (jnp.full(stat_shape, NEGATIVE, jnp.float32), jnp.zeros(stat_shape, jnp.float32))
    (highest, total), _ = lax.scan(running_step, start_state, (key_blocks, key_pos, key_seg))
    log_total = highest + jnp.log(total)

    def output_step(summed, element):
        key_block, value_block, block_pos, block_seg = element
        scores = block_scores(
            heads_of_queries,
            key_block,
            allowed_pairs(query_pos, query_seg, block_pos, block_seg),
            factor,
        )
        weights = jnp.exp(scores - log_total).astype(jnp.bfloat16)
        return (
            summed
            + jnp.einsum(
                "hgqk,khd->qhgd", weights, value_block, preferred_element_type=jnp.float32
            ),
            None,
        )

    summed, _ = lax.scan(
        output_step,
        jnp.zeros(heads_of_queries.shape, jnp.float32),
        (key_blocks, value_blocks, key_pos, key_seg),
    )
    return (summed, log_total)


def attend_backward(
    heads_of_queries,
    head_gradient,
    key_blocks,
    value_blocks,
    key_pos,
    key_seg,
    query_pos,
    query_seg,
    log_total,
    factor,
):

    def probs_and_grads(key_block, value_block, block_pos, block_seg):
        scores = block_scores(
            heads_of_queries,
            key_block,
            allowed_pairs(query_pos, query_seg, block_pos, block_seg),
            factor,
        )
        probs = jnp.exp(scores - log_total)
        grad_probs = jnp.einsum(
            "qhgd,khd->hgqk", head_gradient, value_block, preferred_element_type=jnp.float32
        )
        return (probs, grad_probs)

    def delta_step(delta, element):
        probs, grad_probs = probs_and_grads(element[0], element[1], element[2], element[3])
        return (delta + jnp.sum(probs * grad_probs, axis=-1, keepdims=True), None)

    delta, _ = lax.scan(
        delta_step,
        jnp.zeros(log_total.shape, jnp.float32),
        (key_blocks, value_blocks, key_pos, key_seg),
    )

    def grad_step(grad_query_heads, element):
        key_block, value_block, block_pos, block_seg = element
        probs, grad_probs = probs_and_grads(key_block, value_block, block_pos, block_seg)
        grad_scores = (probs * (grad_probs - delta)).astype(jnp.bfloat16)
        grad_query_heads = grad_query_heads + jnp.einsum(
            "hgqk,khd->qhgd", grad_scores, key_block, preferred_element_type=jnp.float32
        )
        grad_key_block = (
            jnp.einsum(
                "hgqk,qhgd->khd", grad_scores, heads_of_queries, preferred_element_type=jnp.float32
            )
            * factor
        )
        grad_value_block = jnp.einsum(
            "hgqk,qhgd->khd",
            probs.astype(jnp.bfloat16),
            head_gradient,
            preferred_element_type=jnp.float32,
        )
        return (grad_query_heads, (grad_key_block, grad_value_block))

    grad_query_heads, (key_block_gradient, value_block_gradient) = lax.scan(
        grad_step,
        jnp.zeros(heads_of_queries.shape, jnp.float32),
        (key_blocks, value_blocks, key_pos, key_seg),
    )
    return (grad_query_heads * factor, key_block_gradient, value_block_gradient)


MESH = pl.DeviceIdType.MESH

PACK = 4608
HALF = PACK // 2
QUARTER = PACK // 4
RING_ORDERS = (("x", "y", "z"), ("y", "z", "x"), ("z", "x", "y"))


def place():
    dp = lax.axis_index("dp")
    ctx = lax.axis_index("ctx")
    return {"y": dp // 2, "z": (ctx // 8) * 2 + dp % 2, "x": (ctx // 2) % 4, "core": ctx % 2}


def device_of(spot):
    z = spot["z"]
    return (spot["y"] * 2 + z % 2, (z // 2) * 8 + spot["x"] * 2 + spot["core"])


def moved(spot, axis, step):
    other = dict(spot)
    if axis == "core":
        other["core"] = 1 - spot["core"]
    else:
        other[axis] = (spot[axis] + step) % 4
    return other


def member(spot, step):
    index = (spot["x"] % 2) * 2 + spot["core"]
    target = (index // 2 + step // 2) % 2 * 2 + (index % 2 + step % 2) % 2
    other = dict(spot)
    other["x"] = (spot["x"] // 2) * 2 + target // 2
    other["core"] = target % 2
    return other, target


def meet(spot):
    barrier = pltpu.get_barrier_semaphore()
    others = [member(spot, step)[0] for step in (1, 2, 3)]
    others += [moved(spot, axis, step) for axis in "xyz" for step in (1, 2, 3)]
    for other in others:
        pl.semaphore_signal(barrier, inc=1, device_id=device_of(other), device_id_type=MESH)
    pl.semaphore_wait(barrier, len(others))


def region(spot, known, part, base):
    def pick(axis, value, size):
        return pl.ds(0, size) if axis in known else pl.ds(value, 1)

    z = spot["z"]
    if "x" in known:
        columns = pl.ds(base, HALF)
    else:
        columns = pl.ds(pl.multiple_of(base + (spot["x"] % 2) * QUARTER, 128), QUARTER)
    return (
        pick("y", spot["y"], 4),
        pick("z", z % 2, 2),
        pick("z", z // 2, 2),
        pick("x", spot["x"] // 2, 2),
        pl.ds(part * 16, 16),
        columns,
    )


def gather_kernel(shard, merge, out, pieces, joined, send0, recv0, send, recv, send_core, recv_core, local):
    spot = place()
    meet(spot)
    index = (spot["x"] % 2) * 2 + spot["core"]
    quarter = spot["core"] * 2 + spot["x"] % 2
    copies = []
    for step in (1, 2, 3):
        other, target = member(spot, step)
        goal = other["core"] * 2 + other["x"] % 2
        copy = pltpu.make_async_remote_copy(
            src_ref=shard.at[:, pl.ds(pl.multiple_of(goal * QUARTER, 128), QUARTER)],
            dst_ref=pieces.at[index],
            send_sem=send0.at[step - 1],
            recv_sem=recv0.at[step - 1],
            device_id=device_of(other),
            device_id_type=MESH,
        )
        copy.start()
        copies.append(copy)
    pieces[index] = shard[:, pl.ds(pl.multiple_of(quarter * QUARTER, 128), QUARTER)]
    for copy in copies:
        copy.wait()
    joined[...] = jnp.dot(
        merge[...], pieces[...].reshape(64, QUARTER), preferred_element_type=jnp.float32
    ).astype(jnp.bfloat16)
    base = pl.multiple_of(spot["core"] * HALF, 128)
    mine = region(spot, "", 0, base)
    own = pltpu.make_async_copy(
        joined,
        out.at[spot["y"], spot["z"] % 2, spot["z"] // 2, spot["x"] // 2, :, mine[5]],
        local,
    )
    own.start()
    own.wait()
    mate = moved(spot, "core", 1)
    core_copies = []

    def to_mate(number, where):
        copy = pltpu.make_async_remote_copy(
            src_ref=out.at[where],
            dst_ref=out.at[where],
            send_sem=send_core.at[number],
            recv_sem=recv_core.at[number],
            device_id=device_of(mate),
            device_id_type=MESH,
        )
        copy.start()
        core_copies.append(copy)

    flights = {}
    for stage in range(3):
        for part, order in enumerate(RING_ORDERS):
            axis, known = order[stage], order[:stage]
            if stage > 0:
                for copy in flights[part]:
                    copy.wait_recv()
            where = region(spot, known, part, base)
            started = []
            for step in (1, 3, 2):
                number = (stage * 3 + part) * 3 + step - 1
                copy = pltpu.make_async_remote_copy(
                    src_ref=out.at[where],
                    dst_ref=out.at[where],
                    send_sem=send.at[number],
                    recv_sem=recv.at[number],
                    device_id=device_of(moved(spot, axis, step)),
                    device_id_type=MESH,
                )
                copy.start()
                started.append(copy)
            if stage == 2:
                to_mate(part * 4, where)
            flights[part] = started
            copies += started
    for step in (1, 3, 2):
        for part, order in enumerate(RING_ORDERS):
            axis = order[2]
            flights[part][(1, 3, 2).index(step)].wait_recv()
            source = moved(spot, axis, -step)
            to_mate(part * 4 + step, region(source, order[:2], part, base))
    for copy in copies[3:]:
        copy.wait_send()
    for copy in core_copies:
        copy.wait()


def gather_weights(shard):
    shard = jnp.pad(shard, ((0, 4), (0, 0)))
    target = jnp.arange(48, dtype=jnp.int32)[:, None]
    source = jnp.arange(64, dtype=jnp.int32)[None, :]
    merge = ((target // 12 == source // 16) & (target % 12 == source % 16)).astype(jnp.bfloat16)
    out = pl.pallas_call(
        gather_kernel,
        out_shape=jax.ShapeDtypeStruct((4, 2, 2, 2, 48, PACK), jnp.bfloat16),
        in_specs=[pl.BlockSpec(memory_space=pltpu.VMEM)] * 2,
        out_specs=pl.BlockSpec(memory_space=pl.ANY),
        scratch_shapes=[
            pltpu.VMEM((4, 16, QUARTER), jnp.bfloat16),
            pltpu.VMEM((48, QUARTER), jnp.bfloat16),
            pltpu.SemaphoreType.DMA((3,)),
            pltpu.SemaphoreType.DMA((3,)),
            pltpu.SemaphoreType.DMA((27,)),
            pltpu.SemaphoreType.DMA((27,)),
            pltpu.SemaphoreType.DMA((12,)),
            pltpu.SemaphoreType.DMA((12,)),
            pltpu.SemaphoreType.DMA,
        ],
        compiler_params=pltpu.CompilerParams(collective_id=1, has_side_effects=True),
        cost_estimate=pl.CostEstimate(flops=0, bytes_accessed=28 * 2**20, transcendentals=0),
        name="gather_weights",
    )(shard, merge)
    return out.reshape(1536, PACK)


def scatter_kernel(grads, split, out, total, from_mate, done, packed, send_core, recv_core, send, recv, send0, recv0, *flat_landing):
    spot = place()
    meet(spot)
    mate = moved(spot, "core", 1)
    base = pl.multiple_of(spot["core"] * HALF, 128)
    mate_base = pl.multiple_of(mate["core"] * HALF, 128)
    core_copies = []
    for part in range(3):
        rows = pl.ds(part * 16, 16)
        copy = pltpu.make_async_remote_copy(
            src_ref=grads.at[:, :, :, :, rows, pl.ds(mate_base, HALF)],
            dst_ref=from_mate.at[:, :, :, :, rows, :],
            send_sem=send_core.at[part],
            recv_sem=recv_core.at[part],
            device_id=device_of(mate),
            device_id_type=MESH,
        )
        copy.start()
        core_copies.append(copy)
    landing = (flat_landing[:3], flat_landing[3:6], flat_landing[6:])
    all_copies = list(core_copies)

    for part, order in enumerate(RING_ORDERS):
        rows = pl.ds(part * 16, 16)
        core_copies[part].wait_recv()

        @pl.loop(0, 32)
        def _(block):
            at = (block // 8, (block // 4) % 2, (block // 2) % 2, block % 2, rows)
            total[at] = (
                grads[at + (pl.ds(base, HALF),)].astype(jnp.float32)
                + from_mate[at].astype(jnp.float32)
            ).astype(jnp.bfloat16)

        flights = start_ring(spot, part, 0, total, landing, send, recv, all_copies)
        if part == 0:
            pending = []
        pending.append(flights)
    for stage in range(3):
        for part, order in enumerate(RING_ORDERS):
            known = order[: 2 - stage]
            for copy in pending[part]:
                copy.wait_recv()
            where = region(spot, known, part, 0)
            add_ring(spot, known, part, total, landing[stage][part], where)
            if stage < 2:
                pending[part] = start_ring(spot, part, stage + 1, total, landing, send, recv, all_copies)
    index = (spot["x"] % 2) * 2 + spot["core"]
    quarter = spot["core"] * 2 + spot["x"] % 2
    mine = region(spot, "", 0, 0)
    done[...] = total[spot["y"], spot["z"] % 2, spot["z"] // 2, spot["x"] // 2, :, mine[5]]
    packed[...] = (
        jnp.dot(split[...], done[...], preferred_element_type=jnp.float32)
        .astype(jnp.bfloat16)
        .reshape(4, 16, QUARTER)
    )
    columns = pl.ds(pl.multiple_of(quarter * QUARTER, 128), QUARTER)
    copies = []
    for step in (1, 2, 3):
        other, target = member(spot, step)
        copy = pltpu.make_async_remote_copy(
            src_ref=packed.at[target],
            dst_ref=out.at[:, columns],
            send_sem=send0.at[step - 1],
            recv_sem=recv0.at[step - 1],
            device_id=device_of(other),
            device_id_type=MESH,
        )
        copy.start()
        copies.append(copy)
    out[:, columns] = packed[index]
    for copy in copies:
        copy.wait()
    for copy in all_copies:
        copy.wait_send()


def start_ring(spot, part, stage, total, landing, send, recv, all_copies):
    order = RING_ORDERS[part]
    axis, known = order[2 - stage], order[: 2 - stage]
    started = []
    for step in (1, 3, 2):
        other = moved(spot, axis, step)
        number = (stage * 3 + part) * 3 + step - 1
        copy = pltpu.make_async_remote_copy(
            src_ref=total.at[region(other, known, part, 0)],
            dst_ref=landing[stage][part].at[step - 1],
            send_sem=send.at[number],
            recv_sem=recv.at[number],
            device_id=device_of(other),
            device_id_type=MESH,
        )
        copy.start()
        started.append(copy)
    all_copies += started
    return started


def landing_shape(known):
    return (
        4 if "y" in known else 1,
        2 if "z" in known else 1,
        2 if "z" in known else 1,
        2 if "x" in known else 1,
        16,
        HALF if "x" in known else QUARTER,
    )


def add_ring(spot, known, part, total, landing, where):
    shape = landing_shape(known)
    count = shape[0] * shape[1] * shape[2] * shape[3]

    def body(block):
        a, b, c, d = (
            block // (shape[1] * shape[2] * shape[3]),
            (block // (shape[2] * shape[3])) % shape[1],
            (block // shape[3]) % shape[2],
            block % shape[3],
        )
        at = (
            a + (0 if "y" in known else spot["y"]),
            b + (0 if "z" in known else spot["z"] % 2),
            c + (0 if "z" in known else spot["z"] // 2),
            d + (0 if "x" in known else spot["x"] // 2),
            pl.ds(part * 16, 16),
            where[5],
        )
        summed = total[at].astype(jnp.float32)
        for step in range(3):
            summed += landing[step, a, b, c, d].astype(jnp.float32)
        total[at] = summed.astype(jnp.bfloat16)

    if count == 1:
        body(0)
    else:
        pl.loop(0, count)(body)


def scatter_sum(grads):
    source = jnp.arange(48, dtype=jnp.int32)[None, :]
    target = jnp.arange(64, dtype=jnp.int32)[:, None]
    split = ((source // 12 == target // 16) & (source % 12 == target % 16)).astype(jnp.bfloat16)
    landings = [
        pltpu.VMEM((3,) + landing_shape(order[: 2 - stage]), jnp.bfloat16)
        for stage in range(3)
        for order in RING_ORDERS
    ]
    out = pl.pallas_call(
        scatter_kernel,
        out_shape=jax.ShapeDtypeStruct((16, PACK), jnp.bfloat16),
        in_specs=[pl.BlockSpec(memory_space=pltpu.VMEM)] * 2,
        out_specs=pl.BlockSpec(memory_space=pltpu.VMEM),
        scratch_shapes=[
            pltpu.VMEM((4, 2, 2, 2, 48, HALF), jnp.bfloat16),
            pltpu.VMEM((4, 2, 2, 2, 48, HALF), jnp.bfloat16),
            pltpu.VMEM((48, QUARTER), jnp.bfloat16),
            pltpu.VMEM((4, 16, QUARTER), jnp.bfloat16),
            pltpu.SemaphoreType.DMA((3,)),
            pltpu.SemaphoreType.DMA((3,)),
            pltpu.SemaphoreType.DMA((27,)),
            pltpu.SemaphoreType.DMA((27,)),
            pltpu.SemaphoreType.DMA((3,)),
            pltpu.SemaphoreType.DMA((3,)),
        ] + landings,
        compiler_params=pltpu.CompilerParams(
            collective_id=2, has_side_effects=True, vmem_limit_bytes=56 * 2**20
        ),
        cost_estimate=pl.CostEstimate(flops=0, bytes_accessed=28 * 2**20, transcendentals=0),
        name="scatter_sum",
    )(grads.reshape(4, 2, 2, 2, 48, PACK), split)
    return out[:12]


def shards(
    tokens,
    segments,
    routes,
    gain_attn,
    w_query,
    key_weight,
    value_weight,
    w_out,
    w_router,
    gain_ffn,
    w_gate,
    w_up,
    w_down,
    cotangent,
):
    device_local_rows, width = tokens.shape
    sequence_length = segments.shape[0]
    query_group_size = QUERY_HEAD_COUNT // KEY_VALUE_HEADS
    factor = HEAD_SIZE ** (-0.5)
    ctx_index = lax.axis_index("ctx")
    ctx_count = lax.axis_size("ctx")
    rows_per_block = math.gcd(sequence_length, 512)
    count_of_blocks = sequence_length // rows_per_block
    key_pos = jnp.arange(sequence_length, dtype=jnp.int32).reshape(count_of_blocks, rows_per_block)
    key_seg = segments.reshape(count_of_blocks, rows_per_block)
    query_pos = ctx_index * device_local_rows + jnp.arange(device_local_rows, dtype=jnp.int32)
    query_seg = lax.dynamic_slice_in_dim(segments, ctx_index * device_local_rows, device_local_rows)
    key_value_shape = (count_of_blocks, rows_per_block, KEY_VALUE_HEADS, HEAD_SIZE)
    shard = jnp.concatenate(
        [w_query, key_weight, value_weight, w_out, w_router, gain_attn[:, None], gain_ffn[:, None]],
        axis=1,
    )
    packed = gather_weights(jnp.pad(shard, ((0, 0), (0, PACK - shard.shape[1]))))
    query_proj = packed[:, :1536]
    key_proj = packed[:, 1536:2048]
    value_proj = packed[:, 2048:2560]
    out_proj = packed[:, 2560:4096]
    router_proj = packed[:, 4096:4112]
    gain_one = packed[:, 4112]
    gain_two = packed[:, 4113]
    expert_weights = (
        lax.all_gather(w_gate, "dp", axis=1, tiled=True),
        lax.all_gather(w_up, "dp", axis=1, tiled=True),
        lax.all_gather(w_down, "dp", axis=1, tiled=True),
    )
    gate_proj, up_proj, down_proj = expert_weights
    residual = tokens.astype(jnp.float32)
    inverse_one = inverse_rms(residual)
    scale_one = gain_one.astype(jnp.float32)
    normed = (residual * inverse_one * scale_one).astype(jnp.bfloat16)
    rows_of_queries = jnp.dot(normed, query_proj, preferred_element_type=jnp.float32).astype(
        jnp.bfloat16
    )
    rows_of_keys = jnp.dot(normed, key_proj, preferred_element_type=jnp.float32).astype(
        jnp.bfloat16
    )
    rows_of_values = jnp.dot(normed, value_proj, preferred_element_type=jnp.float32).astype(
        jnp.bfloat16
    )
    all_keys, all_values = (
        lax.all_gather(rows_of_keys, "ctx", axis=0, tiled=True),
        lax.all_gather(rows_of_values, "ctx", axis=0, tiled=True),
    )
    heads_of_queries = rows_of_queries.reshape(
        device_local_rows, KEY_VALUE_HEADS, query_group_size, HEAD_SIZE
    )
    summed, log_total = attend_forward(
        heads_of_queries,
        all_keys.reshape(key_value_shape),
        all_values.reshape(key_value_shape),
        key_pos,
        key_seg,
        query_pos,
        query_seg,
        factor,
    )
    attended = summed.reshape(device_local_rows, QUERY_HEAD_COUNT * HEAD_SIZE).astype(jnp.bfloat16)
    hidden_one = residual + contract_cols(attended, out_proj)
    inverse_two = inverse_rms(hidden_one)
    scale_two = gain_two.astype(jnp.float32)
    normed_two = (hidden_one * inverse_two * scale_two).astype(jnp.bfloat16)
    logits = jnp.dot(normed_two, router_proj, preferred_element_type=jnp.float32)
    experts = router_proj.shape[1]
    per_device = experts // ctx_count
    capacity = max(2, 3 * device_local_rows // experts)
    picked = (routes[:, :, None] == jnp.arange(experts, dtype=jnp.int32)[None, None, :]).astype(
        jnp.float32
    )
    chosen = jnp.sum(picked * logits[:, None, :], axis=-1)
    gate_weights = jax.nn.softmax(chosen, axis=-1)
    flat_pick = picked.reshape(-1, experts)
    slot_ids = jnp.sum(flat_pick * (jnp.cumsum(flat_pick, axis=0) - 1.0), axis=-1).astype(jnp.int32)
    targets = routes.reshape(-1) * capacity + slot_ids
    placement = (
        targets[:, None] == jnp.arange(experts * capacity, dtype=jnp.int32)[None, :]
    ).astype(jnp.bfloat16)
    placement = placement.reshape(device_local_rows, TOP, experts * capacity)
    spread = jnp.sum(placement, axis=1)
    outgoing = (
        contract_rows(spread, normed_two)
        .astype(jnp.bfloat16)
        .reshape(ctx_count, per_device, capacity, width)
    )
    received = lax.all_to_all(outgoing, "ctx", split_axis=0, concat_axis=0, tiled=True)
    gate_pre = jnp.einsum("sxid,xdf->sxif", received, gate_proj, preferred_element_type=jnp.float32)
    up_pre = jnp.einsum("sxid,xdf->sxif", received, up_proj, preferred_element_type=jnp.float32)
    hidden = (jax.nn.silu(gate_pre) * up_pre).astype(jnp.bfloat16)
    produced = jnp.einsum(
        "sxif,xfd->sxid", hidden, down_proj, preferred_element_type=jnp.float32
    ).astype(jnp.bfloat16)
    produced, received, gate_pre, up_pre, hidden = (produced, received, gate_pre, up_pre, hidden)
    returned = lax.all_to_all(produced, "ctx", split_axis=0, concat_axis=0, tiled=True).reshape(
        experts * capacity, width
    )
    chosen_rows = jnp.einsum("tcr,rd->tcd", placement, returned, preferred_element_type=jnp.float32)
    mixed = (hidden_one + jnp.sum(gate_weights[:, :, None] * chosen_rows, axis=1)).astype(
        jnp.bfloat16
    )
    gain_back, query_back, key_back, value_back, out_back, router_back, gain_ffn_back = (
        gain_one, query_proj, key_proj, value_proj, out_proj, router_proj, gain_two
    )
    gate_back, up_back, down_back = (
        lax.all_gather(w_gate, "dp", axis=1, tiled=True),
        lax.all_gather(w_up, "dp", axis=1, tiled=True),
        lax.all_gather(w_down, "dp", axis=1, tiled=True),
    )
    keys_back, values_back = (
        lax.all_gather(rows_of_keys, "ctx", axis=0, tiled=True),
        lax.all_gather(rows_of_values, "ctx", axis=0, tiled=True),
    )
    scale_one = gain_back.astype(jnp.float32)
    scale_two = gain_ffn_back.astype(jnp.float32)
    grad_y = cotangent.astype(jnp.float32)
    grad_gates = jnp.sum(chosen_rows * grad_y[:, None, :], axis=-1)
    grad_routed = (gate_weights[:, :, None] * grad_y[:, None, :]).astype(jnp.bfloat16)
    grad_outgoing = jnp.einsum(
        "tcr,tcd->rd", placement, grad_routed, preferred_element_type=jnp.float32
    )
    grad_outgoing = grad_outgoing.astype(jnp.bfloat16).reshape(
        ctx_count, per_device, capacity, width
    )
    grad_received = lax.all_to_all(grad_outgoing, "ctx", split_axis=0, concat_axis=0, tiled=True)
    grad_hidden = jnp.einsum(
        "sxid,xfd->sxif", grad_received, down_back, preferred_element_type=jnp.float32
    )
    sigmoid = jax.nn.sigmoid(gate_pre)
    grad_gate_pre = (grad_hidden * up_pre * sigmoid * (1.0 + gate_pre * (1.0 - sigmoid))).astype(
        jnp.bfloat16
    )
    grad_up_pre = (grad_hidden * gate_pre * sigmoid).astype(jnp.bfloat16)
    grad_expert_in = jnp.einsum(
        "sxif,xdf->sxid", grad_gate_pre, gate_back, preferred_element_type=jnp.float32
    )
    grad_expert_in = grad_expert_in + jnp.einsum(
        "sxif,xdf->sxid", grad_up_pre, up_back, preferred_element_type=jnp.float32
    )
    grad_expert_in = grad_expert_in.astype(jnp.bfloat16)
    grad_gate_full = jnp.einsum(
        "sxid,sxif->xdf", received, grad_gate_pre, preferred_element_type=jnp.float32
    )
    grad_up_full = jnp.einsum(
        "sxid,sxif->xdf", received, grad_up_pre, preferred_element_type=jnp.float32
    )
    grad_down_full = jnp.einsum(
        "sxif,sxid->xfd", hidden, grad_received, preferred_element_type=jnp.float32
    )
    grad_gate, grad_up, grad_down = (
        lax.psum_scatter(
            grad_gate_full.astype(jnp.bfloat16), "dp", scatter_dimension=1, tiled=True
        ).astype(jnp.float32),
        lax.psum_scatter(
            grad_up_full.astype(jnp.bfloat16), "dp", scatter_dimension=1, tiled=True
        ).astype(jnp.float32),
        lax.psum_scatter(
            grad_down_full.astype(jnp.bfloat16), "dp", scatter_dimension=1, tiled=True
        ).astype(jnp.float32),
    )
    grad_back = lax.all_to_all(
        grad_expert_in, "ctx", split_axis=0, concat_axis=0, tiled=True
    ).reshape(experts * capacity, width)
    grad_normed_two = jnp.einsum(
        "tcr,rd->td", placement, grad_back, preferred_element_type=jnp.float32
    )
    grad_chosen = gate_weights * (
        grad_gates - jnp.sum(gate_weights * grad_gates, axis=-1, keepdims=True)
    )
    grad_logits = jnp.sum(picked * grad_chosen[:, :, None], axis=1).astype(jnp.bfloat16)
    grad_normed_two = grad_normed_two + contract_cols(grad_logits, router_back)
    grad_router_full = contract_rows(normed_two, grad_logits)
    grad_hidden_one, grad_gain_two = norm_backward(
        grad_normed_two, hidden_one, inverse_two, scale_two
    )
    grad_hidden_one = grad_hidden_one + grad_y
    grad_branch = grad_hidden_one.astype(jnp.bfloat16)
    grad_out_full = contract_rows(grad_branch, attended)
    attended_gradient = jnp.dot(grad_branch, out_back, preferred_element_type=jnp.float32).astype(
        jnp.bfloat16
    )
    head_gradient = attended_gradient.reshape(
        device_local_rows, KEY_VALUE_HEADS, query_group_size, HEAD_SIZE
    )
    grad_query_heads, key_block_gradient, value_block_gradient = attend_backward(
        heads_of_queries,
        head_gradient,
        keys_back.reshape(key_value_shape),
        values_back.reshape(key_value_shape),
        key_pos,
        key_seg,
        query_pos,
        query_seg,
        log_total,
        factor,
    )
    grad_keys, grad_values = (
        lax.psum_scatter(
            key_block_gradient.reshape(sequence_length, KEY_VALUE_HEADS * HEAD_SIZE).astype(
                jnp.bfloat16
            ),
            "ctx",
            scatter_dimension=0,
            tiled=True,
        ).astype(jnp.float32),
        lax.psum_scatter(
            value_block_gradient.reshape(sequence_length, KEY_VALUE_HEADS * HEAD_SIZE).astype(
                jnp.bfloat16
            ),
            "ctx",
            scatter_dimension=0,
            tiled=True,
        ).astype(jnp.float32),
    )
    grad_queries = grad_query_heads.reshape(device_local_rows, QUERY_HEAD_COUNT * HEAD_SIZE).astype(
        jnp.bfloat16
    )
    grad_keys = grad_keys.astype(jnp.bfloat16)
    grad_values = grad_values.astype(jnp.bfloat16)
    grad_normed = (
        contract_cols(grad_queries, query_back)
        + contract_cols(grad_keys, key_back)
        + contract_cols(grad_values, value_back)
    )
    grad_query_full = contract_rows(normed, grad_queries)
    grad_key_full = contract_rows(normed, grad_keys)
    grad_value_full = contract_rows(normed, grad_values)
    grad_residual, grad_gain_one = norm_backward(grad_normed, residual, inverse_one, scale_one)
    grad_input = (grad_residual + grad_hidden_one).astype(jnp.bfloat16)
    low = jnp.bfloat16
    grads = jnp.concatenate(
        [
            grad_query_full.astype(low),
            grad_key_full.astype(low),
            grad_value_full.astype(low),
            grad_out_full.astype(low),
            grad_router_full.astype(low),
            grad_gain_one.astype(low)[:, None],
            grad_gain_two.astype(low)[:, None],
            jnp.zeros((width, PACK - 4114), low),
        ],
        axis=1,
    )
    share = scatter_sum(grads).astype(jnp.float32)
    shares = (
        share[:, 4112],
        share[:, :1536],
        share[:, 1536:2048],
        share[:, 2048:2560],
        share[:, 2560:4096],
        share[:, 4096:4112],
        share[:, 4113],
    )
    return (
        mixed,
        grad_input,
        shares[0],
        shares[1],
        shares[2],
        shares[3],
        shares[4],
        shares[5],
        shares[6],
        grad_gate,
        grad_up,
        grad_down,
    )


def solution(mesh):
    in_specs = (
        P(("dp", "ctx"), None),
        P("dp"),
        P(("dp", "ctx"), None),
        P(("dp", "ctx")),
        P(("dp", "ctx"), None),
        P(("dp", "ctx"), None),
        P(("dp", "ctx"), None),
        P(("dp", "ctx"), None),
        P(("dp", "ctx"), None),
        P(("dp", "ctx")),
        P("ctx", "dp", None),
        P("ctx", "dp", None),
        P("ctx", "dp", None),
        P(("dp", "ctx"), None),
    )
    out_specs = (
        P(("dp", "ctx"), None),
        P(("dp", "ctx"), None),
        P(("dp", "ctx")),
        P(("dp", "ctx"), None),
        P(("dp", "ctx"), None),
        P(("dp", "ctx"), None),
        P(("dp", "ctx"), None),
        P(("dp", "ctx"), None),
        P(("dp", "ctx")),
        P("ctx", "dp", None),
        P("ctx", "dp", None),
        P("ctx", "dp", None),
    )
    return jax.shard_map(shards, mesh=mesh, in_specs=in_specs, out_specs=out_specs, check_vma=False)
```

```python
import functools

import jax
import jax.numpy as jnp
from jax import lax
from jax.experimental import pallas as pl
from jax.experimental.pallas import tpu as pltpu
from jax.sharding import PartitionSpec as P

QUERY_HEAD_COUNT = 24
KEY_VALUE_HEADS = 8
HEAD_SIZE = 64
TOP = 2

EPSILON = 1e-06
NEGATIVE = -1e30
MESH = pl.DeviceIdType.MESH

PACK = 4608
HALF = PACK // 2
QUARTER = PACK // 4
RING_ORDERS = (("y", "z", "x"), ("y", "z", "x"), ("y", "x", "z"))


def place():
    dp = lax.axis_index("dp")
    ctx = lax.axis_index("ctx")
    return {"y": dp // 2, "z": (ctx // 8) * 2 + dp % 2, "x": (ctx // 2) % 4, "core": ctx % 2}


def device_of(spot):
    z = spot["z"]
    return (spot["y"] * 2 + z % 2, (z // 2) * 8 + spot["x"] * 2 + spot["core"])


def moved(spot, axis, step):
    other = dict(spot)
    if axis == "core":
        other["core"] = 1 - spot["core"]
    else:
        other[axis] = (spot[axis] + step) % 4
    return other


def member(spot, step):
    index = (spot["x"] % 2) * 2 + spot["core"]
    target = (index // 2 + step // 2) % 2 * 2 + (index % 2 + step % 2) % 2
    other = dict(spot)
    other["x"] = (spot["x"] // 2) * 2 + target // 2
    other["core"] = target % 2
    return other, target


def partner(spot):
    other = dict(spot)
    other["z"] = spot["z"] // 2 * 2 + (spot["z"] + 1) % 2
    other["core"] = (spot["core"] + 1) % 2
    return other


def meet(spot):
    barrier = pltpu.get_barrier_semaphore()
    others = [member(spot, step)[0] for step in (1, 2, 3)] + [partner(spot)]
    others += [moved(spot, axis, step) for axis in "xyz" for step in (1, 2, 3)]
    for other in others:
        pl.semaphore_signal(barrier, inc=1, device_id=device_of(other), device_id_type=MESH)
    pl.semaphore_wait(barrier, len(others))


def region(spot, known, part, base):
    def pick(axis, value, size):
        return pl.ds(0, size) if axis in known else pl.ds(value, 1)

    z = spot["z"]
    if "x" in known:
        columns = pl.ds(base, HALF)
    else:
        columns = pl.ds(pl.multiple_of(base + (spot["x"] % 2) * QUARTER, 128), QUARTER)
    return (
        pick("y", spot["y"], 4),
        pick("z", z % 2, 2),
        pick("z", z // 2, 2),
        pick("x", spot["x"] // 2, 2),
        pl.ds(part * 16, 16),
        columns,
    )


def expert_rows(ref, spot, core, half=None):
    rows = ref.shape[0] // 8
    first = (spot["y"] * 2 + core) * rows
    if half is not None:
        rows //= 2
        first += half * rows
    return ref.at[pl.ds(pl.multiple_of(first, 32), rows)]


def half_region(where, axis, half):
    if axis == "y":
        return where[:3] + (pl.ds(half, 1),) + where[4:]
    return (pl.ds(2 * half, 2),) + where[1:]


def relay(ring, numbers, send, recv, whole, half):
    spot, axis = ring

    def copy(ref, step, number):
        return pltpu.make_async_remote_copy(
            src_ref=ref,
            dst_ref=ref,
            send_sem=send.at[numbers + number],
            recv_sem=recv.at[numbers + number],
            device_id=device_of(moved(spot, axis, step)),
            device_id_type=MESH,
        )

    first = [copy(whole(spot), 1, 0), copy(whole(spot), 3, 1)]
    second = [copy(half(moved(spot, axis, 3), 0), 1, 2), copy(half(moved(spot, axis, 1), 1), 3, 3)]
    return first, second


def gather_kernel(
    shard, merge, own_gate, own_up, own_down, out, gate_out, up_out, down_out, pieces, joined,
    send0, recv0, send, recv, send_core, recv_core, local,
    swap_send, swap_recv, swap_local, line_send, line_recv, mate_send, mate_recv, ring_send, ring_recv,
):
    spot = place()
    meet(spot)
    mate = moved(spot, "core", 1)
    stays = spot["core"] == spot["z"] % 2
    experts = ((own_gate, gate_out), (own_up, up_out), (own_down, down_out))

    def swaps():
        return [
            pltpu.make_async_remote_copy(
                src_ref=own,
                dst_ref=expert_rows(whole, spot, spot["z"] % 2),
                send_sem=swap_send.at[n],
                recv_sem=swap_recv.at[n],
                device_id=device_of(partner(spot)),
                device_id_type=MESH,
            )
            for n, (own, whole) in enumerate(experts)
        ]

    def stays_here():
        return [
            pltpu.make_async_copy(own, expert_rows(whole, spot, spot["core"]), swap_local.at[n])
            for n, (own, whole) in enumerate(experts)
        ]

    def line(n):
        whole = experts[n][1]
        return relay(
            (spot, "y"),
            4 * n,
            line_send,
            line_recv,
            lambda at: expert_rows(whole, at, spot["core"]),
            lambda at, half: expert_rows(whole, at, spot["core"], half),
        )

    def to_mates(step):
        source = moved(spot, "y", 4 - step)
        return [
            pltpu.make_async_remote_copy(
                src_ref=expert_rows(whole, source, spot["core"]),
                dst_ref=expert_rows(whole, source, spot["core"]),
                send_sem=mate_send.at[3 * step + n],
                recv_sem=mate_recv.at[3 * step + n],
                device_id=device_of(mate),
                device_id_type=MESH,
            )
            for n, (own, whole) in enumerate(experts)
        ]

    def start_all(copies):
        for copy in copies:
            copy.start()

    @pl.when(stays)
    def _():
        start_all(stays_here())

    @pl.when(jnp.logical_not(stays))
    def _():
        start_all(swaps())

    index = (spot["x"] % 2) * 2 + spot["core"]
    quarter = spot["core"] * 2 + spot["x"] % 2
    copies = []
    for step in (1, 2, 3):
        other, target = member(spot, step)
        goal = other["core"] * 2 + other["x"] % 2
        copy = pltpu.make_async_remote_copy(
            src_ref=shard.at[:, pl.ds(pl.multiple_of(goal * QUARTER, 128), QUARTER)],
            dst_ref=pieces.at[index],
            send_sem=send0.at[step - 1],
            recv_sem=recv0.at[step - 1],
            device_id=device_of(other),
            device_id_type=MESH,
        )
        copy.start()
        copies.append(copy)
    pieces[index] = shard[:, pl.ds(pl.multiple_of(quarter * QUARTER, 128), QUARTER)]
    for copy in copies:
        copy.wait()
    joined[...] = jnp.dot(
        merge[...], pieces[...].reshape(64, QUARTER), preferred_element_type=jnp.float32
    ).astype(jnp.bfloat16)
    base = pl.multiple_of(spot["core"] * HALF, 128)
    mine = region(spot, "", 0, base)
    own = pltpu.make_async_copy(
        joined,
        out.at[spot["y"], spot["z"] % 2, spot["z"] // 2, spot["x"] // 2, :, mine[5]],
        local,
    )
    own.start()
    own.wait()
    core_copies = []

    def to_mate(number, where):
        copy = pltpu.make_async_remote_copy(
            src_ref=out.at[where],
            dst_ref=out.at[where],
            send_sem=send_core.at[number],
            recv_sem=recv_core.at[number],
            device_id=device_of(mate),
            device_id_type=MESH,
        )
        copy.start()
        core_copies.append(copy)

    flights, relays, finals = {}, [], []
    for stage in range(3):
        for part, order in enumerate(RING_ORDERS):
            axis, known = order[stage], order[:stage]
            if stage > 0:
                for copy in flights[part]:
                    copy.wait_recv()
            where = region(spot, known, part, base)
            if stage == 2:
                ring = relay(
                    (spot, axis),
                    4 * part,
                    ring_send,
                    ring_recv,
                    lambda at, known=known, part=part: out.at[region(at, known, part, base)],
                    lambda at, half, known=known, part=part, axis=axis: out.at[
                        half_region(region(at, known, part, base), axis, half)
                    ],
                )
                start_all(ring[0])
                relays.append(ring)
                finals.append((axis, known))
                to_mate(part * 4, where)
                continue
            started = []
            for step in (1, 3, 2):
                number = (stage * 3 + part) * 3 + step - 1
                copy = pltpu.make_async_remote_copy(
                    src_ref=out.at[where],
                    dst_ref=out.at[where],
                    send_sem=send.at[number],
                    recv_sem=recv.at[number],
                    device_id=device_of(moved(spot, axis, step)),
                    device_id_type=MESH,
                )
                copy.start()
                started.append(copy)
            flights[part] = started
            copies += started
        if stage == 1:

            @pl.when(stays)
            def _():
                for copy in stays_here():
                    copy.wait()

            @pl.when(jnp.logical_not(stays))
            def _():
                for copy in swaps():
                    copy.wait()

            lines = [line(n) for n in range(3)]
            for first, _ in lines:
                start_all(first)
            own_mates = to_mates(0)
            start_all(own_mates)

    mates = {step: to_mates(step) for step in (1, 3, 2)}
    for first, second in lines + relays:
        for number in range(2):
            first[number].wait_recv()
            second[number].start()
    for part, (axis, _) in enumerate(finals):
        for step in (1, 3):
            to_mate(part * 4 + step, region(moved(spot, axis, 4 - step), RING_ORDERS[part][:2], part, base))
    for n in range(3):
        mates[1][n].start()
        mates[3][n].start()
    for n, (_, second) in enumerate(lines):
        for copy in second:
            copy.wait_recv()
        mates[2][n].start()
    for part, (_, second) in enumerate(relays):
        for copy in second:
            copy.wait_recv()
        axis = RING_ORDERS[part][2]
        to_mate(part * 4 + 2, region(moved(spot, axis, 2), RING_ORDERS[part][:2], part, base))
    line_copies = [copy for first, second in lines + relays for copy in first + second]
    for copy in copies[3:] + line_copies:
        copy.wait_send()
    for copy in core_copies:
        copy.wait()
    for copy in own_mates + mates[1] + mates[2] + mates[3]:
        copy.wait()


def gather_weights(shard, gate, up, down):
    shard = jnp.pad(shard, ((0, 4), (0, 0)))
    target = jnp.arange(48, dtype=jnp.int32)[:, None]
    source = jnp.arange(64, dtype=jnp.int32)[None, :]
    merge = ((target // 12 == source // 16) & (target % 12 == source % 16)).astype(jnp.bfloat16)
    vmem = pl.BlockSpec(memory_space=pltpu.VMEM)
    anywhere = pl.BlockSpec(memory_space=pl.ANY)
    experts = [
        jax.ShapeDtypeStruct((8 * part.shape[0], part.shape[1]), jnp.bfloat16)
        for part in (gate, up, down)
    ]
    dma = pltpu.SemaphoreType.DMA
    packed, *experts = pl.pallas_call(
        gather_kernel,
        out_shape=[jax.ShapeDtypeStruct((4, 2, 2, 2, 48, PACK), jnp.bfloat16)] + experts,
        in_specs=[vmem] * 2 + [anywhere] * 3,
        out_specs=[anywhere] * 4,
        scratch_shapes=[
            pltpu.VMEM((4, 16, QUARTER), jnp.bfloat16),
            pltpu.VMEM((48, QUARTER), jnp.bfloat16),
            dma((3,)), dma((3,)), dma((18,)), dma((18,)), dma((12,)), dma((12,)), dma,
            dma((3,)), dma((3,)), dma((3,)), dma((12,)), dma((12,)), dma((12,)), dma((12,)),
            dma((12,)), dma((12,)),
        ],
        compiler_params=pltpu.CompilerParams(collective_id=1, has_side_effects=True),
        cost_estimate=pl.CostEstimate(flops=0, bytes_accessed=40 * 2**20, transcendentals=0),
        name="gather_weights",
    )(shard, merge, gate, up, down)
    return packed.reshape(1536, PACK), experts


def scatter_kernel(
    normed, grad_qkv, branch, attended, rest, split, grad_gate, grad_up, grad_down,
    out, gate_out, up_out, down_out,
    grads, total, from_mate, done, packed,
    send_core, recv_core, send, recv, send0, recv0,
    mate_send, mate_recv, own_sem, line_send, line_recv, swap_send, swap_recv,
    *buffers,
):
    spot = place()
    landing = (buffers[:3], buffers[3:6], buffers[6:9])
    held, mates, lines, results, arrived = (buffers[9 + 3 * n : 12 + 3 * n] for n in range(5))
    wholes, finals = (grad_gate, grad_up, grad_down), (gate_out, up_out, down_out)
    mate = moved(spot, "core", 1)
    own_copies, mate_copies = [], []
    for n, whole in enumerate(wholes):
        for y in range(4):
            rows = whole.shape[0] // 8

            def part(core, whole=whole, y=y, rows=rows):
                return whole.at[pl.ds(pl.multiple_of((2 * y + core) * rows, 64), rows)]

            own = pltpu.make_async_copy(part(spot["core"]), held[n].at[y], own_sem.at[4 * n + y])
            own.start()
            own_copies.append(own)
            mate_copies.append(
                pltpu.make_async_remote_copy(
                    src_ref=part(mate["core"]),
                    dst_ref=mates[n].at[y],
                    send_sem=mate_send.at[4 * n + y],
                    recv_sem=mate_recv.at[4 * n + y],
                    device_id=device_of(mate),
                    device_id_type=MESH,
                )
            )
    meet(spot)
    for copy in mate_copies:
        copy.start()

    base = pl.multiple_of(spot["core"] * HALF, 128)
    mate_base = pl.multiple_of(mate["core"] * HALF, 128)
    tile = 256
    grads_shape = (4, 2, 2, 2, 48, tile)

    def fill(turned, right, first):
        @pl.loop(0, right.shape[1] // tile)
        def _(n):
            at = pl.ds(pl.multiple_of(n * tile, tile), tile)
            to = pl.ds(pl.multiple_of(first + n * tile, tile), tile)
            grads[:, :, :, :, :, to] = (
                jnp.dot(turned, right[:, at], preferred_element_type=jnp.float32)
                .astype(jnp.bfloat16)
                .reshape(grads_shape)
            )

    fill(normed[...].T, grad_qkv, 0)
    fill(branch[...].T, attended, grad_qkv.shape[1])
    at = grad_qkv.shape[1] + attended.shape[1]
    grads[:, :, :, :, :, at:] = rest[...].reshape(4, 2, 2, 2, 48, PACK - at)
    core_copies = []
    for part in range(3):
        rows = pl.ds(part * 16, 16)
        copy = pltpu.make_async_remote_copy(
            src_ref=grads.at[:, :, :, :, rows, pl.ds(mate_base, HALF)],
            dst_ref=from_mate.at[:, :, :, :, rows, :],
            send_sem=send_core.at[part],
            recv_sem=recv_core.at[part],
            device_id=device_of(mate),
            device_id_type=MESH,
        )
        copy.start()
        core_copies.append(copy)
    all_copies = core_copies + mate_copies

    line_copies = []
    for n in range(3):
        for copy in mate_copies[4 * n : 4 * n + 4]:
            copy.wait_recv()
        for copy in own_copies[4 * n : 4 * n + 4]:
            copy.wait()

        @pl.loop(0, 4)
        def _(y, n=n):
            held[n][y] = (
                held[n][y].astype(jnp.float32) + mates[n][y].astype(jnp.float32)
            ).astype(jnp.bfloat16)

        for step in (1, 3, 2):
            other = moved(spot, "y", step)
            copy = pltpu.make_async_remote_copy(
                src_ref=held[n].at[other["y"]],
                dst_ref=lines[n].at[step - 1],
                send_sem=line_send.at[3 * n + step - 1],
                recv_sem=line_recv.at[3 * n + step - 1],
                device_id=device_of(other),
                device_id_type=MESH,
            )
            copy.start()
            line_copies.append(copy)
    all_copies += line_copies

    pending = []
    for part, order in enumerate(RING_ORDERS):
        rows = pl.ds(part * 16, 16)
        core_copies[part].wait_recv()

        @pl.loop(0, 32)
        def _(block):
            at = (block // 8, (block // 4) % 2, (block // 2) % 2, block % 2, rows)
            total[at] = (
                grads[at + (pl.ds(base, HALF),)].astype(jnp.float32)
                + from_mate[at].astype(jnp.float32)
            ).astype(jnp.bfloat16)

        pending.append(start_ring(spot, part, 0, total, landing, send, recv, all_copies))
    for stage in range(3):
        if stage == 2:
            sum_lines(spot, held, lines, line_copies, results)
            swap_results(spot, results, arrived, swap_send, swap_recv, True)
        for part, order in enumerate(RING_ORDERS):
            known = order[: 2 - stage]
            for copy in pending[part]:
                copy.wait_recv()
            where = region(spot, known, part, 0)
            add_ring(spot, known, part, total, landing[stage][part], where)
            if stage < 2:
                pending[part] = start_ring(spot, part, stage + 1, total, landing, send, recv, all_copies)
    index = (spot["x"] % 2) * 2 + spot["core"]
    quarter = spot["core"] * 2 + spot["x"] % 2
    mine = region(spot, "", 0, 0)
    done[...] = total[spot["y"], spot["z"] % 2, spot["z"] // 2, spot["x"] // 2, :, mine[5]]
    packed[...] = (
        jnp.dot(split[...], done[...], preferred_element_type=jnp.float32)
        .astype(jnp.bfloat16)
        .reshape(4, 16, QUARTER)
    )
    columns = pl.ds(pl.multiple_of(quarter * QUARTER, 128), QUARTER)
    copies = []
    for step in (1, 2, 3):
        other, target = member(spot, step)
        copy = pltpu.make_async_remote_copy(
            src_ref=packed.at[target],
            dst_ref=out.at[:, columns],
            send_sem=send0.at[step - 1],
            recv_sem=recv0.at[step - 1],
            device_id=device_of(other),
            device_id_type=MESH,
        )
        copy.start()
        copies.append(copy)
    out[:, columns] = packed[index]
    swap_results(spot, results, arrived, swap_send, swap_recv, False)
    stays = spot["core"] == spot["z"] % 2

    @pl.when(stays)
    def _():
        for result, final in zip(results, finals):
            final[...] = result[...].astype(jnp.float32)

    @pl.when(jnp.logical_not(stays))
    def _():
        for result, final in zip(arrived, finals):
            final[...] = result[...].astype(jnp.float32)

    for copy in copies:
        copy.wait()
    for copy in all_copies:
        copy.wait_send()


def sum_lines(spot, held, lines, line_copies, results):
    for copy in line_copies:
        copy.wait_recv()
    for mine, line, result in zip(held, lines, results):
        total = mine[spot["y"]].astype(jnp.float32)
        for step in range(3):
            total += line[step].astype(jnp.float32)
        result[...] = total.astype(jnp.bfloat16)


def swap_results(spot, results, arrived, send, recv, start):
    @pl.when(spot["core"] != spot["z"] % 2)
    def _():
        for n, (result, place_in) in enumerate(zip(results, arrived)):
            copy = pltpu.make_async_remote_copy(
                src_ref=result,
                dst_ref=place_in,
                send_sem=send.at[n],
                recv_sem=recv.at[n],
                device_id=device_of(partner(spot)),
                device_id_type=MESH,
            )
            if start:
                copy.start()
            else:
                copy.wait()


def start_ring(spot, part, stage, total, landing, send, recv, all_copies):
    order = RING_ORDERS[part]
    axis, known = order[2 - stage], order[: 2 - stage]
    started = []
    for step in (1, 3, 2):
        other = moved(spot, axis, step)
        number = (stage * 3 + part) * 3 + step - 1
        copy = pltpu.make_async_remote_copy(
            src_ref=total.at[region(other, known, part, 0)],
            dst_ref=landing[stage][part].at[step - 1],
            send_sem=send.at[number],
            recv_sem=recv.at[number],
            device_id=device_of(other),
            device_id_type=MESH,
        )
        copy.start()
        started.append(copy)
    all_copies += started
    return started


def landing_shape(known):
    return (
        4 if "y" in known else 1,
        2 if "z" in known else 1,
        2 if "z" in known else 1,
        2 if "x" in known else 1,
        16,
        HALF if "x" in known else QUARTER,
    )


def add_ring(spot, known, part, total, landing, where):
    shape = landing_shape(known)
    count = shape[0] * shape[1] * shape[2] * shape[3]

    def body(block):
        a, b, c, d = (
            block // (shape[1] * shape[2] * shape[3]),
            (block // (shape[2] * shape[3])) % shape[1],
            (block // shape[3]) % shape[2],
            block % shape[3],
        )
        at = (
            a + (0 if "y" in known else spot["y"]),
            b + (0 if "z" in known else spot["z"] % 2),
            c + (0 if "z" in known else spot["z"] // 2),
            d + (0 if "x" in known else spot["x"] // 2),
            pl.ds(part * 16, 16),
            where[5],
        )
        summed = total[at].astype(jnp.float32)
        for step in range(3):
            summed += landing[step, a, b, c, d].astype(jnp.float32)
        total[at] = summed.astype(jnp.bfloat16)

    if count == 1:
        body(0)
    else:
        pl.loop(0, count)(body)


def scatter_sum(normed, grad_qkv, branch, attended, rest, expert_grads):
    source = jnp.arange(48, dtype=jnp.int32)[None, :]
    target = jnp.arange(64, dtype=jnp.int32)[:, None]
    split = ((source // 12 == target // 16) & (source % 12 == target % 16)).astype(jnp.bfloat16)
    low = jnp.bfloat16
    landings = [
        pltpu.VMEM((3,) + landing_shape(order[: 2 - stage]), low)
        for stage in range(3)
        for order in RING_ORDERS
    ]
    blocks = [(part.shape[0] // 8, part.shape[1]) for part in expert_grads]
    landings += [pltpu.VMEM((4,) + block, low) for block in blocks] * 2
    landings += [pltpu.VMEM((3,) + block, low) for block in blocks]
    landings += [pltpu.VMEM(block, low) for block in blocks] * 2
    vmem = pl.BlockSpec(memory_space=pltpu.VMEM)
    anywhere = pl.BlockSpec(memory_space=pl.ANY)
    dma = pltpu.SemaphoreType.DMA
    out, *finals = pl.pallas_call(
        scatter_kernel,
        out_shape=[jax.ShapeDtypeStruct((16, PACK), low)]
        + [jax.ShapeDtypeStruct(block, jnp.float32) for block in blocks],
        in_specs=[vmem] * 6 + [anywhere] * 3,
        out_specs=[vmem] * 4,
        scratch_shapes=[
            pltpu.VMEM((4, 2, 2, 2, 48, PACK), low),
            pltpu.VMEM((4, 2, 2, 2, 48, HALF), low),
            pltpu.VMEM((4, 2, 2, 2, 48, HALF), low),
            pltpu.VMEM((48, QUARTER), low),
            pltpu.VMEM((4, 16, QUARTER), low),
            dma((3,)), dma((3,)), dma((27,)), dma((27,)), dma((3,)), dma((3,)),
            dma((12,)), dma((12,)), dma((12,)), dma((9,)), dma((9,)), dma((3,)), dma((3,)),
        ]
        + landings,
        compiler_params=pltpu.CompilerParams(
            collective_id=2, has_side_effects=True, vmem_limit_bytes=62 * 2**20
        ),
        cost_estimate=pl.CostEstimate(
            flops=2 * 192 * 1536 * 4096, bytes_accessed=28 * 2**20, transcendentals=0
        ),
        name="scatter_sum",
    )(normed, grad_qkv, branch, attended, rest, split, *expert_grads)
    return out[:12], finals


def inverse_rms(values):
    return lax.rsqrt(jnp.mean(values * values, axis=-1, keepdims=True) + EPSILON)


def norm_backward(grad_normed, values, inverse, gain):
    unit_rows = values * inverse
    grad_unit = grad_normed * gain
    grad_values = inverse * (
        grad_unit - unit_rows * jnp.mean(grad_unit * unit_rows, axis=-1, keepdims=True)
    )
    return (grad_values, jnp.sum(grad_normed * unit_rows, axis=0))


def contract_rows(left, right):
    return lax.dot_general(
        left, right, (((0,), (0,)), ((), ())), preferred_element_type=jnp.float32
    )


def contract_cols(left, right):
    return lax.dot_general(
        left, right, (((1,), (1,)), ((), ())), preferred_element_type=jnp.float32
    )


MAIN_ROWS = 32
REST_ROWS = 16
REST_WIDTH = 384
CAPACITY = 36
SOURCES = 16
TILE = 256


def across(left, right):
    return lax.dot_general(
        left, right, (((1,), (1,)), ((), ())), preferred_element_type=jnp.float32
    )


def dot32(left, right):
    return jnp.dot(left, right, preferred_element_type=jnp.float32)


def in_three(column, lanes):
    first = column.astype(jnp.bfloat16).astype(jnp.float32)
    second = (column - first).astype(jnp.bfloat16).astype(jnp.float32)
    third = column - first - second
    return jnp.where(lanes % 3 == 0, first, jnp.where(lanes % 3 == 1, second, third))


def dispatch_tables(routes):
    rows = routes.shape[0]
    low = jnp.bfloat16
    experts = jnp.arange(SOURCES, dtype=jnp.int32)
    picked = (routes.reshape(-1)[:, None] == experts[None, :]).astype(jnp.float32)
    earlier = jnp.cumsum(picked, axis=0) - 1.0
    slots = jnp.sum(picked * earlier, axis=-1).astype(jnp.int32).reshape(rows, TOP).T[:, :, None]
    chosen = routes.T[:, :, None]
    main = jnp.arange(SOURCES * MAIN_ROWS, dtype=jnp.int32)[None, None, :]
    place_main = ((chosen == main // MAIN_ROWS) & (slots == main % MAIN_ROWS)).astype(low)
    rest = jnp.arange(SOURCES * REST_ROWS, dtype=jnp.int32)[None, None, None, :]
    quarter = jnp.arange(4, dtype=jnp.int32)[None, :, None, None]
    place_rest = (
        (chosen[:, None] == rest // REST_ROWS)
        & ((rest // 4) % 4 == quarter)
        & (slots[:, None] == MAIN_ROWS + rest % 4)
    ).astype(low)
    place_gate = (
        (chosen == rest[0] // REST_ROWS) & (slots % REST_ROWS == rest[0] % REST_ROWS)
    ).astype(low)
    lanes = jnp.arange(128, dtype=jnp.int32)[None, None, :]
    gate_lanes = (lanes // 3 == slots // REST_ROWS).astype(jnp.float32)
    return place_main, place_rest, place_gate, gate_lanes


def unpack_tables():
    low = jnp.bfloat16
    row = jnp.arange(4 * CAPACITY, dtype=jnp.int32)[:, None]
    device, slot = row // CAPACITY, row % CAPACITY
    main = jnp.arange(4 * MAIN_ROWS, dtype=jnp.int32)[None, :]
    from_main = ((device == main // MAIN_ROWS) & (slot == main % MAIN_ROWS)).astype(low)
    rest = jnp.arange(4 * REST_ROWS, dtype=jnp.int32)[None, :]
    from_rest = jnp.stack(
        [
            (
                (device == rest // REST_ROWS)
                & ((rest // 4) % 4 == quarter)
                & (slot == MAIN_ROWS + rest % 4)
            ).astype(low)
            for quarter in range(4)
        ]
    )
    from_gate = ((device == rest // REST_ROWS) & (slot % REST_ROWS == rest % REST_ROWS)).astype(low)
    lanes = jnp.arange(128, dtype=jnp.int32)[None, :]
    lane_mask = (lanes // 3 == slot // REST_ROWS).astype(jnp.float32)
    return (
        from_main, from_main.T, from_rest, from_rest.transpose(0, 2, 1), from_gate, from_gate.T,
        lane_mask,
    )


def experts_kernel(
    normed, cotangent, gates, place_main, place_rest, place_gate, gate_lanes,
    place_main_t, place_rest_t, place_gate_t,
    from_main, to_main, from_rest, to_rest, from_gate, to_gate, lane_mask,
    *rest_refs,
):
    weight_parts, rest_refs = rest_refs[:WEIGHT_PARTS], rest_refs[WEIGHT_PARTS:]
    grad_outs, rest_refs = rest_refs[3:6], rest_refs[:3] + rest_refs[6:]
    (
        grad_normed, mixture, grad_gates, gate_w, up_w, down_w,
        x_main, x_rest, c_main, c_rest, x_main_in, x_rest_in, c_main_in, c_rest_in,
        d_main, d_rest, d_main_in, d_rest_in, y_main, y_rest, y_main_in, y_rest_in,
        rows_x, rows_c, gate_pre, up_pre, hidden, grad_gate_pre, grad_up_pre, rows_d, rows_y,
        turned,
        weight_sem, out_sem, send, recv,
    ) = rest_refs
    low, wide = jnp.bfloat16, jnp.float32
    dp, ctx = lax.axis_index("dp"), lax.axis_index("ctx")
    loads = [
        pltpu.make_async_copy(part, whole, weight_sem.at[n])
        for n, (part, whole) in enumerate(zip(weight_parts, (gate_w, up_w, down_w)))
    ]
    for load in loads:
        load.start()
    y, z_lo, core = dp // 2, dp % 2, ctx % 2
    expert = ctx // 2 * 2 + z_lo
    at_home = z_lo == core

    def holder(step):
        other = (ctx + step) % SOURCES
        return other, (2 * y + other % 2, other // 2 * 2 + z_lo)

    def sender(step):
        other = (expert + step) % SOURCES
        return other, (2 * y + core, other)

    barrier = pltpu.get_barrier_semaphore()
    for step in range(1, SOURCES):
        for pick in (holder, sender):
            pl.semaphore_signal(barrier, inc=1, device_id=pick(step)[1], device_id_type=MESH)

    @pl.when(jnp.logical_not(at_home))
    def _():
        for pick in (holder, sender):
            pl.semaphore_signal(barrier, inc=1, device_id=pick(0)[1], device_id_type=MESH)

    def wait_barrier():
        pl.semaphore_wait(barrier, 2 * (SOURCES - 1) + 2 * ((z_lo + core) % 2))

    def pack(source, main, rest):
        main[...] = dot32(place_main[...], source[...]).astype(low).reshape(main.shape)
        total = jnp.zeros((SOURCES * REST_ROWS, REST_WIDTH), wide)
        for quarter in range(4):
            total += dot32(
                place_rest[quarter], source[:, quarter * REST_WIDTH : (quarter + 1) * REST_WIDTH]
            )
        rest[:, :, :REST_WIDTH] = total.astype(low).reshape(SOURCES, REST_ROWS, REST_WIDTH)

    def start(number, pick, slot, main, rest, main_in, rest_in):
        copies = []
        pairs = ((main, main_in), (rest, rest_in))

        def remote(step, which):
            other, device = pick(step)
            src, dst = pairs[which]
            at = (number * 2 + which) * SOURCES + step
            return pltpu.make_async_remote_copy(
                src_ref=src.at[other],
                dst_ref=dst.at[slot],
                send_sem=send.at[at],
                recv_sem=recv.at[at],
                device_id=device,
                device_id_type=MESH,
            )

        def local(which):
            src, dst = pairs[which]
            at = (number * 2 + which) * SOURCES
            return pltpu.make_async_copy(src.at[slot], dst.at[slot], recv.at[at])

        for step in range(1, SOURCES):
            for which in range(2):
                copy = remote(step, which)
                copy.start()
                copies.append(copy)

        @pl.when(at_home)
        def _():
            for which in range(2):
                local(which).start()

        @pl.when(jnp.logical_not(at_home))
        def _():
            for which in range(2):
                remote(0, which).start()

        def wait_recv():
            @pl.when(at_home)
            def _():
                for which in range(2):
                    local(which).wait()

            @pl.when(jnp.logical_not(at_home))
            def _():
                for which in range(2):
                    remote(0, which).wait_recv()

            for copy in copies:
                copy.wait_recv()

        def wait_send():
            @pl.when(jnp.logical_not(at_home))
            def _():
                for which in range(2):
                    remote(0, which).wait_send()

            for copy in copies:
                copy.wait_send()

        return wait_recv, wait_send

    def unpack(main_in, rest_in, rows, group):
        at = pl.ds(4 * group, 4)
        main = main_in[at].reshape(4 * MAIN_ROWS, -1)
        rest = rest_in[at].reshape(4 * REST_ROWS, -1)
        for quarter in range(4):
            lanes = slice(quarter * REST_WIDTH, (quarter + 1) * REST_WIDTH)
            rows[pl.ds(group * 4 * CAPACITY, 4 * CAPACITY), lanes] = (
                dot32(from_main[...], main[:, lanes])
                + dot32(from_rest[quarter], rest[:, :REST_WIDTH])
            ).astype(low)

    def repack(rows, main, rest, group):
        at = pl.ds(4 * group, 4)
        block = rows[pl.ds(group * 4 * CAPACITY, 4 * CAPACITY), :]
        main[at] = dot32(to_main[...], block).astype(low).reshape(4, MAIN_ROWS, -1)
        total = jnp.zeros((4 * REST_ROWS, REST_WIDTH), wide)
        for quarter in range(4):
            total += dot32(
                to_rest[quarter], block[:, quarter * REST_WIDTH : (quarter + 1) * REST_WIDTH]
            )
        rest[at, :, :REST_WIDTH] = total.astype(low).reshape(4, REST_ROWS, REST_WIDTH)

    pack(normed, x_main, x_rest)
    lanes = lax.broadcasted_iota(jnp.int32, (normed.shape[0], 128), 1)
    gate_rows = jnp.zeros((SOURCES * REST_ROWS, 128), wide)
    for choice in range(TOP):
        held = in_three(gates[:, choice : choice + 1], lanes) * gate_lanes[choice]
        gate_rows += dot32(place_gate[choice], held.astype(low))
    x_rest[:, :, REST_WIDTH:] = gate_rows.astype(low).reshape(SOURCES, REST_ROWS, 128)
    wait_barrier()
    flights = start(0, holder, ctx, x_main, x_rest, x_main_in, x_rest_in)
    pack(cotangent, c_main, c_rest)
    cotangent_flights = start(1, holder, ctx, c_main, c_rest, c_main_in, c_rest_in)
    for load in loads:
        load.wait()
    flights[0]()
    for group in range(4):
        unpack(x_main_in, x_rest_in, rows_x, group)

    @pl.loop(0, gate_w.shape[1] // TILE)
    def _(tile):
        at = pl.ds(pl.multiple_of(tile * TILE, TILE), TILE)
        gate = dot32(rows_x[...], gate_w[:, at])
        up = dot32(rows_x[...], up_w[:, at])
        gate_pre[:, at] = gate
        up_pre[:, at] = up
        hidden[:, at] = (gate / (1.0 + jnp.exp(-gate)) * up).astype(low)

    @pl.loop(0, down_w.shape[1] // TILE)
    def _(tile):
        at = pl.ds(pl.multiple_of(tile * TILE, TILE), TILE)
        rows_y[:, at] = dot32(hidden[...], down_w[:, at]).astype(low)

    cotangent_flights[0]()
    lanes = lax.broadcasted_iota(jnp.int32, (4 * CAPACITY, 128), 1)
    for group in range(4):
        unpack(c_main_in, c_rest_in, rows_c, group)
        at = pl.ds(group * 4 * CAPACITY, 4 * CAPACITY)
        carried = x_rest_in[pl.ds(4 * group, 4), :, pl.ds(REST_WIDTH, 128)].reshape(4 * REST_ROWS, 128)
        gate = jnp.sum(dot32(from_gate[...], carried) * lane_mask[...], axis=1, keepdims=True)
        grad = rows_c[at, :].astype(wide)
        grad_gate = jnp.sum(grad * rows_y[at, :].astype(wide), axis=1, keepdims=True)
        rows_c[at, :] = (gate * grad).astype(low)
        held = (in_three(grad_gate, lanes) * lane_mask[...]).astype(low)
        d_rest[pl.ds(4 * group, 4), :, pl.ds(REST_WIDTH, 128)] = (
            dot32(to_gate[...], held).astype(low).reshape(4, REST_ROWS, 128)
        )

    @pl.loop(0, down_w.shape[0] // TILE)
    def _(tile):
        at = pl.ds(pl.multiple_of(tile * TILE, TILE), TILE)
        grad_hidden = across(rows_c[...], down_w[at, :])
        gate = gate_pre[:, at]
        sigmoid = 1.0 / (1.0 + jnp.exp(-gate))
        grad_gate_pre[:, at] = (
            grad_hidden * up_pre[:, at] * sigmoid * (1.0 + gate * (1.0 - sigmoid))
        ).astype(low)
        grad_up_pre[:, at] = (grad_hidden * gate * sigmoid).astype(low)

    @pl.loop(0, gate_w.shape[0] // TILE)
    def _(tile):
        at = pl.ds(pl.multiple_of(tile * TILE, TILE), TILE)
        rows_d[:, at] = (
            across(grad_gate_pre[...], gate_w[at, :]) + across(grad_up_pre[...], up_w[at, :])
        ).astype(low)

    for group in range(4):
        repack(rows_d, d_main, d_rest, group)
    flights_d = start(2, sender, expert, d_main, d_rest, d_main_in, d_rest_in)
    for group in range(4):
        repack(rows_y, y_main, y_rest, group)
    flights_y = start(3, sender, expert, y_main, y_rest, y_main_in, y_rest_in)

    turned[...] = rows_x[...].T

    @pl.loop(0, gate_w.shape[1] // TILE)
    def _(tile):
        at = pl.ds(pl.multiple_of(tile * TILE, TILE), TILE)
        gate_w[:, at] = dot32(turned[...], grad_gate_pre[:, at]).astype(low)
        up_w[:, at] = dot32(turned[...], grad_up_pre[:, at]).astype(low)

    turned[pl.ds(0, hidden.shape[1]), :] = hidden[...].T

    @pl.loop(0, down_w.shape[1] // TILE)
    def _(tile):
        at = pl.ds(pl.multiple_of(tile * TILE, TILE), TILE)
        down_w[:, at] = dot32(turned[pl.ds(0, hidden.shape[1]), :], rows_c[:, at]).astype(low)

    stores = [
        pltpu.make_async_copy(whole, grad, out_sem.at[n])
        for n, (whole, grad) in enumerate(zip((gate_w, up_w, down_w), grad_outs))
    ]
    for store in stores:
        store.start()
    flights_d[0]()
    main = d_main_in[...].reshape(SOURCES * MAIN_ROWS, -1)
    rest = d_rest_in[...].reshape(SOURCES * REST_ROWS, -1)
    for quarter in range(4):
        at = slice(quarter * REST_WIDTH, (quarter + 1) * REST_WIDTH)
        grad_normed[:, at] = dot32(place_main_t[0] + place_main_t[1], main[:, at]) + dot32(
            place_rest_t[0, quarter] + place_rest_t[1, quarter], rest[:, :REST_WIDTH]
        )
    for choice in range(TOP):
        grad_gates[:, choice : choice + 1] = jnp.sum(
            dot32(place_gate_t[choice], rest[:, REST_WIDTH:]) * gate_lanes[choice],
            axis=1,
            keepdims=True,
        )
    flights_y[0]()
    main = y_main_in[...].reshape(SOURCES * MAIN_ROWS, -1)
    rest = y_rest_in[...].reshape(SOURCES * REST_ROWS, -1)
    for quarter in range(4):
        at = slice(quarter * REST_WIDTH, (quarter + 1) * REST_WIDTH)
        total = jnp.zeros((normed.shape[0], REST_WIDTH), wide)
        for choice in range(TOP):
            total += gates[:, choice : choice + 1] * (
                dot32(place_main_t[choice], main[:, at])
                + dot32(place_rest_t[choice, quarter], rest[:, :REST_WIDTH])
            )
        mixture[:, at] = total
    for flight in (flights, cotangent_flights, flights_d, flights_y):
        flight[1]()
    for copy in stores:
        copy.wait()


WEIGHT_PARTS = 3


def run_experts(normed, cotangent, gates, routes, weights):
    rows, width = normed.shape
    hidden_width = weights[0].shape[-1]
    low, wide = jnp.bfloat16, jnp.float32
    count = SOURCES * CAPACITY
    place_main, place_rest, place_gate, gate_lanes = dispatch_tables(routes)
    send_main = (place_main[0] + place_main[1]).T
    send_rest = (place_rest[0] + place_rest[1]).transpose(0, 2, 1)
    send_gate = place_gate.transpose(0, 2, 1)
    vmem = pl.BlockSpec(memory_space=pltpu.VMEM)
    anywhere = pl.BlockSpec(memory_space=pl.ANY)
    main = pltpu.VMEM((SOURCES, MAIN_ROWS, width), low)
    long_rest = pltpu.VMEM((SOURCES, REST_ROWS, REST_WIDTH + 128), low)
    rest = pltpu.VMEM((SOURCES, REST_ROWS, REST_WIDTH), low)
    flights = 8 * SOURCES
    return pl.pallas_call(
        experts_kernel,
        out_shape=(
            jax.ShapeDtypeStruct((rows, width), wide),
            jax.ShapeDtypeStruct((rows, width), wide),
            jax.ShapeDtypeStruct((rows, TOP), wide),
            *[jax.ShapeDtypeStruct((width, hidden_width), low)] * 2,
            jax.ShapeDtypeStruct((hidden_width, width), low),
        ),
        in_specs=[vmem] * 17 + [anywhere] * WEIGHT_PARTS,
        out_specs=[vmem] * 3 + [anywhere] * 3,
        scratch_shapes=[
            pltpu.VMEM((width, hidden_width), low),
            pltpu.VMEM((width, hidden_width), low),
            pltpu.VMEM((hidden_width, width), low),
            main, long_rest, main, rest, main, long_rest, main, rest,
            main, long_rest, main, long_rest, main, rest, main, rest,
            pltpu.VMEM((count, width), low),
            pltpu.VMEM((count, width), low),
            pltpu.VMEM((count, hidden_width), wide),
            pltpu.VMEM((count, hidden_width), wide),
            pltpu.VMEM((count, hidden_width), low),
            pltpu.VMEM((count, hidden_width), low),
            pltpu.VMEM((count, hidden_width), low),
            pltpu.VMEM((count, width), low),
            pltpu.VMEM((count, width), low),
            pltpu.VMEM((width, count), low),
            pltpu.SemaphoreType.DMA((3,)),
            pltpu.SemaphoreType.DMA((3,)),
            pltpu.SemaphoreType.DMA((flights,)),
            pltpu.SemaphoreType.DMA((flights,)),
        ],
        compiler_params=pltpu.CompilerParams(
            collective_id=3, has_side_effects=True, vmem_limit_bytes=60 * 2**20
        ),
        cost_estimate=pl.CostEstimate(
            flops=18 * count * width * hidden_width, bytes_accessed=32 * 2**20, transcendentals=0
        ),
        name="run_experts",
    )(
        normed, cotangent, gates, send_main, send_rest, send_gate, gate_lanes,
        place_main, place_rest, place_gate, *unpack_tables(), *weights,
    )


def others_of(ctx):
    return [(step, (ctx + step) % SOURCES) for step in range(1, SOURCES)]


def greet(dp, ctx):
    barrier = pltpu.get_barrier_semaphore()
    for _, other in others_of(ctx):
        pl.semaphore_signal(barrier, inc=1, device_id=(dp, other), device_id_type=MESH)
    return barrier


def send_blocks(pairs, dp, ctx, send, recv):
    copies = []
    for step, other in others_of(ctx):
        for source, place_in, first in pairs:
            copy = pltpu.make_async_remote_copy(
                src_ref=source(other),
                dst_ref=place_in,
                send_sem=send.at[first + step - 1],
                recv_sem=recv.at[first + step - 1],
                device_id=(dp, other),
                device_id_type=MESH,
            )
            copy.start()
            copies.append(copy)
    return copies


def to_heads_kernel(with_kv, rows_ref, *refs):
    if with_kv:
        head_rows, head_kv, packed, send, recv, local = refs
    else:
        head_rows, packed, send, recv, local = refs
    dp, ctx = lax.axis_index("dp"), lax.axis_index("ctx")
    barrier = greet(dp, ctx)
    half = rows_ref.shape[0] // 2
    for head in range(KEY_VALUE_HEADS):
        for core in range(2):
            packed[2 * head + core] = rows_ref[
                core * half : (core + 1) * half, head * HEADS_WIDE : (head + 1) * HEADS_WIDE
            ]
    pl.semaphore_wait(barrier, SOURCES - 1)

    def kv_of(other):
        start = QUERY_HEAD_COUNT * HEAD_SIZE + (other // 2) * 2 * HEAD_SIZE
        return rows_ref.at[:, pl.ds(pl.multiple_of(start, 128), 2 * HEAD_SIZE)]

    pairs = [(lambda other: packed.at[other], head_rows.at[ctx], 0)]
    if with_kv:
        pairs = [(kv_of, head_kv.at[ctx], SOURCES - 1)] + pairs
    copies = send_blocks(pairs, dp, ctx, send, recv)
    own = [pltpu.make_async_copy(packed.at[ctx], head_rows.at[ctx], local.at[0])]
    if with_kv:
        own.append(pltpu.make_async_copy(kv_of(ctx), head_kv.at[ctx], local.at[1]))
    for copy in own:
        copy.start()
    for copy in own + copies:
        copy.wait()


def to_heads(rows, with_kv, number):
    half = rows.shape[0] // 2
    low = jnp.bfloat16
    vmem = pl.BlockSpec(memory_space=pltpu.VMEM)
    count = (2 if with_kv else 1) * (SOURCES - 1)
    shapes = [jax.ShapeDtypeStruct((SOURCES, half, HEADS_WIDE), low)]
    if with_kv:
        shapes.append(jax.ShapeDtypeStruct((SOURCES, 2 * half, 2 * HEAD_SIZE), low))
    out = pl.pallas_call(
        functools.partial(to_heads_kernel, with_kv),
        out_shape=shapes,
        in_specs=[vmem],
        out_specs=[vmem] * len(shapes),
        scratch_shapes=[
            pltpu.VMEM((SOURCES, half, HEADS_WIDE), low),
            pltpu.SemaphoreType.DMA((count,)),
            pltpu.SemaphoreType.DMA((count,)),
            pltpu.SemaphoreType.DMA((2,)),
        ],
        compiler_params=pltpu.CompilerParams(
            collective_id=number, has_side_effects=True, vmem_limit_bytes=16 * 2**20
        ),
        cost_estimate=pl.CostEstimate(flops=0, bytes_accessed=4 * 2**20, transcendentals=0),
        name="to_heads",
    )(rows)
    return [part.reshape(-1, part.shape[-1]) for part in out]


def to_tokens_kernel(with_kv, head_rows, *refs):
    if with_kv:
        head_kv, out, rows_in, kv_in, send, recv = refs
    else:
        out, rows_in, send, recv = refs
    dp, ctx = lax.axis_index("dp"), lax.axis_index("ctx")
    barrier = greet(dp, ctx)
    half = head_rows.shape[1]
    pl.semaphore_wait(barrier, SOURCES - 1)
    pairs = [(lambda other: head_rows.at[other], rows_in.at[ctx], 0)]
    if with_kv:
        pairs = [(lambda other: head_kv.at[other], kv_in.at[ctx], SOURCES - 1)] + pairs
    copies = send_blocks(pairs, dp, ctx, send, recv)
    rows_in[ctx] = head_rows[ctx]
    if with_kv:
        kv_in[ctx] = head_kv[ctx]
    for copy in copies:
        copy.wait()
    for head in range(KEY_VALUE_HEADS):
        for core in range(2):
            out[
                core * half : (core + 1) * half, head * HEADS_WIDE : (head + 1) * HEADS_WIDE
            ] = rows_in[2 * head + core]
        if with_kv:
            start = QUERY_HEAD_COUNT * HEAD_SIZE + head * 2 * HEAD_SIZE
            out[:, start : start + 2 * HEAD_SIZE] = (
                kv_in[2 * head].astype(jnp.float32) + kv_in[2 * head + 1].astype(jnp.float32)
            ).astype(jnp.bfloat16)


def to_tokens(head_rows, head_kv, number):
    half = head_rows.shape[0] // SOURCES
    low = jnp.bfloat16
    vmem = pl.BlockSpec(memory_space=pltpu.VMEM)
    with_kv = head_kv is not None
    width = QUERY_HEAD_COUNT * HEAD_SIZE
    arrays = [head_rows.reshape(SOURCES, half, HEADS_WIDE)]
    landing = [pltpu.VMEM((SOURCES, half, HEADS_WIDE), low)]
    if with_kv:
        arrays.append(head_kv.reshape(SOURCES, 2 * half, 2 * HEAD_SIZE))
        landing.append(pltpu.VMEM((SOURCES, 2 * half, 2 * HEAD_SIZE), low))
        width += KEY_VALUE_HEADS * 2 * HEAD_SIZE
    count = len(arrays) * (SOURCES - 1)
    return pl.pallas_call(
        functools.partial(to_tokens_kernel, with_kv),
        out_shape=jax.ShapeDtypeStruct((2 * half, width), low),
        in_specs=[vmem] * len(arrays),
        out_specs=vmem,
        scratch_shapes=landing
        + [pltpu.SemaphoreType.DMA((count,)), pltpu.SemaphoreType.DMA((count,))],
        compiler_params=pltpu.CompilerParams(
            collective_id=number, has_side_effects=True, vmem_limit_bytes=16 * 2**20
        ),
        cost_estimate=pl.CostEstimate(flops=0, bytes_accessed=4 * 2**20, transcendentals=0),
        name="to_tokens",
    )(*arrays)


KEY_STEP = 256
QUERY_STEP = 256
GROUP = QUERY_HEAD_COUNT // KEY_VALUE_HEADS
HEADS_WIDE = GROUP * HEAD_SIZE


def allowed_block(block, pos, start):
    keys = lax.broadcasted_iota(jnp.int32, (KEY_STEP, QUERY_STEP), 0) + block * KEY_STEP
    return (keys <= pos) & (keys >= start)


def attend_kernel(low, high, pos_ref, start_ref, query_ref, kv_ref, kvt_ref, out_ref, outt_ref, log_ref):
    zeros = jnp.zeros((QUERY_STEP, HEAD_SIZE), jnp.bfloat16)

    @pl.loop(0, query_ref.shape[0] // QUERY_STEP)
    def _(tile):
        rows = pl.ds(pl.multiple_of(tile * QUERY_STEP, QUERY_STEP), QUERY_STEP)
        pos, start = pos_ref[:, rows], start_ref[:, rows]
        queries = query_ref[rows, :]
        padded = [
            jnp.concatenate([queries[:, h * HEAD_SIZE : (h + 1) * HEAD_SIZE], zeros], axis=1)
            for h in range(GROUP)
        ]

        def step(block, carry):
            keys = pl.ds(pl.multiple_of(block * KEY_STEP, KEY_STEP), KEY_STEP)
            kv = kv_ref[keys, :]
            values_t = kvt_ref[HEAD_SIZE:, keys]
            allowed = allowed_block(block, pos, start)
            new = []
            for h in range(GROUP):
                highest, total, summed = carry[h]
                scores = jnp.where(allowed, across(kv, padded[h]), NEGATIVE)
                new_high = jnp.maximum(highest, jnp.max(scores, axis=0, keepdims=True))
                weights = jnp.exp(scores - new_high)
                shrink = jnp.exp(highest - new_high)
                total = total * shrink + jnp.sum(weights, axis=0, keepdims=True)
                summed = summed * shrink + dot32(values_t, weights.astype(jnp.bfloat16))
                new.append((new_high, total, summed))
            return tuple(new)

        first = tuple(
            (
                jnp.full((1, QUERY_STEP), NEGATIVE, jnp.float32),
                jnp.zeros((1, QUERY_STEP), jnp.float32),
                jnp.zeros((HEAD_SIZE, QUERY_STEP), jnp.float32),
            )
            for _ in range(GROUP)
        )
        last = lax.fori_loop(low[tile], high[tile], step, first)
        pieces = []
        for h in range(GROUP):
            highest, total, summed = last[h]
            log_ref[h : h + 1, rows] = highest + jnp.log(total)
            summed = summed / total
            outt_ref[h, :, rows] = summed
            pieces.append(summed)
        out_ref[rows, :] = jnp.concatenate(pieces, axis=0).T.astype(jnp.bfloat16)


def attend_back_kernel(
    low, high, pos_ref, start_ref, query_ref, kv_ref, kvt_ref, outt_ref, log_ref, grad_ref,
    grad_query_ref, grad_kv_ref, sums,
):
    zeros = jnp.zeros((QUERY_STEP, HEAD_SIZE), jnp.bfloat16)
    sums[...] = jnp.zeros_like(sums)

    @pl.loop(0, query_ref.shape[0] // QUERY_STEP)
    def _(tile):
        rows = pl.ds(pl.multiple_of(tile * QUERY_STEP, QUERY_STEP), QUERY_STEP)
        pos, start = pos_ref[:, rows], start_ref[:, rows]
        queries, grads = query_ref[rows, :], grad_ref[rows, :]
        grads_t = grads.astype(jnp.float32).T
        query_pads, grad_pads, deltas, logs = [], [], [], []
        for h in range(GROUP):
            part = slice(h * HEAD_SIZE, (h + 1) * HEAD_SIZE)
            query_pads.append(jnp.concatenate([queries[:, part], zeros], axis=1))
            grad_pads.append(jnp.concatenate([zeros, grads[:, part]], axis=1))
            deltas.append(jnp.sum(grads_t[part, :] * outt_ref[h, :, rows], axis=0, keepdims=True))
            logs.append(log_ref[h : h + 1, rows])

        def step(block, carry):
            keys = pl.ds(pl.multiple_of(block * KEY_STEP, KEY_STEP), KEY_STEP)
            kv = kv_ref[keys, :]
            keys_t = kvt_ref[:HEAD_SIZE, keys]
            allowed = allowed_block(block, pos, start)
            new = []
            total = sums[keys, :]
            for h in range(GROUP):
                scores = jnp.where(allowed, across(kv, query_pads[h]), NEGATIVE)
                probs = jnp.exp(scores - logs[h])
                grad_probs = across(kv, grad_pads[h])
                grad_scores = (probs * (grad_probs - deltas[h])).astype(jnp.bfloat16)
                total += dot32(probs.astype(jnp.bfloat16), grad_pads[h])
                total += dot32(grad_scores, query_pads[h])
                new.append(carry[h] + dot32(keys_t, grad_scores))
            sums[keys, :] = total
            return tuple(new)

        first = tuple(jnp.zeros((HEAD_SIZE, QUERY_STEP), jnp.float32) for _ in range(GROUP))
        last = lax.fori_loop(low[tile], high[tile], step, first)
        factor = HEAD_SIZE ** (-0.5)
        grad_query_ref[rows, :] = (jnp.concatenate(last, axis=0) * factor).T.astype(jnp.bfloat16)

    grad_kv_ref[...] = sums[...].astype(jnp.bfloat16)


def attend_call(kernel, name, bounds, arrays, out_shape, scratch, matmuls, area):
    vmem = pl.BlockSpec(memory_space=pltpu.VMEM)
    return pl.pallas_call(
        kernel,
        out_shape=out_shape,
        grid_spec=pltpu.PrefetchScalarGridSpec(
            num_scalar_prefetch=2,
            grid=(1,),
            in_specs=[vmem] * len(arrays),
            out_specs=[vmem] * len(out_shape),
            scratch_shapes=scratch,
        ),
        compiler_params=pltpu.CompilerParams(vmem_limit_bytes=32 * 2**20),
        cost_estimate=pl.CostEstimate(
            flops=matmuls * 2 * HEAD_SIZE * area, bytes_accessed=8 * 2**20, transcendentals=area
        ),
        name=name,
    )(*bounds, *arrays)


def shards(
    tokens,
    segments,
    routes,
    gain_attn,
    w_query,
    key_weight,
    value_weight,
    w_out,
    w_router,
    gain_ffn,
    w_gate,
    w_up,
    w_down,
    cotangent,
):
    low = jnp.bfloat16
    wide = jnp.float32
    device_rows, width = tokens.shape
    sequence = segments.shape[0]
    half = device_rows // 2
    core = lax.axis_index("ctx") % 2
    ctx_count = lax.axis_size("ctx")
    slice_rows = w_query.shape[0]
    kv_shards = jnp.stack(
        [
            key_weight.reshape(slice_rows, KEY_VALUE_HEADS, HEAD_SIZE),
            value_weight.reshape(slice_rows, KEY_VALUE_HEADS, HEAD_SIZE),
        ],
        axis=2,
    ).reshape(slice_rows, 2 * KEY_VALUE_HEADS * HEAD_SIZE)
    shard = jnp.concatenate(
        [w_query, kv_shards, w_out, w_router, gain_attn[:, None], gain_ffn[:, None]], axis=1
    )
    shard = jnp.pad(shard, ((0, 0), (0, PACK - shard.shape[1])))
    packed, expert_weights = gather_weights(shard, w_gate[0], w_up[0], w_down[0])
    qkv_proj = packed[:, :2560]
    out_proj = packed[:, 2560:4096]
    router_proj = packed[:, 4096:4112]
    scale_one = packed[:, 4112].astype(wide)
    scale_two = packed[:, 4113].astype(wide)
    order = jnp.arange(ctx_count * half, dtype=jnp.int32)
    query_pos = (order // half) * device_rows + core * half + order % half
    first_of = jnp.stack([jnp.sum((segments < n).astype(jnp.int32)) for n in range(5)])
    starts = jnp.sum(
        jnp.where(segments[:, None] == jnp.arange(5, dtype=jnp.int32)[None, :], first_of[None, :], 0),
        axis=1,
    )
    query_start = lax.dynamic_slice_in_dim(
        starts.reshape(ctx_count, device_rows), core * half, half, axis=1
    ).reshape(-1)
    tiles = query_pos.reshape(-1, QUERY_STEP)
    bounds = (
        query_start.reshape(-1, QUERY_STEP)[:, 0] // KEY_STEP,
        tiles[:, -1] // KEY_STEP + 1,
    )
    mask_rows = (query_pos[None, :], query_start[None, :])

    residual = tokens.astype(wide)
    inverse_one = inverse_rms(residual)
    normed = (residual * inverse_one * scale_one).astype(low)
    qkv = jnp.dot(normed, qkv_proj, preferred_element_type=wide).astype(low)

    factor = HEAD_SIZE ** (-0.5)
    qkv = jnp.concatenate([qkv[:, :width] * factor, qkv[:, width:]], axis=1)
    head_queries, head_kv = to_heads(qkv, True, 4)
    head_kvt = head_kv.T
    count = head_queries.shape[0]
    area = GROUP * count * sequence // 3
    head_out, head_outt, log_total = attend_call(
        attend_kernel,
        "attend",
        bounds,
        (*mask_rows, head_queries, head_kv, head_kvt),
        (
            jax.ShapeDtypeStruct((count, HEADS_WIDE), low),
            jax.ShapeDtypeStruct((GROUP, HEAD_SIZE, count), wide),
            jax.ShapeDtypeStruct((GROUP, count), wide),
        ),
        [],
        2,
        area,
    )
    attended = to_tokens(head_out, None, 5)

    hidden_one = residual + contract_cols(attended, out_proj)
    inverse_two = inverse_rms(hidden_one)
    normed_two = (hidden_one * inverse_two * scale_two).astype(low)
    logits = jnp.dot(normed_two, router_proj, preferred_element_type=wide)
    picked = (
        routes[:, :, None] == jnp.arange(SOURCES, dtype=jnp.int32)[None, None, :]
    ).astype(wide)
    chosen = jnp.sum(picked * logits[:, None, :], axis=-1)
    gate_weights = jax.nn.softmax(chosen, axis=-1)
    grad_normed_two, mixture, grad_gates, *expert_grads = run_experts(
        normed_two, cotangent, gate_weights, routes, expert_weights
    )
    mixed = (hidden_one + mixture).astype(low)
    grad_y = cotangent.astype(wide)
    grad_chosen = gate_weights * (
        grad_gates - jnp.sum(gate_weights * grad_gates, axis=-1, keepdims=True)
    )
    grad_logits = jnp.sum(picked * grad_chosen[:, :, None], axis=1).astype(low)
    grad_normed_two = grad_normed_two + contract_cols(grad_logits, router_proj)
    grad_router_full = contract_rows(normed_two, grad_logits)
    grad_hidden_one, grad_gain_two = norm_backward(
        grad_normed_two, hidden_one, inverse_two, scale_two
    )
    grad_hidden_one = grad_hidden_one + grad_y
    grad_branch = grad_hidden_one.astype(low)
    grad_attended = jnp.dot(grad_branch, out_proj, preferred_element_type=wide).astype(low)

    (head_grads,) = to_heads(grad_attended, False, 6)
    head_grad_queries, head_grad_kv = attend_call(
        attend_back_kernel,
        "attend_back",
        bounds,
        (*mask_rows, head_queries, head_kv, head_kvt, head_outt, log_total, head_grads),
        (
            jax.ShapeDtypeStruct((count, HEADS_WIDE), low),
            jax.ShapeDtypeStruct((sequence, 2 * HEAD_SIZE), low),
        ),
        [pltpu.VMEM((sequence, 2 * HEAD_SIZE), wide)],
        5,
        area,
    )
    grad_qkv = to_tokens(head_grad_queries, head_grad_kv, 7)
    grad_normed = contract_cols(grad_qkv, qkv_proj)
    grad_residual, grad_gain_one = norm_backward(grad_normed, residual, inverse_one, scale_one)
    grad_input = (grad_residual + grad_hidden_one).astype(low)
    rest = jnp.concatenate(
        [
            grad_router_full.astype(low),
            grad_gain_one.astype(low)[:, None],
            grad_gain_two.astype(low)[:, None],
            jnp.zeros((width, PACK - 4114), low),
        ],
        axis=1,
    )
    share, (grad_gate, grad_up, grad_down) = scatter_sum(
        normed, grad_qkv, grad_branch, attended, rest, expert_grads
    )
    share = share.astype(wide)
    kv_share = share[:, 1536:2560].reshape(slice_rows, KEY_VALUE_HEADS, 2, HEAD_SIZE)
    return (
        mixed,
        grad_input,
        share[:, 4112],
        share[:, :1536],
        kv_share[:, :, 0].reshape(slice_rows, -1),
        kv_share[:, :, 1].reshape(slice_rows, -1),
        share[:, 2560:4096],
        share[:, 4096:4112],
        share[:, 4113],
        grad_gate[None],
        grad_up[None],
        grad_down[None],
    )


def solution(mesh):
    in_specs = (
        P(("dp", "ctx"), None),
        P("dp"),
        P(("dp", "ctx"), None),
        P(("dp", "ctx")),
        P(("dp", "ctx"), None),
        P(("dp", "ctx"), None),
        P(("dp", "ctx"), None),
        P(("dp", "ctx"), None),
        P(("dp", "ctx"), None),
        P(("dp", "ctx")),
        P("ctx", "dp", None),
        P("ctx", "dp", None),
        P("ctx", "dp", None),
        P(("dp", "ctx"), None),
    )
    out_specs = (
        P(("dp", "ctx"), None),
        P(("dp", "ctx"), None),
        P(("dp", "ctx")),
        P(("dp", "ctx"), None),
        P(("dp", "ctx"), None),
        P(("dp", "ctx"), None),
        P(("dp", "ctx"), None),
        P(("dp", "ctx"), None),
        P(("dp", "ctx")),
        P("ctx", "dp", None),
        P("ctx", "dp", None),
        P("ctx", "dp", None),
    )
    return jax.shard_map(shards, mesh=mesh, in_specs=in_specs, out_specs=out_specs, check_vma=False)
```

```python
import functools

import jax
import jax.numpy as jnp
import numpy as np
from jax import lax
from jax.experimental import pallas as pl
from jax.experimental.pallas import tpu as pltpu
from jax.sharding import PartitionSpec as P

QUERY_HEAD_COUNT = 24
KEY_VALUE_HEADS = 8
HEAD_SIZE = 64
TOP = 2

EPSILON = 1e-06
NEGATIVE = -1e30
SOURCES = 16
GROUP = QUERY_HEAD_COUNT // KEY_VALUE_HEADS
HEADS_WIDE = GROUP * HEAD_SIZE
MESH = pl.DeviceIdType.MESH

PACK = 4608
HALF = PACK // 2
QUARTER = PACK // 4
RING_ORDERS = (("x", "y", "z"), ("y", "z", "x"), ("z", "x", "y"))


def place():
    dp = lax.axis_index("dp")
    ctx = lax.axis_index("ctx")
    return {"y": dp // 2, "z": (ctx // 8) * 2 + dp % 2, "x": (ctx // 2) % 4, "core": ctx % 2}


def device_of(spot):
    z = spot["z"]
    return (spot["y"] * 2 + z % 2, (z // 2) * 8 + spot["x"] * 2 + spot["core"])


def moved(spot, axis, step):
    other = dict(spot)
    if axis == "core":
        other["core"] = 1 - spot["core"]
    else:
        other[axis] = (spot[axis] + step) % 4
    return other


def member(spot, step):
    index = (spot["x"] % 2) * 2 + spot["core"]
    target = (index // 2 + step // 2) % 2 * 2 + (index % 2 + step % 2) % 2
    other = dict(spot)
    other["x"] = (spot["x"] // 2) * 2 + target // 2
    other["core"] = target % 2
    return other, target


def partner(spot):
    other = dict(spot)
    other["z"] = spot["z"] // 2 * 2 + (spot["z"] + 1) % 2
    other["core"] = (spot["core"] + 1) % 2
    return other


def others_of(ctx):
    return [(step, (ctx + step) % SOURCES) for step in range(1, SOURCES)]


def meet(spot, heads):
    barrier = pltpu.get_barrier_semaphore()
    others = [member(spot, step)[0] for step in (1, 2, 3)] + [partner(spot)]
    others += [moved(spot, axis, step) for axis in "xyz" for step in (1, 2, 3)]
    others = [device_of(other) for other in others]
    others += [(lax.axis_index("dp"), other) for _, other in heads]
    for other in others:
        pl.semaphore_signal(barrier, inc=1, device_id=other, device_id_type=MESH)
    pl.semaphore_wait(barrier, len(others))


def region(spot, known, part, base):
    def pick(axis, value, size):
        return pl.ds(0, size) if axis in known else pl.ds(value, 1)

    z = spot["z"]
    if "x" in known:
        columns = pl.ds(base, HALF)
    else:
        columns = pl.ds(pl.multiple_of(base + (spot["x"] % 2) * QUARTER, 128), QUARTER)
    return (
        pick("y", spot["y"], 4),
        pick("z", z % 2, 2),
        pick("z", z // 2, 2),
        pick("x", spot["x"] // 2, 2),
        pl.ds(part * 16, 16),
        columns,
    )


def expert_rows(ref, spot, core, half=None):
    rows = ref.shape[0] // 8
    first = (spot["y"] * 2 + core) * rows
    if half is not None:
        rows //= 2
        first += half * rows
    return ref.at[pl.ds(pl.multiple_of(first, 32), rows)]


def half_region(where, axis, half):
    if axis == "y":
        return where[:1] + (pl.ds(half, 1),) + where[2:]
    return (pl.ds(2 * half, 2),) + where[1:]


def relay(ring, numbers, send, recv, whole, half):
    spot, axis = ring

    def copy(ref, step, number):
        return pltpu.make_async_remote_copy(
            src_ref=ref,
            dst_ref=ref,
            send_sem=send.at[numbers + number],
            recv_sem=recv.at[numbers + number],
            device_id=device_of(moved(spot, axis, step)),
            device_id_type=MESH,
        )

    first = [copy(whole(spot), 1, 0), copy(whole(spot), 3, 1)]
    second = [copy(half(moved(spot, axis, 3), 0), 1, 2), copy(half(moved(spot, axis, 1), 1), 3, 3)]
    return first, second


def gather_kernel(
    shard, merge, tokens, own_gate, own_up, own_down,
    out, gate_out, up_out, down_out, head_rows, head_kv, scales,
    pieces, joined, qkv_w, rest_w, normed, qkv, packed,
    send0, recv0, send, recv, send_core, recv_core, local,
    swap_send, swap_recv, swap_local, line_send, line_recv, mate_send, mate_recv, ring_send, ring_recv,
    head_send, head_recv, head_local,
):
    spot = place()
    dp, ctx = lax.axis_index("dp"), lax.axis_index("ctx")
    meet(spot, others_of(ctx))
    mate = moved(spot, "core", 1)
    stays = spot["core"] == spot["z"] % 2
    experts = ((own_gate, gate_out), (own_up, up_out), (own_down, down_out))

    def swaps():
        return [
            pltpu.make_async_remote_copy(
                src_ref=own,
                dst_ref=expert_rows(whole, spot, spot["z"] % 2),
                send_sem=swap_send.at[n],
                recv_sem=swap_recv.at[n],
                device_id=device_of(partner(spot)),
                device_id_type=MESH,
            )
            for n, (own, whole) in enumerate(experts)
        ]

    def stays_here():
        return [
            pltpu.make_async_copy(own, expert_rows(whole, spot, spot["core"]), swap_local.at[n])
            for n, (own, whole) in enumerate(experts)
        ]

    def line(n):
        whole = experts[n][1]
        return relay(
            (spot, "y"),
            4 * n,
            line_send,
            line_recv,
            lambda at: expert_rows(whole, at, spot["core"]),
            lambda at, half: expert_rows(whole, at, spot["core"], half),
        )

    def to_mates(step):
        source = moved(spot, "y", 4 - step)
        return [
            pltpu.make_async_remote_copy(
                src_ref=expert_rows(whole, source, spot["core"]),
                dst_ref=expert_rows(whole, source, spot["core"]),
                send_sem=mate_send.at[3 * step + n],
                recv_sem=mate_recv.at[3 * step + n],
                device_id=device_of(mate),
                device_id_type=MESH,
            )
            for n, (own, whole) in enumerate(experts)
        ]

    def start_all(copies):
        for copy in copies:
            copy.start()

    @pl.when(stays)
    def _():
        start_all(stays_here())

    @pl.when(jnp.logical_not(stays))
    def _():
        start_all(swaps())

    index = (spot["x"] % 2) * 2 + spot["core"]
    quarter = spot["core"] * 2 + spot["x"] % 2
    copies = []
    for step in (1, 2, 3):
        other, target = member(spot, step)
        goal = other["core"] * 2 + other["x"] % 2
        copy = pltpu.make_async_remote_copy(
            src_ref=shard.at[:, pl.ds(pl.multiple_of(goal * QUARTER, 128), QUARTER)],
            dst_ref=pieces.at[index],
            send_sem=send0.at[step - 1],
            recv_sem=recv0.at[step - 1],
            device_id=device_of(other),
            device_id_type=MESH,
        )
        copy.start()
        copies.append(copy)
    pieces[index] = shard[:, pl.ds(pl.multiple_of(quarter * QUARTER, 128), QUARTER)]
    for copy in copies:
        copy.wait()
    joined[...] = jnp.dot(
        merge[...], pieces[...].reshape(64, QUARTER), preferred_element_type=jnp.float32
    ).astype(jnp.bfloat16)
    base = pl.multiple_of(spot["core"] * HALF, 128)
    mine = region(spot, "", 0, base)
    own = pltpu.make_async_copy(
        joined,
        out.at[spot["y"], spot["z"] % 2, spot["z"] // 2, spot["x"] // 2, :, mine[5]],
        local,
    )
    own.start()
    own.wait()
    core_copies = []

    def to_mate(number, where):
        copy = pltpu.make_async_remote_copy(
            src_ref=out.at[where],
            dst_ref=out.at[where],
            send_sem=send_core.at[number],
            recv_sem=recv_core.at[number],
            device_id=device_of(mate),
            device_id_type=MESH,
        )
        copy.start()
        core_copies.append(copy)

    flights, relays, finals = {}, [], []
    for stage in range(3):
        for part, order in enumerate(RING_ORDERS):
            axis, known = order[stage], order[:stage]
            if stage > 0:
                for copy in flights[part]:
                    copy.wait_recv()
            where = region(spot, known, part, base)
            if stage == 2:
                ring = relay(
                    (spot, axis),
                    4 * part,
                    ring_send,
                    ring_recv,
                    lambda at, known=known, part=part: out.at[region(at, known, part, base)],
                    lambda at, half, known=known, part=part, axis=axis: out.at[
                        half_region(region(at, known, part, base), axis, half)
                    ],
                )
                start_all(ring[0])
                relays.append(ring)
                finals.append((axis, known))
                to_mate(part * 4, where)
                continue
            started = []
            for step in (1, 3, 2):
                number = (stage * 3 + part) * 3 + step - 1
                copy = pltpu.make_async_remote_copy(
                    src_ref=out.at[where],
                    dst_ref=out.at[where],
                    send_sem=send.at[number],
                    recv_sem=recv.at[number],
                    device_id=device_of(moved(spot, axis, step)),
                    device_id_type=MESH,
                )
                copy.start()
                started.append(copy)
            flights[part] = started
            copies += started
        if stage == 1:

            @pl.when(stays)
            def _():
                for copy in stays_here():
                    copy.wait()

            @pl.when(jnp.logical_not(stays))
            def _():
                for copy in swaps():
                    copy.wait()


    mates = {step: to_mates(step) for step in (1, 3, 2)}

    def pass_on(ring):
        first, second = ring
        for number in range(2):
            first[number].wait_recv()
            second[number].start()

    residual = tokens[...].astype(jnp.float32)
    inverse = lax.rsqrt(jnp.mean(residual * residual, axis=1, keepdims=True) + EPSILON)
    for ring in relays:
        pass_on(ring)
    lines = [line(n) for n in range(3)]
    for first, _ in lines:
        start_all(first)
    own_mates = to_mates(0)
    for part, (axis, _) in enumerate(finals):
        for step in (1, 3):
            to_mate(part * 4 + step, region(moved(spot, axis, 4 - step), RING_ORDERS[part][:2], part, base))
    for part, (_, second) in enumerate(relays):
        for copy in second:
            copy.wait_recv()
        axis = RING_ORDERS[part][2]
        to_mate(part * 4 + 2, region(moved(spot, axis, 2), RING_ORDERS[part][:2], part, base))
    for copy in core_copies:
        copy.wait_recv()
    kv_at = QUERY_HEAD_COUNT * HEAD_SIZE
    qkv_width = qkv.shape[1]
    loads = [
        pltpu.make_async_copy(
            out.at[:, :, :, :, :, pl.ds(PACK - 512, 128)], rest_w, head_local.at[2]
        ),
        pltpu.make_async_copy(out.at[:, :, :, :, :, pl.ds(0, qkv_width)], qkv_w, head_local.at[3]),
    ]
    for load in loads:
        load.start()
    loads[0].wait()
    gains = rest_w[...].reshape(1536, 128).astype(jnp.float32).T
    scales[...] = gains[16:24, :]
    normed[...] = (residual * inverse * gains[16:17, :]).astype(jnp.bfloat16)
    loads[1].wait()
    factor = HEAD_SIZE ** (-0.5)

    @pl.loop(0, qkv_width // 256)
    def _(n):
        at = pl.ds(pl.multiple_of(n * 256, 256), 256)
        rows = jnp.dot(
            normed[...], qkv_w[:, :, :, :, :, at].reshape(1536, 256), preferred_element_type=jnp.float32
        )
        qkv[:, at] = (rows * jnp.where(n < kv_at // 256, factor, 1.0)).astype(jnp.bfloat16)

    half = tokens.shape[0] // 2
    for head in range(KEY_VALUE_HEADS):
        for core in range(2):
            packed[2 * head + core] = qkv[
                core * half : (core + 1) * half, head * HEADS_WIDE : (head + 1) * HEADS_WIDE
            ]

    def kv_of(other):
        start = kv_at + (other // 2) * 2 * HEAD_SIZE
        return qkv.at[:, pl.ds(pl.multiple_of(start, 128), 2 * HEAD_SIZE)]

    own_heads = [
        pltpu.make_async_copy(packed.at[ctx], head_rows.at[ctx], head_local.at[0]),
        pltpu.make_async_copy(kv_of(ctx), head_kv.at[ctx], head_local.at[1]),
    ]
    for copy in own_heads:
        copy.start()
    head_copies = []
    for step, other in others_of(ctx):
        for source, place_in, first in (
            (kv_of(other), head_kv.at[ctx], SOURCES),
            (packed.at[other], head_rows.at[ctx], 0),
        ):
            copy = pltpu.make_async_remote_copy(
                src_ref=source,
                dst_ref=place_in,
                send_sem=head_send.at[first + step],
                recv_sem=head_recv.at[first + step],
                device_id=(dp, other),
                device_id_type=MESH,
            )
            copy.start()
            head_copies.append(copy)
    start_all(own_mates)
    for n, ring in enumerate(lines):
        pass_on(ring)
        mates[1][n].start()
        mates[3][n].start()
    for n, (_, second) in enumerate(lines):
        for copy in second:
            copy.wait_recv()
        mates[2][n].start()
    line_copies = [copy for first, second in lines + relays for copy in first + second]
    for copy in own_heads + head_copies:
        copy.wait()
    for copy in copies[3:] + line_copies:
        copy.wait_send()
    for copy in core_copies:
        copy.wait_send()
    for copy in own_mates + mates[1] + mates[2] + mates[3]:
        copy.wait()


def gather_weights(shard, tokens, gate, up, down):
    shard = jnp.pad(shard, ((0, 4), (0, 0)))
    target, source = np.arange(48)[:, None], np.arange(64)[None, :]
    merge = jnp.asarray(
        (target // 12 == source // 16) & (target % 12 == source % 16), jnp.bfloat16
    )
    vmem = pl.BlockSpec(memory_space=pltpu.VMEM)
    anywhere = pl.BlockSpec(memory_space=pltpu.HBM)
    low = jnp.bfloat16
    rows, width = tokens.shape
    qkv_width = QUERY_HEAD_COUNT * HEAD_SIZE + 2 * KEY_VALUE_HEADS * HEAD_SIZE
    experts = [
        jax.ShapeDtypeStruct((8 * part.shape[0], part.shape[1]), low) for part in (gate, up, down)
    ]
    dma = pltpu.SemaphoreType.DMA
    packed, *rest = pl.pallas_call(
        gather_kernel,
        out_shape=[jax.ShapeDtypeStruct((4, 2, 2, 2, 48, PACK), low)]
        + experts
        + [
            jax.ShapeDtypeStruct((SOURCES, rows // 2, HEADS_WIDE), low),
            jax.ShapeDtypeStruct((SOURCES, rows, 2 * HEAD_SIZE), low),
            jax.ShapeDtypeStruct((8, width), jnp.float32),
        ],
        in_specs=[vmem] * 3 + [anywhere] * 3,
        out_specs=[anywhere] * 4 + [vmem] * 3,
        scratch_shapes=[
            pltpu.VMEM((4, 16, QUARTER), low),
            pltpu.VMEM((48, QUARTER), low),
            pltpu.VMEM((4, 2, 2, 2, 48, qkv_width), low),
            pltpu.VMEM((4, 2, 2, 2, 48, 128), low),
            pltpu.VMEM((rows, width), low),
            pltpu.VMEM((rows, qkv_width), low),
            pltpu.VMEM((SOURCES, rows // 2, HEADS_WIDE), low),
            dma((3,)), dma((3,)), dma((18,)), dma((18,)), dma((12,)), dma((12,)), dma,
            dma((3,)), dma((3,)), dma((3,)), dma((12,)), dma((12,)), dma((12,)), dma((12,)),
            dma((12,)), dma((12,)),
            dma((2 * SOURCES,)), dma((2 * SOURCES,)), dma((4,)),
        ],
        compiler_params=pltpu.CompilerParams(
            collective_id=1, has_side_effects=True, vmem_limit_bytes=62 * 2**20
        ),
        cost_estimate=pl.CostEstimate(
            flops=2 * rows * width * qkv_width, bytes_accessed=40 * 2**20, transcendentals=0
        ),
        name="gather_weights",
    )(shard, merge, tokens, gate, up, down)
    return packed.reshape(1536, PACK), rest[:3], *rest[3:]


EARLY = 1536
SCATTER_ORDERS = (("x", "y", "z"), ("y", "z", "x"), ("z", "x", "y"))


def cut(spot, known, part, half):
    z = spot["z"]

    def pick(axis, value, size):
        return pl.ds(0, size) if axis in known else pl.ds(value, 1)

    columns = pl.ds(0, half)
    if "x" not in known:
        columns = pl.ds(pl.multiple_of((spot["x"] % 2) * (half // 2), 128), half // 2)
    return (
        pick("y", spot["y"], 4),
        pick("z", z % 2, 2),
        pick("z", z // 2, 2),
        pick("x", spot["x"] // 2, 2),
        pl.ds(part * 16, 16),
        columns,
    )


def landing_shape(known, half):
    return (
        4 if "y" in known else 1,
        2 if "z" in known else 1,
        2 if "z" in known else 1,
        2 if "x" in known else 1,
        16,
        half if "x" in known else half // 2,
    )


class Scatter:
    def __init__(self, spot, split, grads, total, done, packed, out, sems, landing):
        self.spot, self.split, self.grads, self.total, self.out = spot, split, grads, total, out
        self.done, self.packed = done, packed
        self.send_core, self.recv_core, self.send, self.recv, self.send_last, self.recv_last = sems
        self.landing = (landing[:3], landing[3:6], landing[6:9])
        self.half = total.shape[-1]
        self.base = pl.multiple_of(spot["core"] * self.half, 128)
        self.pending, self.copies = [], []

    def start(self):
        mate = moved(self.spot, "core", 1)
        mate_base = pl.multiple_of(mate["core"] * self.half, 128)
        for part in range(3):
            rows = pl.ds(part * 16, 16)
            copy = pltpu.make_async_remote_copy(
                src_ref=self.grads.at[:, :, :, :, rows, pl.ds(mate_base, self.half)],
                dst_ref=self.total.at[:, :, :, :, rows, :],
                send_sem=self.send_core.at[part],
                recv_sem=self.recv_core.at[part],
                device_id=device_of(mate),
                device_id_type=MESH,
            )
            copy.start()
            self.copies.append(copy)

    def first(self):
        cores = list(self.copies)
        for part in range(3):
            rows = pl.ds(part * 16, 16)
            cores[part].wait_recv()

            @pl.loop(0, 32)
            def _(block):
                at = (block // 8, (block // 4) % 2, (block // 2) % 2, block % 2, rows)
                self.total[at] = (
                    self.grads[at + (pl.ds(self.base, self.half),)].astype(jnp.float32)
                    + self.total[at].astype(jnp.float32)
                ).astype(jnp.bfloat16)

            self.pending.append(self.ring(part, 0))

    def ring(self, part, stage):
        axis, known = SCATTER_ORDERS[part][2 - stage], SCATTER_ORDERS[part][: 2 - stage]
        started = []
        for step in (1, 3, 2):
            other = moved(self.spot, axis, step)
            number = (stage * 3 + part) * 3 + step - 1
            copy = pltpu.make_async_remote_copy(
                src_ref=self.total.at[cut(other, known, part, self.half)],
                dst_ref=self.landing[stage][part].at[step - 1],
                send_sem=self.send.at[number],
                recv_sem=self.recv.at[number],
                device_id=device_of(other),
                device_id_type=MESH,
            )
            copy.start()
            started.append(copy)
        self.copies += started
        return started

    def next(self, stage):
        for part in range(3):
            known = SCATTER_ORDERS[part][: 2 - stage]
            for copy in self.pending[part]:
                copy.wait_recv()
            self.add(known, part, self.landing[stage][part])
            if stage < 2:
                self.pending[part] = self.ring(part, stage + 1)

    def add(self, known, part, landing):
        spot = self.spot
        shape = landing_shape(known, self.half)
        columns = cut(spot, known, part, self.half)[5]

        def body(block):
            a, b, c, d = (
                block // (shape[1] * shape[2] * shape[3]),
                (block // (shape[2] * shape[3])) % shape[1],
                (block // shape[3]) % shape[2],
                block % shape[3],
            )
            at = (
                a + (0 if "y" in known else spot["y"]),
                b + (0 if "z" in known else spot["z"] % 2),
                c + (0 if "z" in known else spot["z"] // 2),
                d + (0 if "x" in known else spot["x"] // 2),
                pl.ds(part * 16, 16),
                columns,
            )
            summed = self.total[at].astype(jnp.float32)
            for step in range(3):
                summed += landing[step, a, b, c, d].astype(jnp.float32)
            self.total[at] = summed.astype(jnp.bfloat16)

        count = shape[0] * shape[1] * shape[2] * shape[3]
        if count == 1:
            body(0)
        else:
            pl.loop(0, count)(body)

    def finish(self):
        spot = self.spot
        quarter = self.half // 2
        index = (spot["x"] % 2) * 2 + spot["core"]
        place_in = spot["core"] * 2 + spot["x"] % 2
        mine = cut(spot, "", 0, self.half)
        self.done[...] = self.total[
            spot["y"], spot["z"] % 2, spot["z"] // 2, spot["x"] // 2, :, mine[5]
        ]
        self.packed[...] = (
            jnp.dot(self.split[...], self.done[...], preferred_element_type=jnp.float32)
            .astype(jnp.bfloat16)
            .reshape(4, 16, quarter)
        )
        columns = pl.ds(pl.multiple_of(place_in * quarter, 128), quarter)
        self.last = []
        for step in (1, 2, 3):
            other, target = member(spot, step)
            copy = pltpu.make_async_remote_copy(
                src_ref=self.packed.at[target],
                dst_ref=self.out.at[:, columns],
                send_sem=self.send_last.at[step - 1],
                recv_sem=self.recv_last.at[step - 1],
                device_id=device_of(other),
                device_id_type=MESH,
            )
            copy.start()
            self.last.append(copy)
        self.out[:, columns] = self.packed[index]

    def end(self):
        for copy in self.last:
            copy.wait()
        for copy in self.copies:
            copy.wait_send()


def scatter_kernel(
    head_rows, head_kv, tokens, scales, grad_hidden, branch, attended, router_grad, gain_grad, split,
    packed_w, grad_gate, grad_up, grad_down,
    grad_input, out, late_out, gate_out, up_out, down_out,
    rows_in, kv_in, grad_qkv, grad_normed, normed,
    mate_send, mate_recv, own_sem, line_send, line_recv, swap_send, swap_recv,
    head_send, head_recv, weight_sem,
    *buffers,
):
    spot = place()
    dp, ctx = lax.axis_index("dp"), lax.axis_index("ctx")
    held, mates, lines, results, arrived = (buffers[3 * n : 3 * n + 3] for n in range(5))
    early = Scatter(spot, split, *buffers[15:19], out, buffers[19:25], buffers[25:34])
    late = Scatter(spot, split, *buffers[34:38], late_out, buffers[38:44], buffers[44:])
    wholes, finals = (grad_gate, grad_up, grad_down), (gate_out, up_out, down_out)
    mate = moved(spot, "core", 1)
    qkv_width = grad_qkv.shape[1]
    load = pltpu.make_async_copy(
        packed_w.at[:, :, :, :, :, pl.ds(0, qkv_width)],
        late.grads.at[:, :, :, :, :, pl.ds(0, qkv_width)],
        weight_sem,
    )
    load.start()
    own_copies, mate_copies = [], []
    for n, whole in enumerate(wholes):
        for y in range(4):
            rows = whole.shape[0] // 8

            def part(core, whole=whole, y=y, rows=rows):
                return whole.at[pl.ds(pl.multiple_of((2 * y + core) * rows, 64), rows)]

            own = pltpu.make_async_copy(part(spot["core"]), held[n].at[y], own_sem.at[4 * n + y])
            own.start()
            own_copies.append(own)
            mate_copies.append(
                pltpu.make_async_remote_copy(
                    src_ref=part(mate["core"]),
                    dst_ref=mates[n].at[y],
                    send_sem=mate_send.at[4 * n + y],
                    recv_sem=mate_recv.at[4 * n + y],
                    device_id=device_of(mate),
                    device_id_type=MESH,
                )
            )
    meet(spot, others_of(ctx))
    for copy in mate_copies:
        copy.start()
    head_copies = []
    for step, other in others_of(ctx):
        for source, place_in, first in ((head_kv, kv_in, SOURCES), (head_rows, rows_in, 0)):
            copy = pltpu.make_async_remote_copy(
                src_ref=source.at[other],
                dst_ref=place_in.at[ctx],
                send_sem=head_send.at[first + step],
                recv_sem=head_recv.at[first + step],
                device_id=(dp, other),
                device_id_type=MESH,
            )
            copy.start()
            head_copies.append(copy)
    rows_in[ctx] = head_rows[ctx]
    kv_in[ctx] = head_kv[ctx]

    tile = 256
    grads_shape = (4, 2, 2, 2, 48, tile)

    def fill(turned, right, grads):
        @pl.loop(0, right.shape[1] // tile)
        def _(n):
            at = pl.ds(pl.multiple_of(n * tile, tile), tile)
            grads[:, :, :, :, :, at] = (
                jnp.dot(turned, right[:, at], preferred_element_type=jnp.float32)
                .astype(jnp.bfloat16)
                .reshape(grads_shape)
            )

    fill(branch[...].T, attended, early.grads)
    early.start()

    line_copies = []
    for n in range(3):
        for copy in mate_copies[4 * n : 4 * n + 4]:
            copy.wait_recv()
        for copy in own_copies[4 * n : 4 * n + 4]:
            copy.wait()

        @pl.loop(0, 4)
        def _(y, n=n):
            held[n][y] = (
                held[n][y].astype(jnp.float32) + mates[n][y].astype(jnp.float32)
            ).astype(jnp.bfloat16)

        for step in (1, 3, 2):
            other = moved(spot, "y", step)
            copy = pltpu.make_async_remote_copy(
                src_ref=held[n].at[other["y"]],
                dst_ref=lines[n].at[step - 1],
                send_sem=line_send.at[3 * n + step - 1],
                recv_sem=line_recv.at[3 * n + step - 1],
                device_id=device_of(other),
                device_id_type=MESH,
            )
            copy.start()
            line_copies.append(copy)

    early.first()

    half = tokens.shape[0] // 2
    residual = tokens[...].astype(jnp.float32)
    inverse = lax.rsqrt(jnp.mean(residual * residual, axis=1, keepdims=True) + EPSILON)
    unit = residual * inverse
    scale = scales[0:1, :]
    normed[...] = (unit * scale).astype(jnp.bfloat16)
    for copy in head_copies:
        copy.wait_recv()
    for head in range(KEY_VALUE_HEADS):
        for core in range(2):
            grad_qkv[
                core * half : (core + 1) * half, head * HEADS_WIDE : (head + 1) * HEADS_WIDE
            ] = rows_in[2 * head + core]
        start = QUERY_HEAD_COUNT * HEAD_SIZE + head * 2 * HEAD_SIZE
        grad_qkv[:, start : start + 2 * HEAD_SIZE] = (
            kv_in[2 * head].astype(jnp.float32) + kv_in[2 * head + 1].astype(jnp.float32)
        ).astype(jnp.bfloat16)
    load.wait()
    grad_normed[...] = jnp.zeros_like(grad_normed)

    @pl.loop(0, qkv_width // tile)
    def _(n):
        at = pl.ds(pl.multiple_of(n * tile, tile), tile)
        grad_normed[...] += contract_cols(
            grad_qkv[:, at], late.grads[:, :, :, :, :, at].reshape(1536, tile)
        )

    fill(normed[...].T, grad_qkv, late.grads)
    gain_column = jnp.sum(grad_normed[...] * unit, axis=0, keepdims=True)
    lanes = lax.broadcasted_iota(jnp.int32, (1536, 128), 1)
    first_column = jnp.broadcast_to(gain_column, (128, 1536)).T
    second_column = jnp.broadcast_to(gain_grad[...], (128, 1536)).T
    rest = jnp.where(
        lanes < 16,
        router_grad[...].astype(jnp.float32),
        jnp.where(lanes == 16, first_column, jnp.where(lanes == 17, second_column, 0.0)),
    )
    at = qkv_width
    late.grads[:, :, :, :, :, at : at + 128] = rest.astype(jnp.bfloat16).reshape(4, 2, 2, 2, 48, 128)
    late.grads[:, :, :, :, :, at + 128 :] = jnp.zeros(
        (4, 2, 2, 2, 48, late.grads.shape[-1] - at - 128), jnp.bfloat16
    )
    late.start()
    early.next(0)
    grads_here = grad_normed[...] * scale
    grads_here = inverse * (
        grads_here - unit * jnp.mean(grads_here * unit, axis=1, keepdims=True)
    )
    grad_input[...] = (grads_here + grad_hidden[...]).astype(jnp.bfloat16)
    late.first()
    early.next(1)
    sum_lines(spot, held, lines, line_copies, results)
    swap_results(spot, results, arrived, swap_send, swap_recv, True)
    late.next(0)
    early.next(2)
    early.finish()
    late.next(1)
    late.next(2)
    late.finish()
    swap_results(spot, results, arrived, swap_send, swap_recv, False)
    stays = spot["core"] == spot["z"] % 2

    @pl.when(stays)
    def _():
        for result, final in zip(results, finals):
            final[...] = result[...]

    @pl.when(jnp.logical_not(stays))
    def _():
        for result, final in zip(arrived, finals):
            final[...] = result[...]

    early.end()
    late.end()
    for copy in mate_copies + head_copies + line_copies:
        copy.wait_send()


def sum_lines(spot, held, lines, line_copies, results):
    for copy in line_copies:
        copy.wait_recv()
    for mine, line, result in zip(held, lines, results):
        total = mine[spot["y"]].astype(jnp.float32)
        for step in range(3):
            total += line[step].astype(jnp.float32)
        result[...] = total.astype(jnp.bfloat16)


def swap_results(spot, results, arrived, send, recv, start):
    @pl.when(spot["core"] != spot["z"] % 2)
    def _():
        for n, (result, place_in) in enumerate(zip(results, arrived)):
            copy = pltpu.make_async_remote_copy(
                src_ref=result,
                dst_ref=place_in,
                send_sem=send.at[n],
                recv_sem=recv.at[n],
                device_id=device_of(partner(spot)),
                device_id_type=MESH,
            )
            if start:
                copy.start()
            else:
                copy.wait()


def scatter_sum(
    head_rows, head_kv, tokens, scales, grad_hidden, branch, attended, router_grad, gain_grad, packed,
    expert_grads,
):
    source, target = np.arange(48)[None, :], np.arange(64)[:, None]
    split = jnp.asarray(
        (source // 12 == target // 16) & (source % 12 == target % 16), jnp.bfloat16
    )
    low = jnp.bfloat16
    dma = pltpu.SemaphoreType.DMA
    blocks = [(part.shape[0] // 8, part.shape[1]) for part in expert_grads]
    buffers = [pltpu.VMEM((4,) + block, low) for block in blocks] * 2
    buffers += [pltpu.VMEM((3,) + block, low) for block in blocks]
    buffers += [pltpu.VMEM(block, low) for block in blocks] * 2
    for columns in (EARLY, PACK - EARLY):
        buffers += [
            pltpu.VMEM((4, 2, 2, 2, 48, columns), low),
            pltpu.VMEM((4, 2, 2, 2, 48, columns // 2), low),
            pltpu.VMEM((48, columns // 4), low),
            pltpu.VMEM((4, 16, columns // 4), low),
            dma((3,)), dma((3,)), dma((27,)), dma((27,)), dma((3,)), dma((3,)),
        ]
        buffers += [
            pltpu.VMEM((3,) + landing_shape(order[: 2 - stage], columns // 2), low)
            for stage in range(3)
            for order in SCATTER_ORDERS
        ]
    vmem = pl.BlockSpec(memory_space=pltpu.VMEM)
    anywhere = pl.BlockSpec(memory_space=pltpu.HBM)
    rows, width = tokens.shape
    head_rows = head_rows.reshape(SOURCES, rows // 2, HEADS_WIDE)
    head_kv = head_kv.reshape(SOURCES, rows, 2 * HEAD_SIZE)
    qkv_width = QUERY_HEAD_COUNT * HEAD_SIZE + 2 * KEY_VALUE_HEADS * HEAD_SIZE
    grad_input, out, late_out, *finals = pl.pallas_call(
        scatter_kernel,
        out_shape=[jax.ShapeDtypeStruct((rows, width), low)]
        + [jax.ShapeDtypeStruct((16, columns), low) for columns in (EARLY, PACK - EARLY)]
        + [jax.ShapeDtypeStruct(block, low) for block in blocks],
        in_specs=[vmem] * 10 + [anywhere] * 4,
        out_specs=[vmem] * 6,
        scratch_shapes=[
            pltpu.VMEM(head_rows.shape, low),
            pltpu.VMEM(head_kv.shape, low),
            pltpu.VMEM((rows, qkv_width), low),
            pltpu.VMEM((rows, width), jnp.float32),
            pltpu.VMEM((rows, width), low),
            dma((12,)), dma((12,)), dma((12,)), dma((9,)), dma((9,)), dma((3,)), dma((3,)),
            dma((2 * SOURCES,)), dma((2 * SOURCES,)), dma,
        ]
        + buffers,
        compiler_params=pltpu.CompilerParams(
            collective_id=2, has_side_effects=True, vmem_limit_bytes=62 * 2**20
        ),
        cost_estimate=pl.CostEstimate(
            flops=2 * rows * width * 6656, bytes_accessed=28 * 2**20, transcendentals=0
        ),
        name="scatter_sum",
    )(
        head_rows, head_kv, tokens, scales, grad_hidden, branch, attended, router_grad, gain_grad, split,
        packed.reshape(4, 2, 2, 2, 48, PACK), *expert_grads,
    )
    return grad_input, out[:12], late_out[:12], [final.astype(jnp.float32) for final in finals]


def contract_cols(left, right):
    return lax.dot_general(
        left, right, (((1,), (1,)), ((), ())), preferred_element_type=jnp.float32
    )


MAIN_ROWS = 32
REST_ROWS = 16
REST_WIDTH = 384
CAPACITY = 36
TILE = 256


def across(left, right):
    return lax.dot_general(
        left, right, (((1,), (1,)), ((), ())), preferred_element_type=jnp.float32
    )


def dot32(left, right):
    return jnp.dot(left, right, preferred_element_type=jnp.float32)


def tiles(extent, body):
    pl.loop(0, extent // TILE)(lambda n: body(pl.ds(pl.multiple_of(n * TILE, TILE), TILE)))


def ones_at(condition):
    return jnp.where(condition, 1.0, 0.0).astype(jnp.bfloat16)


def in_three(column, lanes):
    first = column.astype(jnp.bfloat16).astype(jnp.float32)
    second = (column - first).astype(jnp.bfloat16).astype(jnp.float32)
    third = column - first - second
    return jnp.where(lanes % 3 == 0, first, jnp.where(lanes % 3 == 1, second, third))


def unpack_tables():
    row = np.arange(4 * CAPACITY)[:, None]
    device, slot = row // CAPACITY, row % CAPACITY
    main = np.arange(4 * MAIN_ROWS)[None, :]
    from_main = (device == main // MAIN_ROWS) & (slot == main % MAIN_ROWS)
    rest = np.arange(4 * REST_ROWS)[None, :]
    from_rest = np.stack(
        [
            (device == rest // REST_ROWS)
            & ((rest // 4) % 4 == quarter)
            & (slot == MAIN_ROWS + rest % 4)
            for quarter in range(4)
        ]
    )
    from_gate = (device == rest // REST_ROWS) & (slot % REST_ROWS == rest % REST_ROWS)
    lane_mask = np.arange(128)[None, :] // 3 == slot // REST_ROWS
    return [
        jnp.asarray(table, jnp.bfloat16)
        for table in (from_main, from_main.T, from_rest, from_rest.transpose(0, 2, 1), from_gate, from_gate.T)
    ] + [jnp.asarray(lane_mask, jnp.float32)]


def place_rows(routes, axis):
    rows = routes[0].shape[axis]
    experts = lax.broadcasted_iota(jnp.int32, (rows, 128) if axis == 0 else (128, rows), 1 - axis)
    picked = [jnp.where(route == experts, 1.0, 0.0) for route in routes]
    both = (picked[0] + picked[1]).astype(jnp.bfloat16)
    first = lax.broadcasted_iota(jnp.int32, (rows, rows), 0)
    second = lax.broadcasted_iota(jnp.int32, (rows, rows), 1)
    if axis == 0:
        earlier = dot32(ones_at(second < first), both)
    else:
        earlier = dot32(both, ones_at(first < second))
    places = []
    for route, pick in zip(routes, picked):
        slot = jnp.sum(pick * earlier, axis=1 - axis, keepdims=True).astype(jnp.int32)
        whole = slot < MAIN_ROWS
        main = jnp.where(whole, route * MAIN_ROWS + slot, -1)
        rest = jnp.where(whole, -64, route * REST_ROWS + slot - MAIN_ROWS)
        block = jnp.where(slot < REST_ROWS, 0, jnp.where(whole, 1, 2))
        places.append((main, rest, route * REST_ROWS + slot - REST_ROWS * block, block))
    return places


def middle_kernel(
    head_out, tokens, cotangent, routes, routes_t, scale,
    from_main, to_main, from_rest, to_rest, from_gate, to_gate, lane_mask,
    packed_w, gate_src, up_src, down_src,
    attended, mixed, grad_hidden, grad_branch, router_grad, gain_grad, head_grads,
    gate_grad, up_grad, down_grad,
    gate_w, up_w, down_w, out_w, router_w,
    rows_in, head_send, hidden_one, normed, grad_normed,
    send_main, send_rest, send_gate, place_main, place_rest, place_gate,
    x_main, x_rest, c_main, c_rest, x_main_in, x_rest_in, c_main_in, c_rest_in,
    d_main_in, d_rest_in, y_main_in, y_rest_in,
    rows_x, rows_c, gate_pre, up_pre, hidden, grad_gate_pre, grad_up_pre, rows_y, turned,
    weight_sem, out_sem, swap_send, swap_recv, send, recv,
):
    low, wide = jnp.bfloat16, jnp.float32
    dp, ctx = lax.axis_index("dp"), lax.axis_index("ctx")
    rows, width = tokens.shape
    half = rows // 2
    out_at = QUERY_HEAD_COUNT * HEAD_SIZE + 2 * KEY_VALUE_HEADS * HEAD_SIZE
    loads = [
        pltpu.make_async_copy(part, whole, weight_sem.at[n])
        for n, (part, whole) in enumerate(
            (
                (packed_w.at[:, pl.ds(out_at, width)], out_w),
                (packed_w.at[:, pl.ds(out_at + width, 128)], router_w),
                (gate_src, gate_w),
                (up_src, up_w),
                (down_src, down_w),
            )
        )
    ]
    for load in loads:
        load.start()
    y, z_lo, core = dp // 2, dp % 2, ctx % 2
    expert = ctx // 2 * 2 + z_lo
    at_home = z_lo == core

    def holder(step):
        other = (ctx + step) % SOURCES
        return other, (2 * y + other % 2, other // 2 * 2 + z_lo)

    def sender(step):
        other = (expert + step) % SOURCES
        return other, (2 * y + core, other)

    def neighbour(step):
        other = (ctx + step) % SOURCES
        return other, (dp, other)

    barrier = pltpu.get_barrier_semaphore()
    for step in range(1, SOURCES):
        for pick in (neighbour, holder, sender):
            pl.semaphore_signal(barrier, inc=1, device_id=pick(step)[1], device_id_type=MESH)

    @pl.when(jnp.logical_not(at_home))
    def _():
        for pick in (holder, sender):
            pl.semaphore_signal(barrier, inc=1, device_id=pick(0)[1], device_id_type=MESH)

    def start(number, pick, slot, main, rest, main_in, rest_in):
        copies = []
        pairs = ((main, main_in), (rest, rest_in))

        def remote(step, which):
            other, device = pick(step)
            src, dst = pairs[which]
            at = (number * 2 + which) * SOURCES + step
            return pltpu.make_async_remote_copy(
                src_ref=src.at[other],
                dst_ref=dst.at[slot],
                send_sem=send.at[at],
                recv_sem=recv.at[at],
                device_id=device,
                device_id_type=MESH,
            )

        def local(which):
            src, dst = pairs[which]
            at = (number * 2 + which) * SOURCES
            return pltpu.make_async_copy(src.at[slot], dst.at[slot], recv.at[at])

        for step in range(1, SOURCES):
            for which in range(2):
                copy = remote(step, which)
                copy.start()
                copies.append(copy)

        @pl.when(at_home)
        def _():
            for which in range(2):
                local(which).start()

        @pl.when(jnp.logical_not(at_home))
        def _():
            for which in range(2):
                remote(0, which).start()

        def wait_recv():
            @pl.when(at_home)
            def _():
                for which in range(2):
                    local(which).wait()

            @pl.when(jnp.logical_not(at_home))
            def _():
                for which in range(2):
                    remote(0, which).wait_recv()

            for copy in copies:
                copy.wait_recv()

        def wait_send():
            @pl.when(jnp.logical_not(at_home))
            def _():
                for which in range(2):
                    remote(0, which).wait_send()

            for copy in copies:
                copy.wait_send()

        return wait_recv, wait_send

    def swap(number, source, place_in):
        copies = []
        for step in range(1, SOURCES):
            other, device = neighbour(step)
            at = number * SOURCES + step
            copy = pltpu.make_async_remote_copy(
                src_ref=source.at[other],
                dst_ref=place_in.at[ctx],
                send_sem=swap_send.at[at],
                recv_sem=swap_recv.at[at],
                device_id=device,
                device_id_type=MESH,
            )
            copy.start()
            copies.append(copy)
        place_in[ctx] = source[ctx]
        return copies

    def pack(source, main, rest):
        main[...] = dot32(send_main[...], source[...]).astype(low).reshape(main.shape)
        total = jnp.zeros((SOURCES * REST_ROWS, REST_WIDTH), wide)
        for quarter in range(4):
            total += dot32(
                send_rest[quarter], source[:, quarter * REST_WIDTH : (quarter + 1) * REST_WIDTH]
            )
        rest[:, :, :REST_WIDTH] = total.astype(low).reshape(SOURCES, REST_ROWS, REST_WIDTH)

    def unpack(main_in, rest_in, out, group):
        at = pl.ds(4 * group, 4)
        main = main_in[at].reshape(4 * MAIN_ROWS, -1)
        rest = rest_in[at].reshape(4 * REST_ROWS, -1)
        for quarter in range(4):
            lanes = slice(quarter * REST_WIDTH, (quarter + 1) * REST_WIDTH)
            out[pl.ds(group * 4 * CAPACITY, 4 * CAPACITY), lanes] = (
                dot32(from_main[...], main[:, lanes])
                + dot32(from_rest[quarter], rest[:, :REST_WIDTH])
            ).astype(low)

    def repack(source, main, rest, group):
        at = pl.ds(4 * group, 4)
        block = source[pl.ds(group * 4 * CAPACITY, 4 * CAPACITY), :]
        main[at] = dot32(to_main[...], block).astype(low).reshape(4, MAIN_ROWS, -1)
        total = jnp.zeros((4 * REST_ROWS, REST_WIDTH), wide)
        for quarter in range(4):
            total += dot32(
                to_rest[quarter], block[:, quarter * REST_WIDTH : (quarter + 1) * REST_WIDTH]
            )
        rest[at, :, :REST_WIDTH] = total.astype(low).reshape(4, REST_ROWS, REST_WIDTH)

    pl.semaphore_wait(barrier, 3 * (SOURCES - 1) + 2 * ((z_lo + core) % 2))
    heads_in = swap(0, head_out, rows_in)

    main_rows = lax.broadcasted_iota(jnp.int32, (SOURCES * MAIN_ROWS, rows), 0)
    rest_rows = lax.broadcasted_iota(jnp.int32, (SOURCES * REST_ROWS, rows), 0)
    places = place_rows([routes_t[c : c + 1, :] for c in range(TOP)], 1)
    send_main[...] = ones_at((main_rows == places[0][0]) | (main_rows == places[1][0]))
    for quarter in range(4):
        send_rest[quarter] = ones_at(
            (rest_rows == places[0][1] + 4 * quarter) | (rest_rows == places[1][1] + 4 * quarter)
        )
    for choice in range(TOP):
        send_gate[choice] = ones_at(rest_rows == places[choice][2])
    main_lanes = lax.broadcasted_iota(jnp.int32, (rows, SOURCES * MAIN_ROWS), 1)
    rest_lanes = lax.broadcasted_iota(jnp.int32, (rows, SOURCES * REST_ROWS), 1)
    lanes = lax.broadcasted_iota(jnp.int32, (rows, 128), 1)
    places = place_rows([routes[:, c : c + 1] for c in range(TOP)], 0)
    gate_lanes = []
    for choice, (main, rest, gate, block) in enumerate(places):
        place_main[choice] = ones_at(main_lanes == main)
        for quarter in range(4):
            place_rest[choice, quarter] = ones_at(rest_lanes == rest + 4 * quarter)
        place_gate[choice] = ones_at(rest_lanes == gate)
        gate_lanes.append(jnp.where((lanes >= 3 * block) & (lanes < 3 * block + 3), 1.0, 0.0))
    pack(cotangent, c_main, c_rest)
    cotangent_flights = start(1, holder, ctx, c_main, c_rest, c_main_in, c_rest_in)

    for load in loads:
        load.wait()
    for copy in heads_in:
        copy.wait_recv()
    for head in range(KEY_VALUE_HEADS):
        for part in range(2):
            attended[
                part * half : (part + 1) * half, head * HEADS_WIDE : (head + 1) * HEADS_WIDE
            ] = rows_in[2 * head + part]

    @functools.partial(tiles, width)
    def _(at):
        hidden_one[:, at] = tokens[:, at].astype(wide) + across(attended[...], out_w[at, :])

    inverse = lax.rsqrt(jnp.mean(hidden_one[...] * hidden_one[...], axis=1, keepdims=True) + EPSILON)
    normed[...] = (hidden_one[...] * inverse * scale[...]).astype(low)
    logits = dot32(normed[...], router_w[...])
    on_route = [lanes == routes[:, choice : choice + 1] for choice in range(TOP)]
    chosen = [jnp.sum(jnp.where(on, logits, 0.0), axis=1, keepdims=True) for on in on_route]
    highest = jnp.maximum(chosen[0], chosen[1])
    powers = [jnp.exp(value - highest) for value in chosen]
    gates = [power / (powers[0] + powers[1]) for power in powers]

    pack(normed, x_main, x_rest)
    total = jnp.zeros((SOURCES * REST_ROWS, 128), wide)
    for choice in range(TOP):
        carried = in_three(gates[choice], lanes) * gate_lanes[choice]
        total += dot32(send_gate[choice], carried.astype(low))
    x_rest[:, :, REST_WIDTH:] = total.astype(low).reshape(SOURCES, REST_ROWS, 128)
    flights = start(0, holder, ctx, x_main, x_rest, x_main_in, x_rest_in)

    flights[0]()
    for group in range(4):
        unpack(x_main_in, x_rest_in, rows_x, group)

    @functools.partial(tiles, gate_w.shape[1])
    def _(at):
        gate = dot32(rows_x[...], gate_w[:, at])
        up = dot32(rows_x[...], up_w[:, at])
        gate_pre[:, at] = gate
        up_pre[:, at] = up
        hidden[:, at] = (gate / (1.0 + jnp.exp(-gate)) * up).astype(low)

    @functools.partial(tiles, width)
    def _(at):
        rows_y[:, at] = dot32(hidden[...], down_w[:, at]).astype(low)

    cotangent_flights[0]()
    cotangent_flights[1]()
    for group in range(4):
        repack(rows_y, c_main, c_rest, group)
    flights_y = start(3, sender, expert, c_main, c_rest, y_main_in, y_rest_in)

    flights[1]()
    expert_lanes = lax.broadcasted_iota(jnp.int32, (4 * CAPACITY, 128), 1)
    for group in range(4):
        unpack(c_main_in, c_rest_in, rows_c, group)
        at = pl.ds(group * 4 * CAPACITY, 4 * CAPACITY)
        carried = x_rest_in[pl.ds(4 * group, 4), :, pl.ds(REST_WIDTH, 128)].reshape(4 * REST_ROWS, 128)
        gate = jnp.sum(dot32(from_gate[...], carried) * lane_mask[...], axis=1, keepdims=True)
        grad = rows_c[at, :].astype(wide)
        grad_gate = jnp.sum(grad * rows_y[at, :].astype(wide), axis=1, keepdims=True)
        rows_c[at, :] = (gate * grad).astype(low)
        held = (in_three(grad_gate, expert_lanes) * lane_mask[...]).astype(low)
        x_rest[pl.ds(4 * group, 4), :, pl.ds(REST_WIDTH, 128)] = (
            dot32(to_gate[...], held).astype(low).reshape(4, REST_ROWS, 128)
        )

    @functools.partial(tiles, down_w.shape[0])
    def _(at):
        grad_hidden_rows = across(rows_c[...], down_w[at, :])
        gate = gate_pre[:, at]
        sigmoid = 1.0 / (1.0 + jnp.exp(-gate))
        grad_gate_pre[:, at] = (
            grad_hidden_rows * up_pre[:, at] * sigmoid * (1.0 + gate * (1.0 - sigmoid))
        ).astype(low)
        grad_up_pre[:, at] = (grad_hidden_rows * gate * sigmoid).astype(low)

    @functools.partial(tiles, width)
    def _(at):
        rows_y[:, at] = (
            across(grad_gate_pre[...], gate_w[at, :]) + across(grad_up_pre[...], up_w[at, :])
        ).astype(low)

    for group in range(4):
        repack(rows_y, x_main, x_rest, group)
    flights_d = start(2, sender, expert, x_main, x_rest, d_main_in, d_rest_in)

    turned[...] = rows_x[...].T

    @functools.partial(tiles, gate_w.shape[1])
    def _(at):
        gate_w[:, at] = dot32(turned[...], grad_gate_pre[:, at]).astype(low)
        up_w[:, at] = dot32(turned[...], grad_up_pre[:, at]).astype(low)

    turned[pl.ds(0, hidden.shape[1]), :] = hidden[...].T

    @functools.partial(tiles, width)
    def _(at):
        down_w[:, at] = dot32(turned[pl.ds(0, hidden.shape[1]), :], rows_c[:, at]).astype(low)

    stores = [
        pltpu.make_async_copy(whole, grad, out_sem.at[n])
        for n, (whole, grad) in enumerate(
            ((gate_w, gate_grad), (up_w, up_grad), (down_w, down_grad))
        )
    ]
    for store in stores:
        store.start()

    flights_d[0]()
    main = d_main_in[...].reshape(SOURCES * MAIN_ROWS, -1)
    rest = d_rest_in[...].reshape(SOURCES * REST_ROWS, -1)
    grad_gates = [
        jnp.sum(
            dot32(place_gate[choice], rest[:, REST_WIDTH:]) * gate_lanes[choice],
            axis=1,
            keepdims=True,
        )
        for choice in range(TOP)
    ]
    mean = gates[0] * grad_gates[0] + gates[1] * grad_gates[1]
    grad_logits = jnp.zeros((rows, 128), wide)
    for choice in range(TOP):
        grad_logits += jnp.where(
            on_route[choice], gates[choice] * (grad_gates[choice] - mean), 0.0
        )
    grad_logits = grad_logits.astype(low)
    for quarter in range(4):
        at = slice(quarter * REST_WIDTH, (quarter + 1) * REST_WIDTH)
        grad_normed[:, at] = (
            dot32(place_main[0] + place_main[1], main[:, at])
            + dot32(place_rest[0, quarter] + place_rest[1, quarter], rest[:, :REST_WIDTH])
            + across(grad_logits, router_w[at, :])
        )
    unit = hidden_one[...] * inverse
    grads = grad_normed[...]
    gain_grad[...] = jnp.sum(grads * unit, axis=0, keepdims=True)
    grads = grads * scale[...]
    grads = inverse * (grads - unit * jnp.mean(grads * unit, axis=1, keepdims=True))
    grad_hidden[...] = grads + cotangent[...].astype(wide)
    grad_branch[...] = grad_hidden[...].astype(low)

    @functools.partial(tiles, width)
    def _(at):
        grad_normed[:, at] = dot32(grad_branch[...], out_w[:, at])

    for head in range(KEY_VALUE_HEADS):
        for part in range(2):
            head_send[2 * head + part] = grad_normed[
                part * half : (part + 1) * half, head * HEADS_WIDE : (head + 1) * HEADS_WIDE
            ].astype(low)
    grads_in = swap(1, head_send, head_grads)
    router_grad[...] = dot32(normed[...].T, grad_logits).astype(low)

    flights_y[0]()
    main = y_main_in[...].reshape(SOURCES * MAIN_ROWS, -1)
    rest = y_rest_in[...].reshape(SOURCES * REST_ROWS, -1)
    for quarter in range(4):
        at = slice(quarter * REST_WIDTH, (quarter + 1) * REST_WIDTH)
        total = hidden_one[:, at]
        for choice in range(TOP):
            total += gates[choice] * (
                dot32(place_main[choice], main[:, at])
                + dot32(place_rest[choice, quarter], rest[:, :REST_WIDTH])
            )
        mixed[:, at] = total.astype(low)
    for copy in grads_in:
        copy.wait_recv()
    for copy in heads_in + grads_in:
        copy.wait_send()
    flights_d[1]()
    flights_y[1]()
    for copy in stores:
        copy.wait()


def run_middle(head_out, tokens, cotangent, routes, scale, packed, weights):
    rows, width = tokens.shape
    half = rows // 2
    hidden_width = weights[0].shape[-1]
    low, wide = jnp.bfloat16, jnp.float32
    count = SOURCES * CAPACITY
    vmem = pl.BlockSpec(memory_space=pltpu.VMEM)
    anywhere = pl.BlockSpec(memory_space=pltpu.HBM)
    main = pltpu.VMEM((SOURCES, MAIN_ROWS, width), low)
    long_rest = pltpu.VMEM((SOURCES, REST_ROWS, REST_WIDTH + 128), low)
    rest = pltpu.VMEM((SOURCES, REST_ROWS, REST_WIDTH), low)
    heads = pltpu.VMEM((SOURCES, half, HEADS_WIDE), low)
    dma = pltpu.SemaphoreType.DMA
    return pl.pallas_call(
        middle_kernel,
        out_shape=(
            jax.ShapeDtypeStruct((rows, width), low),
            jax.ShapeDtypeStruct((rows, width), low),
            jax.ShapeDtypeStruct((rows, width), wide),
            jax.ShapeDtypeStruct((rows, width), low),
            jax.ShapeDtypeStruct((width, 128), low),
            jax.ShapeDtypeStruct((1, width), wide),
            jax.ShapeDtypeStruct((SOURCES, half, HEADS_WIDE), low),
            jax.ShapeDtypeStruct((width, hidden_width), low),
            jax.ShapeDtypeStruct((width, hidden_width), low),
            jax.ShapeDtypeStruct((hidden_width, width), low),
        ),
        in_specs=[vmem] * 13 + [anywhere] * 4,
        out_specs=[vmem] * 7 + [anywhere] * 3,
        scratch_shapes=[
            pltpu.VMEM((width, hidden_width), low),
            pltpu.VMEM((width, hidden_width), low),
            pltpu.VMEM((hidden_width, width), low),
            pltpu.VMEM((width, width), low),
            pltpu.VMEM((width, 128), low),
            heads,
            heads,
            pltpu.VMEM((rows, width), wide),
            pltpu.VMEM((rows, width), low),
            pltpu.VMEM((rows, width), wide),

            pltpu.VMEM((SOURCES * MAIN_ROWS, rows), low),
            pltpu.VMEM((4, SOURCES * REST_ROWS, rows), low),
            pltpu.VMEM((TOP, SOURCES * REST_ROWS, rows), low),
            pltpu.VMEM((TOP, rows, SOURCES * MAIN_ROWS), low),
            pltpu.VMEM((TOP, 4, rows, SOURCES * REST_ROWS), low),
            pltpu.VMEM((TOP, rows, SOURCES * REST_ROWS), low),
            main, long_rest, main, rest, main, long_rest, main, rest,
            main, long_rest, main, rest,
            pltpu.VMEM((count, width), low),
            pltpu.VMEM((count, width), low),
            pltpu.VMEM((count, hidden_width), wide),
            pltpu.VMEM((count, hidden_width), wide),
            pltpu.VMEM((count, hidden_width), low),
            pltpu.VMEM((count, hidden_width), low),
            pltpu.VMEM((count, hidden_width), low),
            pltpu.VMEM((count, width), low),
            pltpu.VMEM((width, count), low),
            dma((5,)), dma((3,)), dma((2 * SOURCES,)), dma((2 * SOURCES,)),
            dma((8 * SOURCES,)), dma((8 * SOURCES,)),
        ],
        compiler_params=pltpu.CompilerParams(
            collective_id=3, has_side_effects=True, vmem_limit_bytes=62 * 2**20
        ),
        cost_estimate=pl.CostEstimate(
            flops=18 * count * width * hidden_width, bytes_accessed=40 * 2**20, transcendentals=0
        ),
        name="run_middle",
    )(
        head_out.reshape(SOURCES, half, HEADS_WIDE), tokens, cotangent, routes, routes.T, scale[None, :],
        *unpack_tables(), packed, *weights,
    )


KEY_STEP = 256
QUERY_STEP = 256


def allowed_block(block, pos, start):
    keys = lax.broadcasted_iota(jnp.int32, (KEY_STEP, QUERY_STEP), 0) + block * KEY_STEP
    return (keys <= pos) & (keys >= start)


def attend_kernel(low, high, pos_ref, start_ref, query_ref, kv_ref, kvt_ref, out_ref, outt_ref, log_ref):
    zeros = jnp.zeros((QUERY_STEP, HEAD_SIZE), jnp.bfloat16)

    @pl.loop(0, query_ref.shape[0] // QUERY_STEP)
    def _(tile):
        rows = pl.ds(pl.multiple_of(tile * QUERY_STEP, QUERY_STEP), QUERY_STEP)
        pos, start = pos_ref[:, rows], start_ref[:, rows]
        queries = query_ref[rows, :]
        padded = [
            jnp.concatenate([queries[:, h * HEAD_SIZE : (h + 1) * HEAD_SIZE], zeros], axis=1)
            for h in range(GROUP)
        ]

        def step(block, carry):
            keys = pl.ds(pl.multiple_of(block * KEY_STEP, KEY_STEP), KEY_STEP)
            kv = kv_ref[keys, :]
            values_t = kvt_ref[HEAD_SIZE:, keys]
            allowed = allowed_block(block, pos, start)
            new = []
            for h in range(GROUP):
                highest, total, summed = carry[h]
                scores = jnp.where(allowed, across(kv, padded[h]), NEGATIVE)
                new_high = jnp.maximum(highest, jnp.max(scores, axis=0, keepdims=True))
                weights = jnp.exp(scores - new_high)
                shrink = jnp.exp(highest - new_high)
                total = total * shrink + jnp.sum(weights, axis=0, keepdims=True)
                summed = summed * shrink + dot32(values_t, weights.astype(jnp.bfloat16))
                new.append((new_high, total, summed))
            return tuple(new)

        first = tuple(
            (
                jnp.full((1, QUERY_STEP), NEGATIVE, jnp.float32),
                jnp.zeros((1, QUERY_STEP), jnp.float32),
                jnp.zeros((HEAD_SIZE, QUERY_STEP), jnp.float32),
            )
            for _ in range(GROUP)
        )
        last = lax.fori_loop(low[tile], high[tile], step, first)
        pieces = []
        for h in range(GROUP):
            highest, total, summed = last[h]
            log_ref[h : h + 1, rows] = highest + jnp.log(total)
            summed = summed / total
            outt_ref[h, :, rows] = summed
            pieces.append(summed)
        out_ref[rows, :] = jnp.concatenate(pieces, axis=0).T.astype(jnp.bfloat16)


def attend_back_kernel(
    low, high, pos_ref, start_ref, query_ref, kv_ref, kvt_ref, outt_ref, log_ref, grad_ref,
    grad_query_ref, grad_kv_ref, sums,
):
    zeros = jnp.zeros((QUERY_STEP, HEAD_SIZE), jnp.bfloat16)
    sums[...] = jnp.zeros_like(sums)

    @pl.loop(0, query_ref.shape[0] // QUERY_STEP)
    def _(tile):
        rows = pl.ds(pl.multiple_of(tile * QUERY_STEP, QUERY_STEP), QUERY_STEP)
        pos, start = pos_ref[:, rows], start_ref[:, rows]
        queries, grads = query_ref[rows, :], grad_ref[rows, :]
        grads_t = grads.astype(jnp.float32).T
        query_pads, grad_pads, deltas, logs = [], [], [], []
        for h in range(GROUP):
            part = slice(h * HEAD_SIZE, (h + 1) * HEAD_SIZE)
            query_pads.append(jnp.concatenate([queries[:, part], zeros], axis=1))
            grad_pads.append(jnp.concatenate([zeros, grads[:, part]], axis=1))
            deltas.append(jnp.sum(grads_t[part, :] * outt_ref[h, :, rows], axis=0, keepdims=True))
            logs.append(log_ref[h : h + 1, rows])

        def step(block, carry):
            keys = pl.ds(pl.multiple_of(block * KEY_STEP, KEY_STEP), KEY_STEP)
            kv = kv_ref[keys, :]
            keys_t = kvt_ref[:HEAD_SIZE, keys]
            allowed = allowed_block(block, pos, start)
            new = []
            total = sums[keys, :]
            for h in range(GROUP):
                scores = jnp.where(allowed, across(kv, query_pads[h]), NEGATIVE)
                probs = jnp.exp(scores - logs[h])
                grad_probs = across(kv, grad_pads[h])
                grad_scores = (probs * (grad_probs - deltas[h])).astype(jnp.bfloat16)
                total += dot32(probs.astype(jnp.bfloat16), grad_pads[h])
                total += dot32(grad_scores, query_pads[h])
                new.append(carry[h] + dot32(keys_t, grad_scores))
            sums[keys, :] = total
            return tuple(new)

        first = tuple(jnp.zeros((HEAD_SIZE, QUERY_STEP), jnp.float32) for _ in range(GROUP))
        last = lax.fori_loop(low[tile], high[tile], step, first)
        factor = HEAD_SIZE ** (-0.5)
        grad_query_ref[rows, :] = (jnp.concatenate(last, axis=0) * factor).T.astype(jnp.bfloat16)

    grad_kv_ref[...] = sums[...].astype(jnp.bfloat16)


def attend_call(kernel, name, bounds, arrays, out_shape, scratch, matmuls, area):
    vmem = pl.BlockSpec(memory_space=pltpu.VMEM)
    return pl.pallas_call(
        kernel,
        out_shape=out_shape,
        grid_spec=pltpu.PrefetchScalarGridSpec(
            num_scalar_prefetch=2,
            grid=(1,),
            in_specs=[vmem] * len(arrays),
            out_specs=[vmem] * len(out_shape),
            scratch_shapes=scratch,
        ),
        compiler_params=pltpu.CompilerParams(vmem_limit_bytes=32 * 2**20),
        cost_estimate=pl.CostEstimate(
            flops=matmuls * 2 * HEAD_SIZE * area, bytes_accessed=8 * 2**20, transcendentals=area
        ),
        name=name,
    )(*bounds, *arrays)


def shards(
    tokens,
    segments,
    routes,
    gain_attn,
    w_query,
    key_weight,
    value_weight,
    w_out,
    w_router,
    gain_ffn,
    w_gate,
    w_up,
    w_down,
    cotangent,
):
    low = jnp.bfloat16
    wide = jnp.float32
    device_rows, width = tokens.shape
    sequence = segments.shape[0]
    half = device_rows // 2
    core = lax.axis_index("ctx") % 2
    ctx_count = lax.axis_size("ctx")
    slice_rows = w_query.shape[0]
    kv_shards = jnp.stack(
        [
            key_weight.reshape(slice_rows, KEY_VALUE_HEADS, HEAD_SIZE),
            value_weight.reshape(slice_rows, KEY_VALUE_HEADS, HEAD_SIZE),
        ],
        axis=2,
    ).reshape(slice_rows, 2 * KEY_VALUE_HEADS * HEAD_SIZE)
    shard = jnp.concatenate(
        [w_query, kv_shards, w_out, w_router, gain_attn[:, None], gain_ffn[:, None]], axis=1
    )
    shard = jnp.pad(shard, ((0, 0), (0, PACK - shard.shape[1])))
    packed, expert_weights, head_queries, head_kv, scales = gather_weights(
        shard, tokens, w_gate[0], w_up[0], w_down[0]
    )
    head_queries = head_queries.reshape(-1, HEADS_WIDE)
    head_kv = head_kv.reshape(sequence, 2 * HEAD_SIZE)
    order = jnp.arange(ctx_count * half, dtype=jnp.int32)
    query_pos = (order // half) * device_rows + core * half + order % half
    first_of = jnp.sum(
        (segments[:, None] < jnp.arange(5, dtype=jnp.int32)[None, :]).astype(jnp.int32), axis=0
    )
    starts = jnp.sum(
        jnp.where(segments[:, None] == jnp.arange(5, dtype=jnp.int32)[None, :], first_of[None, :], 0),
        axis=1,
    )
    query_start = lax.dynamic_slice_in_dim(
        starts.reshape(ctx_count, device_rows), core * half, half, axis=1
    ).reshape(-1)
    tiles = query_pos.reshape(-1, QUERY_STEP)
    bounds = (
        query_start.reshape(-1, QUERY_STEP)[:, 0] // KEY_STEP,
        tiles[:, -1] // KEY_STEP + 1,
    )
    mask_rows = (query_pos[None, :], query_start[None, :])

    head_kvt = head_kv.T
    count = head_queries.shape[0]
    area = GROUP * count * sequence // 3
    head_out, head_outt, log_total = attend_call(
        attend_kernel,
        "attend",
        bounds,
        (*mask_rows, head_queries, head_kv, head_kvt),
        (
            jax.ShapeDtypeStruct((count, HEADS_WIDE), low),
            jax.ShapeDtypeStruct((GROUP, HEAD_SIZE, count), wide),
            jax.ShapeDtypeStruct((GROUP, count), wide),
        ),
        [],
        2,
        area,
    )
    (
        attended, mixed, grad_hidden_one, grad_branch, grad_router_full, grad_gain_two, head_grads,
        *expert_grads,
    ) = run_middle(head_out, tokens, cotangent, routes, scales[1], packed, expert_weights)
    head_grads = head_grads.reshape(-1, HEADS_WIDE)

    head_grad_queries, head_grad_kv = attend_call(
        attend_back_kernel,
        "attend_back",
        bounds,
        (*mask_rows, head_queries, head_kv, head_kvt, head_outt, log_total, head_grads),
        (
            jax.ShapeDtypeStruct((count, HEADS_WIDE), low),
            jax.ShapeDtypeStruct((sequence, 2 * HEAD_SIZE), low),
        ),
        [pltpu.VMEM((sequence, 2 * HEAD_SIZE), wide)],
        5,
        area,
    )
    grad_input, out_share, share, (grad_gate, grad_up, grad_down) = scatter_sum(
        head_grad_queries, head_grad_kv, tokens, scales, grad_hidden_one, grad_branch, attended,
        grad_router_full, grad_gain_two, packed, expert_grads,
    )
    share, out_share = share.astype(wide), out_share.astype(wide)
    kv_share = share[:, 1536:2560].reshape(slice_rows, KEY_VALUE_HEADS, 2, HEAD_SIZE)
    return (
        mixed,
        grad_input,
        share[:, 2576],
        share[:, :1536],
        kv_share[:, :, 0].reshape(slice_rows, -1),
        kv_share[:, :, 1].reshape(slice_rows, -1),
        out_share,
        share[:, 2560:2576],
        share[:, 2577],
        grad_gate[None],
        grad_up[None],
        grad_down[None],
    )


def solution(mesh):
    in_specs = (
        P(("dp", "ctx"), None),
        P("dp"),
        P(("dp", "ctx"), None),
        P(("dp", "ctx")),
        P(("dp", "ctx"), None),
        P(("dp", "ctx"), None),
        P(("dp", "ctx"), None),
        P(("dp", "ctx"), None),
        P(("dp", "ctx"), None),
        P(("dp", "ctx")),
        P("ctx", "dp", None),
        P("ctx", "dp", None),
        P("ctx", "dp", None),
        P(("dp", "ctx"), None),
    )
    out_specs = (
        P(("dp", "ctx"), None),
        P(("dp", "ctx"), None),
        P(("dp", "ctx")),
        P(("dp", "ctx"), None),
        P(("dp", "ctx"), None),
        P(("dp", "ctx"), None),
        P(("dp", "ctx"), None),
        P(("dp", "ctx"), None),
        P(("dp", "ctx")),
        P("ctx", "dp", None),
        P("ctx", "dp", None),
        P("ctx", "dp", None),
    )
    return jax.shard_map(shards, mesh=mesh, in_specs=in_specs, out_specs=out_specs, check_vma=False)
```

```python
import functools

import jax
import jax.numpy as jnp
import numpy as np
from jax import lax
from jax.experimental import pallas as pl
from jax.experimental.pallas import tpu as pltpu
from jax.sharding import PartitionSpec as P

QUERY_HEAD_COUNT = 24
KEY_VALUE_HEADS = 8
HEAD_SIZE = 64
TOP = 2

EPSILON = 1e-06
NEGATIVE = -1e30
SOURCES = 16
GROUP = QUERY_HEAD_COUNT // KEY_VALUE_HEADS
HEADS_WIDE = GROUP * HEAD_SIZE
MESH = pl.DeviceIdType.MESH

PACK = 4608
HALF = PACK // 2
QUARTER = PACK // 4
RING_ORDERS = (("x", "y", "z"), ("y", "z", "x"), ("z", "x", "y"))


def place():
    dp = lax.axis_index("dp")
    ctx = lax.axis_index("ctx")
    return {"y": dp // 2, "z": (ctx // 8) * 2 + dp % 2, "x": (ctx // 2) % 4, "core": ctx % 2}


def device_of(spot):
    z = spot["z"]
    return (spot["y"] * 2 + z % 2, (z // 2) * 8 + spot["x"] * 2 + spot["core"])


def moved(spot, axis, step):
    other = dict(spot)
    if axis == "core":
        other["core"] = 1 - spot["core"]
    else:
        other[axis] = (spot[axis] + step) % 4
    return other


def member(spot, step):
    index = (spot["x"] % 2) * 2 + spot["core"]
    target = (index // 2 + step // 2) % 2 * 2 + (index % 2 + step % 2) % 2
    other = dict(spot)
    other["x"] = (spot["x"] // 2) * 2 + target // 2
    other["core"] = target % 2
    return other, target


def partner(spot):
    other = dict(spot)
    other["z"] = spot["z"] // 2 * 2 + (spot["z"] + 1) % 2
    other["core"] = (spot["core"] + 1) % 2
    return other


def others_of(ctx):
    return [(step, (ctx + step) % SOURCES) for step in range(1, SOURCES)]


def meet(spot, heads, picks=()):
    barrier = pltpu.get_barrier_semaphore()
    others = [member(spot, step)[0] for step in (1, 2, 3)] + [partner(spot)]
    others += [moved(spot, axis, step) for axis in "xyz" for step in (1, 2, 3)]
    others = [device_of(other) for other in others]
    others += [(lax.axis_index("dp"), other) for _, other in heads]
    for other in others:
        pl.semaphore_signal(barrier, inc=1, device_id=other, device_id_type=MESH)
    for pick in picks:
        for step in range(1, SOURCES):
            pl.semaphore_signal(barrier, inc=1, device_id=pick(step)[1], device_id_type=MESH)

    if picks:

        @pl.when(spot["z"] % 2 != spot["core"])
        def _():
            for pick in picks:
                pl.semaphore_signal(barrier, inc=1, device_id=pick(0)[1], device_id_type=MESH)

    away = (spot["z"] + spot["core"]) % 2
    amount = len(others) + len(picks) * (SOURCES - 1)
    pl.semaphore_wait(barrier, amount + len(picks) * away if picks else amount)


def region(spot, known, part, base):
    def pick(axis, value, size):
        return pl.ds(0, size) if axis in known else pl.ds(value, 1)

    z = spot["z"]
    if "x" in known:
        columns = pl.ds(base, HALF)
    else:
        columns = pl.ds(pl.multiple_of(base + (spot["x"] % 2) * QUARTER, 128), QUARTER)
    return (
        pick("y", spot["y"], 4),
        pick("z", z % 2, 2),
        pick("z", z // 2, 2),
        pick("x", spot["x"] // 2, 2),
        pl.ds(part * 16, 16),
        columns,
    )


def expert_rows(ref, spot, core, half=None):
    rows = ref.shape[0] // 8
    first = (spot["y"] * 2 + core) * rows
    if half is not None:
        rows //= 2
        first += half * rows
    return ref.at[pl.ds(pl.multiple_of(first, 32), rows)]


def half_region(where, axis, half):
    if axis == "y":
        return where[:1] + (pl.ds(half, 1),) + where[2:]
    return (pl.ds(2 * half, 2),) + where[1:]


def relay(ring, numbers, send, recv, whole, half):
    spot, axis = ring

    def copy(ref, step, number):
        return pltpu.make_async_remote_copy(
            src_ref=ref,
            dst_ref=ref,
            send_sem=send.at[numbers + number],
            recv_sem=recv.at[numbers + number],
            device_id=device_of(moved(spot, axis, step)),
            device_id_type=MESH,
        )

    first = [copy(whole(spot), 1, 0), copy(whole(spot), 3, 1)]
    second = [copy(half(moved(spot, axis, 3), 0), 1, 2), copy(half(moved(spot, axis, 1), 1), 3, 3)]
    return first, second


def gather_kernel(
    shard, merge, tokens, cotangent, routes_t, own_gate, own_up, own_down,
    out, gate_out, up_out, down_out, head_rows, head_kv, scales, c_main_in, c_rest_in,
    pieces, joined, qkv_w, rest_w, normed, qkv, packed,
    send0, recv0, send, recv, send_core, recv_core, local,
    swap_send, swap_recv, swap_local, line_send, line_recv, mate_send, mate_recv, ring_send, ring_recv,
    head_send, head_recv, head_local,
    send_main, send_rest, c_main, c_rest, route_send, route_recv,
):
    spot = place()
    dp, ctx = lax.axis_index("dp"), lax.axis_index("ctx")
    holder, sender, start = expert_routes(dp, ctx, route_send, route_recv)
    meet(spot, others_of(ctx), (holder, sender))
    mate = moved(spot, "core", 1)
    stays = spot["core"] == spot["z"] % 2
    experts = ((own_gate, gate_out), (own_up, up_out), (own_down, down_out))

    def swaps():
        return [
            pltpu.make_async_remote_copy(
                src_ref=own,
                dst_ref=expert_rows(whole, spot, spot["z"] % 2),
                send_sem=swap_send.at[n],
                recv_sem=swap_recv.at[n],
                device_id=device_of(partner(spot)),
                device_id_type=MESH,
            )
            for n, (own, whole) in enumerate(experts)
        ]

    def stays_here():
        return [
            pltpu.make_async_copy(own, expert_rows(whole, spot, spot["core"]), swap_local.at[n])
            for n, (own, whole) in enumerate(experts)
        ]

    def line(n):
        whole = experts[n][1]
        return relay(
            (spot, "y"),
            4 * n,
            line_send,
            line_recv,
            lambda at: expert_rows(whole, at, spot["core"]),
            lambda at, half: expert_rows(whole, at, spot["core"], half),
        )

    def to_mates(step):
        source = moved(spot, "y", 4 - step)
        return [
            pltpu.make_async_remote_copy(
                src_ref=expert_rows(whole, source, spot["core"]),
                dst_ref=expert_rows(whole, source, spot["core"]),
                send_sem=mate_send.at[3 * step + n],
                recv_sem=mate_recv.at[3 * step + n],
                device_id=device_of(mate),
                device_id_type=MESH,
            )
            for n, (own, whole) in enumerate(experts)
        ]

    def start_all(copies):
        for copy in copies:
            copy.start()

    @pl.when(stays)
    def _():
        start_all(stays_here())

    @pl.when(jnp.logical_not(stays))
    def _():
        start_all(swaps())

    index = (spot["x"] % 2) * 2 + spot["core"]
    quarter = spot["core"] * 2 + spot["x"] % 2
    copies = []
    for step in (1, 2, 3):
        other, target = member(spot, step)
        goal = other["core"] * 2 + other["x"] % 2
        copy = pltpu.make_async_remote_copy(
            src_ref=shard.at[:, pl.ds(pl.multiple_of(goal * QUARTER, 128), QUARTER)],
            dst_ref=pieces.at[index],
            send_sem=send0.at[step - 1],
            recv_sem=recv0.at[step - 1],
            device_id=device_of(other),
            device_id_type=MESH,
        )
        copy.start()
        copies.append(copy)
    pieces[index] = shard[:, pl.ds(pl.multiple_of(quarter * QUARTER, 128), QUARTER)]
    fill_tables(routes_t, send_main, send_rest)
    pack((send_main, send_rest), cotangent, c_main, c_rest)
    for copy in copies:
        copy.wait()
    joined[...] = jnp.dot(
        merge[...], pieces[...].reshape(64, QUARTER), preferred_element_type=jnp.float32
    ).astype(jnp.bfloat16)
    base = pl.multiple_of(spot["core"] * HALF, 128)
    mine = region(spot, "", 0, base)
    own = pltpu.make_async_copy(
        joined,
        out.at[spot["y"], spot["z"] % 2, spot["z"] // 2, spot["x"] // 2, :, mine[5]],
        local,
    )
    own.start()
    own.wait()
    core_copies = []

    def to_mate(number, where):
        copy = pltpu.make_async_remote_copy(
            src_ref=out.at[where],
            dst_ref=out.at[where],
            send_sem=send_core.at[number],
            recv_sem=recv_core.at[number],
            device_id=device_of(mate),
            device_id_type=MESH,
        )
        copy.start()
        core_copies.append(copy)

    flights, relays, finals = {}, [], []
    for stage in range(3):
        for part, order in enumerate(RING_ORDERS):
            axis, known = order[stage], order[:stage]
            if stage > 0:
                for copy in flights[part]:
                    copy.wait_recv()
            where = region(spot, known, part, base)
            if stage == 2:
                ring = relay(
                    (spot, axis),
                    4 * part,
                    ring_send,
                    ring_recv,
                    lambda at, known=known, part=part: out.at[region(at, known, part, base)],
                    lambda at, half, known=known, part=part, axis=axis: out.at[
                        half_region(region(at, known, part, base), axis, half)
                    ],
                )
                start_all(ring[0])
                relays.append(ring)
                finals.append((axis, known))
                to_mate(part * 4, where)
                continue
            started = []
            for step in (1, 3, 2):
                number = (stage * 3 + part) * 3 + step - 1
                copy = pltpu.make_async_remote_copy(
                    src_ref=out.at[where],
                    dst_ref=out.at[where],
                    send_sem=send.at[number],
                    recv_sem=recv.at[number],
                    device_id=device_of(moved(spot, axis, step)),
                    device_id_type=MESH,
                )
                copy.start()
                started.append(copy)
            flights[part] = started
            copies += started
        if stage == 1:

            @pl.when(stays)
            def _():
                for copy in stays_here():
                    copy.wait()

            @pl.when(jnp.logical_not(stays))
            def _():
                for copy in swaps():
                    copy.wait()


    mates = {step: to_mates(step) for step in (1, 3, 2)}

    def pass_on(ring):
        first, second = ring
        for number in range(2):
            first[number].wait_recv()
            second[number].start()

    residual = tokens[...].astype(jnp.float32)
    inverse = lax.rsqrt(jnp.mean(residual * residual, axis=1, keepdims=True) + EPSILON)
    for ring in relays:
        pass_on(ring)
    lines = [line(n) for n in range(3)]
    for first, _ in lines:
        start_all(first)
    own_mates = to_mates(0)
    flights = start(0, holder, ctx, c_main, c_rest, c_main_in, c_rest_in)
    for part, (axis, _) in enumerate(finals):
        for step in (1, 3):
            to_mate(part * 4 + step, region(moved(spot, axis, 4 - step), RING_ORDERS[part][:2], part, base))
    for part, (_, second) in enumerate(relays):
        for copy in second:
            copy.wait_recv()
        axis = RING_ORDERS[part][2]
        to_mate(part * 4 + 2, region(moved(spot, axis, 2), RING_ORDERS[part][:2], part, base))
    for copy in core_copies:
        copy.wait_recv()
    kv_at = QUERY_HEAD_COUNT * HEAD_SIZE
    qkv_width = qkv.shape[1]
    loads = [
        pltpu.make_async_copy(
            out.at[:, :, :, :, :, pl.ds(PACK - 512, 128)], rest_w, head_local.at[2]
        ),
        pltpu.make_async_copy(out.at[:, :, :, :, :, pl.ds(0, qkv_width)], qkv_w, head_local.at[3]),
    ]
    for load in loads:
        load.start()
    loads[0].wait()
    gains = rest_w[...].reshape(1536, 128).astype(jnp.float32).T
    scales[...] = gains[16:24, :]
    normed[...] = (residual * inverse * gains[16:17, :]).astype(jnp.bfloat16)
    loads[1].wait()
    factor = HEAD_SIZE ** (-0.5)

    @pl.loop(0, qkv_width // 256)
    def _(n):
        at = pl.ds(pl.multiple_of(n * 256, 256), 256)
        rows = jnp.dot(
            normed[...], qkv_w[:, :, :, :, :, at].reshape(1536, 256), preferred_element_type=jnp.float32
        )
        qkv[:, at] = (rows * jnp.where(n < kv_at // 256, factor, 1.0)).astype(jnp.bfloat16)

    half = tokens.shape[0] // 2
    for head in range(KEY_VALUE_HEADS):
        for core in range(2):
            packed[2 * head + core] = qkv[
                core * half : (core + 1) * half, head * HEADS_WIDE : (head + 1) * HEADS_WIDE
            ]

    def kv_of(other):
        start = kv_at + (other // 2) * 2 * HEAD_SIZE
        return qkv.at[:, pl.ds(pl.multiple_of(start, 128), 2 * HEAD_SIZE)]

    own_heads = [
        pltpu.make_async_copy(packed.at[ctx], head_rows.at[ctx], head_local.at[0]),
        pltpu.make_async_copy(kv_of(ctx), head_kv.at[ctx], head_local.at[1]),
    ]
    for copy in own_heads:
        copy.start()
    head_copies = []
    for step, other in others_of(ctx):
        for source, place_in, first in (
            (kv_of(other), head_kv.at[ctx], SOURCES),
            (packed.at[other], head_rows.at[ctx], 0),
        ):
            copy = pltpu.make_async_remote_copy(
                src_ref=source,
                dst_ref=place_in,
                send_sem=head_send.at[first + step],
                recv_sem=head_recv.at[first + step],
                device_id=(dp, other),
                device_id_type=MESH,
            )
            copy.start()
            head_copies.append(copy)
    start_all(own_mates)
    for n, ring in enumerate(lines):
        pass_on(ring)
        mates[1][n].start()
        mates[3][n].start()
    for n, (_, second) in enumerate(lines):
        for copy in second:
            copy.wait_recv()
        mates[2][n].start()
    line_copies = [copy for first, second in lines + relays for copy in first + second]
    for copy in own_heads + head_copies:
        copy.wait()
    flights[0]()
    flights[1]()
    for copy in copies[3:] + line_copies:
        copy.wait_send()
    for copy in core_copies:
        copy.wait_send()
    for copy in own_mates + mates[1] + mates[2] + mates[3]:
        copy.wait()


def gather_weights(shard, tokens, cotangent, routes, gate, up, down):
    shard = jnp.pad(shard, ((0, 4), (0, 0)))
    target, source = np.arange(48)[:, None], np.arange(64)[None, :]
    merge = jnp.asarray(
        (target // 12 == source // 16) & (target % 12 == source % 16), jnp.bfloat16
    )
    vmem = pl.BlockSpec(memory_space=pltpu.VMEM)
    anywhere = pl.BlockSpec(memory_space=pltpu.HBM)
    low = jnp.bfloat16
    rows, width = tokens.shape
    qkv_width = QUERY_HEAD_COUNT * HEAD_SIZE + 2 * KEY_VALUE_HEADS * HEAD_SIZE
    experts = [
        jax.ShapeDtypeStruct((8 * part.shape[0], part.shape[1]), low) for part in (gate, up, down)
    ]
    dma = pltpu.SemaphoreType.DMA
    packed, *rest = pl.pallas_call(
        gather_kernel,
        out_shape=[jax.ShapeDtypeStruct((4, 2, 2, 2, 48, PACK), low)]
        + experts
        + [
            jax.ShapeDtypeStruct((SOURCES, rows // 2, HEADS_WIDE), low),
            jax.ShapeDtypeStruct((SOURCES, rows, 2 * HEAD_SIZE), low),
            jax.ShapeDtypeStruct((8, width), jnp.float32),
            jax.ShapeDtypeStruct((SOURCES, MAIN_ROWS, width), low),
            jax.ShapeDtypeStruct((SOURCES, REST_ROWS, REST_WIDTH), low),
        ],
        in_specs=[vmem] * 5 + [anywhere] * 3,
        out_specs=[anywhere] * 4 + [vmem] * 5,
        scratch_shapes=[
            pltpu.VMEM((4, 16, QUARTER), low),
            pltpu.VMEM((48, QUARTER), low),
            pltpu.VMEM((4, 2, 2, 2, 48, qkv_width), low),
            pltpu.VMEM((4, 2, 2, 2, 48, 128), low),
            pltpu.VMEM((rows, width), low),
            pltpu.VMEM((rows, qkv_width), low),
            pltpu.VMEM((SOURCES, rows // 2, HEADS_WIDE), low),
            dma((3,)), dma((3,)), dma((18,)), dma((18,)), dma((12,)), dma((12,)), dma,
            dma((3,)), dma((3,)), dma((3,)), dma((12,)), dma((12,)), dma((12,)), dma((12,)),
            dma((12,)), dma((12,)),
            dma((2 * SOURCES,)), dma((2 * SOURCES,)), dma((4,)),
            pltpu.VMEM((SOURCES * MAIN_ROWS, rows), low),
            pltpu.VMEM((4, SOURCES * REST_ROWS, rows), low),
            pltpu.VMEM((SOURCES, MAIN_ROWS, width), low),
            pltpu.VMEM((SOURCES, REST_ROWS, REST_WIDTH), low),
            dma((2 * SOURCES,)), dma((2 * SOURCES,)),
        ],
        compiler_params=pltpu.CompilerParams(
            collective_id=1, has_side_effects=True, vmem_limit_bytes=62 * 2**20
        ),
        cost_estimate=pl.CostEstimate(
            flops=2 * rows * width * qkv_width, bytes_accessed=40 * 2**20, transcendentals=0
        ),
        name="gather_weights",
    )(shard, merge, tokens, cotangent, routes.T, gate, up, down)
    return packed.reshape(1536, PACK), rest[:3], *rest[3:]


EARLY = 1536
EARLY_ORDERS = (("y", "z", "x"), ("y", "x", "z"), ("y", "z", "x"))
LATE_ORDERS = (("y", "z", "x"), ("y", "x", "z"), ("y", "x", "z"))


def cut(spot, known, part, half):
    z = spot["z"]

    def pick(axis, value, size):
        return pl.ds(0, size) if axis in known else pl.ds(value, 1)

    columns = pl.ds(0, half)
    if "x" not in known:
        columns = pl.ds(pl.multiple_of((spot["x"] % 2) * (half // 2), 128), half // 2)
    return (
        pick("y", spot["y"], 4),
        pick("z", z % 2, 2),
        pick("z", z // 2, 2),
        pick("x", spot["x"] // 2, 2),
        pl.ds(part * 16, 16),
        columns,
    )


def landing_shape(known, half):
    return (
        4 if "y" in known else 1,
        2 if "z" in known else 1,
        2 if "z" in known else 1,
        2 if "x" in known else 1,
        16,
        half if "x" in known else half // 2,
    )


class Scatter:
    def __init__(self, orders, spot, split, grads, total, done, packed, out, sems, landing):
        self.spot, self.split, self.grads, self.total, self.out = spot, split, grads, total, out
        self.done, self.packed = done, packed
        self.orders = orders
        self.send_core, self.recv_core, self.send, self.recv, self.send_last, self.recv_last = sems
        self.landing = (landing[:3], landing[3:6], landing[6:9])
        self.half = total.shape[-1]
        self.base = pl.multiple_of(spot["core"] * self.half, 128)
        self.pending, self.copies = [], []

    def start(self):
        mate = moved(self.spot, "core", 1)
        mate_base = pl.multiple_of(mate["core"] * self.half, 128)
        for part in range(3):
            rows = pl.ds(part * 16, 16)
            copy = pltpu.make_async_remote_copy(
                src_ref=self.grads.at[:, :, :, :, rows, pl.ds(mate_base, self.half)],
                dst_ref=self.total.at[:, :, :, :, rows, :],
                send_sem=self.send_core.at[part],
                recv_sem=self.recv_core.at[part],
                device_id=device_of(mate),
                device_id_type=MESH,
            )
            copy.start()
            self.copies.append(copy)

    def first(self):
        cores = list(self.copies)
        for part in range(3):
            rows = pl.ds(part * 16, 16)
            cores[part].wait_recv()

            @pl.loop(0, 32)
            def _(block):
                at = (block // 8, (block // 4) % 2, (block // 2) % 2, block % 2, rows)
                self.total[at] = (
                    self.grads[at + (pl.ds(self.base, self.half),)].astype(jnp.float32)
                    + self.total[at].astype(jnp.float32)
                ).astype(jnp.bfloat16)

            self.pending.append(self.ring(part, 0))

    def ring(self, part, stage):
        axis, known = self.orders[part][2 - stage], self.orders[part][: 2 - stage]
        started = []
        for step in (1, 3, 2):
            other = moved(self.spot, axis, step)
            number = (stage * 3 + part) * 3 + step - 1
            copy = pltpu.make_async_remote_copy(
                src_ref=self.total.at[cut(other, known, part, self.half)],
                dst_ref=self.landing[stage][part].at[step - 1],
                send_sem=self.send.at[number],
                recv_sem=self.recv.at[number],
                device_id=device_of(other),
                device_id_type=MESH,
            )
            copy.start()
            started.append(copy)
        self.copies += started
        return started

    def next(self, stage):
        for part in range(3):
            known = self.orders[part][: 2 - stage]
            for copy in self.pending[part]:
                copy.wait_recv()
            self.add(known, part, self.landing[stage][part])
            if stage < 2:
                self.pending[part] = self.ring(part, stage + 1)

    def add(self, known, part, landing):
        spot = self.spot
        shape = landing_shape(known, self.half)
        columns = cut(spot, known, part, self.half)[5]

        def body(block):
            a, b, c, d = (
                block // (shape[1] * shape[2] * shape[3]),
                (block // (shape[2] * shape[3])) % shape[1],
                (block // shape[3]) % shape[2],
                block % shape[3],
            )
            at = (
                a + (0 if "y" in known else spot["y"]),
                b + (0 if "z" in known else spot["z"] % 2),
                c + (0 if "z" in known else spot["z"] // 2),
                d + (0 if "x" in known else spot["x"] // 2),
                pl.ds(part * 16, 16),
                columns,
            )
            summed = self.total[at].astype(jnp.float32)
            for step in range(3):
                summed += landing[step, a, b, c, d].astype(jnp.float32)
            self.total[at] = summed.astype(jnp.bfloat16)

        count = shape[0] * shape[1] * shape[2] * shape[3]
        if count == 1:
            body(0)
        else:
            pl.loop(0, count)(body)

    def finish(self):
        spot = self.spot
        quarter = self.half // 2
        index = (spot["x"] % 2) * 2 + spot["core"]
        place_in = spot["core"] * 2 + spot["x"] % 2
        mine = cut(spot, "", 0, self.half)
        self.done[...] = self.total[
            spot["y"], spot["z"] % 2, spot["z"] // 2, spot["x"] // 2, :, mine[5]
        ]
        self.packed[...] = (
            jnp.dot(self.split[...], self.done[...], preferred_element_type=jnp.float32)
            .astype(jnp.bfloat16)
            .reshape(4, 16, quarter)
        )
        columns = pl.ds(pl.multiple_of(place_in * quarter, 128), quarter)
        self.last = []
        for step in (1, 2, 3):
            other, target = member(spot, step)
            copy = pltpu.make_async_remote_copy(
                src_ref=self.packed.at[target],
                dst_ref=self.out.at[:, columns],
                send_sem=self.send_last.at[step - 1],
                recv_sem=self.recv_last.at[step - 1],
                device_id=device_of(other),
                device_id_type=MESH,
            )
            copy.start()
            self.last.append(copy)
        self.out[:, columns] = self.packed[index]

    def end(self):
        for copy in self.last:
            copy.wait()
        for copy in self.copies:
            copy.wait_send()


def scatter_kernel(
    head_rows, head_kv, tokens, scales, grad_hidden, branch, attended, router_grad, gain_grad, split,
    packed_w, grad_gate, grad_up, grad_down,
    grad_input, out, late_out, gate_out, up_out, down_out,
    rows_in, kv_in, grad_qkv, grad_normed, normed,
    mate_send, mate_recv, own_sem, line_send, line_recv, swap_send, swap_recv,
    head_send, head_recv, weight_sem,
    *buffers,
):
    spot = place()
    dp, ctx = lax.axis_index("dp"), lax.axis_index("ctx")
    held, mates, lines, results, arrived = (buffers[3 * n : 3 * n + 3] for n in range(5))
    early = Scatter(EARLY_ORDERS, spot, split, *buffers[15:19], out, buffers[19:25], buffers[25:34])
    late = Scatter(LATE_ORDERS, spot, split, *buffers[34:38], late_out, buffers[38:44], buffers[44:])
    wholes, finals = (grad_gate, grad_up, grad_down), (gate_out, up_out, down_out)
    mate = moved(spot, "core", 1)
    qkv_width = grad_qkv.shape[1]
    load = pltpu.make_async_copy(
        packed_w.at[:, :, :, :, :, pl.ds(0, qkv_width)],
        late.grads.at[:, :, :, :, :, pl.ds(0, qkv_width)],
        weight_sem,
    )
    load.start()
    own_copies, mate_copies = [], []
    for n, whole in enumerate(wholes):
        for y in range(4):
            rows = whole.shape[0] // 8

            def part(core, whole=whole, y=y, rows=rows):
                return whole.at[pl.ds(pl.multiple_of((2 * y + core) * rows, 64), rows)]

            own = pltpu.make_async_copy(part(spot["core"]), held[n].at[y], own_sem.at[4 * n + y])
            own.start()
            own_copies.append(own)
            mate_copies.append(
                pltpu.make_async_remote_copy(
                    src_ref=part(mate["core"]),
                    dst_ref=mates[n].at[y],
                    send_sem=mate_send.at[4 * n + y],
                    recv_sem=mate_recv.at[4 * n + y],
                    device_id=device_of(mate),
                    device_id_type=MESH,
                )
            )
    meet(spot, others_of(ctx))
    for copy in mate_copies:
        copy.start()
    head_copies = []
    for step, other in others_of(ctx):
        for source, place_in, first in ((head_kv, kv_in, SOURCES), (head_rows, rows_in, 0)):
            copy = pltpu.make_async_remote_copy(
                src_ref=source.at[other],
                dst_ref=place_in.at[ctx],
                send_sem=head_send.at[first + step],
                recv_sem=head_recv.at[first + step],
                device_id=(dp, other),
                device_id_type=MESH,
            )
            copy.start()
            head_copies.append(copy)
    rows_in[ctx] = head_rows[ctx]
    kv_in[ctx] = head_kv[ctx]

    tile = 256
    grads_shape = (4, 2, 2, 2, 48, tile)

    def fill(turned, right, grads):
        @pl.loop(0, right.shape[1] // tile)
        def _(n):
            at = pl.ds(pl.multiple_of(n * tile, tile), tile)
            grads[:, :, :, :, :, at] = (
                jnp.dot(turned, right[:, at], preferred_element_type=jnp.float32)
                .astype(jnp.bfloat16)
                .reshape(grads_shape)
            )

    fill(branch[...].T, attended, early.grads)
    early.start()

    line_copies = []
    for n in range(3):
        for copy in mate_copies[4 * n : 4 * n + 4]:
            copy.wait_recv()
        for copy in own_copies[4 * n : 4 * n + 4]:
            copy.wait()

        @pl.loop(0, 4)
        def _(y, n=n):
            held[n][y] = (
                held[n][y].astype(jnp.float32) + mates[n][y].astype(jnp.float32)
            ).astype(jnp.bfloat16)

        for step in (1, 3, 2):
            other = moved(spot, "y", step)
            copy = pltpu.make_async_remote_copy(
                src_ref=held[n].at[other["y"]],
                dst_ref=lines[n].at[step - 1],
                send_sem=line_send.at[3 * n + step - 1],
                recv_sem=line_recv.at[3 * n + step - 1],
                device_id=device_of(other),
                device_id_type=MESH,
            )
            copy.start()
            line_copies.append(copy)

    early.first()

    half = tokens.shape[0] // 2
    residual = tokens[...].astype(jnp.float32)
    inverse = lax.rsqrt(jnp.mean(residual * residual, axis=1, keepdims=True) + EPSILON)
    unit = residual * inverse
    scale = scales[0:1, :]
    normed[...] = (unit * scale).astype(jnp.bfloat16)
    for copy in head_copies:
        copy.wait_recv()
    for head in range(KEY_VALUE_HEADS):
        for core in range(2):
            grad_qkv[
                core * half : (core + 1) * half, head * HEADS_WIDE : (head + 1) * HEADS_WIDE
            ] = rows_in[2 * head + core]
        start = QUERY_HEAD_COUNT * HEAD_SIZE + head * 2 * HEAD_SIZE
        grad_qkv[:, start : start + 2 * HEAD_SIZE] = (
            kv_in[2 * head].astype(jnp.float32) + kv_in[2 * head + 1].astype(jnp.float32)
        ).astype(jnp.bfloat16)
    load.wait()
    grad_normed[...] = jnp.zeros_like(grad_normed)

    @pl.loop(0, qkv_width // tile)
    def _(n):
        at = pl.ds(pl.multiple_of(n * tile, tile), tile)
        grad_normed[...] += contract_cols(
            grad_qkv[:, at], late.grads[:, :, :, :, :, at].reshape(1536, tile)
        )

    fill(normed[...].T, grad_qkv, late.grads)
    gain_column = jnp.sum(grad_normed[...] * unit, axis=0, keepdims=True)
    lanes = lax.broadcasted_iota(jnp.int32, (1536, 128), 1)
    first_column = jnp.broadcast_to(gain_column, (128, 1536)).T
    second_column = jnp.broadcast_to(gain_grad[...], (128, 1536)).T
    rest = jnp.where(
        lanes < 16,
        router_grad[...].astype(jnp.float32),
        jnp.where(lanes == 16, first_column, jnp.where(lanes == 17, second_column, 0.0)),
    )
    at = qkv_width
    late.grads[:, :, :, :, :, at : at + 128] = rest.astype(jnp.bfloat16).reshape(4, 2, 2, 2, 48, 128)
    late.grads[:, :, :, :, :, at + 128 :] = jnp.zeros(
        (4, 2, 2, 2, 48, late.grads.shape[-1] - at - 128), jnp.bfloat16
    )
    late.start()
    grads_here = grad_normed[...] * scale
    grads_here = inverse * (
        grads_here - unit * jnp.mean(grads_here * unit, axis=1, keepdims=True)
    )
    grad_input[...] = (grads_here + grad_hidden[...]).astype(jnp.bfloat16)
    late.first()
    early.next(0)
    early.next(1)
    early.next(2)
    early.finish()
    late.next(0)
    sum_lines(spot, held, lines, line_copies, results)
    swap_results(spot, results, arrived, swap_send, swap_recv, True)
    late.next(1)
    late.next(2)
    late.finish()
    swap_results(spot, results, arrived, swap_send, swap_recv, False)
    stays = spot["core"] == spot["z"] % 2

    @pl.when(stays)
    def _():
        for result, final in zip(results, finals):
            final[...] = result[...]

    @pl.when(jnp.logical_not(stays))
    def _():
        for result, final in zip(arrived, finals):
            final[...] = result[...]

    early.end()
    late.end()
    for copy in mate_copies + head_copies + line_copies:
        copy.wait_send()


def sum_lines(spot, held, lines, line_copies, results):
    for copy in line_copies:
        copy.wait_recv()
    for mine, line, result in zip(held, lines, results):
        total = mine[spot["y"]].astype(jnp.float32)
        for step in range(3):
            total += line[step].astype(jnp.float32)
        result[...] = total.astype(jnp.bfloat16)


def swap_results(spot, results, arrived, send, recv, start):
    @pl.when(spot["core"] != spot["z"] % 2)
    def _():
        for n, (result, place_in) in enumerate(zip(results, arrived)):
            copy = pltpu.make_async_remote_copy(
                src_ref=result,
                dst_ref=place_in,
                send_sem=send.at[n],
                recv_sem=recv.at[n],
                device_id=device_of(partner(spot)),
                device_id_type=MESH,
            )
            if start:
                copy.start()
            else:
                copy.wait()


def scatter_sum(
    head_rows, head_kv, tokens, scales, grad_hidden, branch, attended, router_grad, gain_grad, packed,
    expert_grads,
):
    source, target = np.arange(48)[None, :], np.arange(64)[:, None]
    split = jnp.asarray(
        (source // 12 == target // 16) & (source % 12 == target % 16), jnp.bfloat16
    )
    low = jnp.bfloat16
    dma = pltpu.SemaphoreType.DMA
    blocks = [(part.shape[0] // 8, part.shape[1]) for part in expert_grads]
    buffers = [pltpu.VMEM((4,) + block, low) for block in blocks] * 2
    buffers += [pltpu.VMEM((3,) + block, low) for block in blocks]
    buffers += [pltpu.VMEM(block, low) for block in blocks] * 2
    for columns, orders in ((EARLY, EARLY_ORDERS), (PACK - EARLY, LATE_ORDERS)):
        buffers += [
            pltpu.VMEM((4, 2, 2, 2, 48, columns), low),
            pltpu.VMEM((4, 2, 2, 2, 48, columns // 2), low),
            pltpu.VMEM((48, columns // 4), low),
            pltpu.VMEM((4, 16, columns // 4), low),
            dma((3,)), dma((3,)), dma((27,)), dma((27,)), dma((3,)), dma((3,)),
        ]
        buffers += [
            pltpu.VMEM((3,) + landing_shape(order[: 2 - stage], columns // 2), low)
            for stage in range(3)
            for order in orders
        ]
    vmem = pl.BlockSpec(memory_space=pltpu.VMEM)
    anywhere = pl.BlockSpec(memory_space=pltpu.HBM)
    rows, width = tokens.shape
    head_rows = head_rows.reshape(SOURCES, rows // 2, HEADS_WIDE)
    head_kv = head_kv.reshape(SOURCES, rows, 2 * HEAD_SIZE)
    qkv_width = QUERY_HEAD_COUNT * HEAD_SIZE + 2 * KEY_VALUE_HEADS * HEAD_SIZE
    grad_input, out, late_out, *finals = pl.pallas_call(
        scatter_kernel,
        out_shape=[jax.ShapeDtypeStruct((rows, width), low)]
        + [jax.ShapeDtypeStruct((16, columns), low) for columns in (EARLY, PACK - EARLY)]
        + [jax.ShapeDtypeStruct(block, low) for block in blocks],
        in_specs=[vmem] * 10 + [anywhere] * 4,
        out_specs=[vmem] * 6,
        scratch_shapes=[
            pltpu.VMEM(head_rows.shape, low),
            pltpu.VMEM(head_kv.shape, low),
            pltpu.VMEM((rows, qkv_width), low),
            pltpu.VMEM((rows, width), jnp.float32),
            pltpu.VMEM((rows, width), low),
            dma((12,)), dma((12,)), dma((12,)), dma((9,)), dma((9,)), dma((3,)), dma((3,)),
            dma((2 * SOURCES,)), dma((2 * SOURCES,)), dma,
        ]
        + buffers,
        compiler_params=pltpu.CompilerParams(
            collective_id=2, has_side_effects=True, vmem_limit_bytes=62 * 2**20
        ),
        cost_estimate=pl.CostEstimate(
            flops=2 * rows * width * 6656, bytes_accessed=28 * 2**20, transcendentals=0
        ),
        name="scatter_sum",
    )(
        head_rows, head_kv, tokens, scales, grad_hidden, branch, attended, router_grad, gain_grad, split,
        packed.reshape(4, 2, 2, 2, 48, PACK), *expert_grads,
    )
    return grad_input, out[:12], late_out[:12], [final.astype(jnp.float32) for final in finals]


def contract_cols(left, right):
    return lax.dot_general(
        left, right, (((1,), (1,)), ((), ())), preferred_element_type=jnp.float32
    )


MAIN_ROWS = 32
REST_ROWS = 16
REST_WIDTH = 384
CAPACITY = 36
TILE = 256


def across(left, right):
    return lax.dot_general(
        left, right, (((1,), (1,)), ((), ())), preferred_element_type=jnp.float32
    )


def dot32(left, right):
    return jnp.dot(left, right, preferred_element_type=jnp.float32)


def tiles(extent, body):
    pl.loop(0, extent // TILE)(lambda n: body(pl.ds(pl.multiple_of(n * TILE, TILE), TILE)))


def ones_at(condition):
    return jnp.where(condition, 1.0, 0.0).astype(jnp.bfloat16)


def in_three(column, lanes):
    first = column.astype(jnp.bfloat16).astype(jnp.float32)
    second = (column - first).astype(jnp.bfloat16).astype(jnp.float32)
    third = column - first - second
    return jnp.where(lanes % 3 == 0, first, jnp.where(lanes % 3 == 1, second, third))


def unpack_tables():
    row = np.arange(4 * CAPACITY)[:, None]
    device, slot = row // CAPACITY, row % CAPACITY
    main = np.arange(4 * MAIN_ROWS)[None, :]
    from_main = (device == main // MAIN_ROWS) & (slot == main % MAIN_ROWS)
    rest = np.arange(4 * REST_ROWS)[None, :]
    from_rest = np.stack(
        [
            (device == rest // REST_ROWS)
            & ((rest // 4) % 4 == quarter)
            & (slot == MAIN_ROWS + rest % 4)
            for quarter in range(4)
        ]
    )
    from_gate = (device == rest // REST_ROWS) & (slot % REST_ROWS == rest % REST_ROWS)
    lane_mask = np.arange(128)[None, :] // 3 == slot // REST_ROWS
    return [
        jnp.asarray(table, jnp.bfloat16)
        for table in (from_main, from_main.T, from_rest, from_rest.transpose(0, 2, 1), from_gate, from_gate.T)
    ] + [jnp.asarray(lane_mask, jnp.float32)]


def place_rows(routes, axis):
    rows = routes[0].shape[axis]
    experts = lax.broadcasted_iota(jnp.int32, (rows, 128) if axis == 0 else (128, rows), 1 - axis)
    picked = [jnp.where(route == experts, 1.0, 0.0) for route in routes]
    both = (picked[0] + picked[1]).astype(jnp.bfloat16)
    first = lax.broadcasted_iota(jnp.int32, (rows, rows), 0)
    second = lax.broadcasted_iota(jnp.int32, (rows, rows), 1)
    if axis == 0:
        earlier = dot32(ones_at(second < first), both)
    else:
        earlier = dot32(both, ones_at(first < second))
    places = []
    for route, pick in zip(routes, picked):
        slot = jnp.sum(pick * earlier, axis=1 - axis, keepdims=True).astype(jnp.int32)
        whole = slot < MAIN_ROWS
        main = jnp.where(whole, route * MAIN_ROWS + slot, -1)
        rest = jnp.where(whole, -64, route * REST_ROWS + slot - MAIN_ROWS)
        block = jnp.where(slot < REST_ROWS, 0, jnp.where(whole, 1, 2))
        places.append((main, rest, route * REST_ROWS + slot - REST_ROWS * block, block))
    return places


def expert_routes(dp, ctx, send, recv):
    y, z_lo, core = dp // 2, dp % 2, ctx % 2
    expert = ctx // 2 * 2 + z_lo
    at_home = z_lo == core

    def holder(step):
        other = (ctx + step) % SOURCES
        return other, (2 * y + other % 2, other // 2 * 2 + z_lo)

    def sender(step):
        other = (expert + step) % SOURCES
        return other, (2 * y + core, other)

    def start(number, pick, slot, main, rest, main_in, rest_in):
        copies = []
        pairs = ((main, main_in), (rest, rest_in))

        def remote(step, which):
            other, device = pick(step)
            src, dst = pairs[which]
            at = (number * 2 + which) * SOURCES + step
            return pltpu.make_async_remote_copy(
                src_ref=src.at[other],
                dst_ref=dst.at[slot],
                send_sem=send.at[at],
                recv_sem=recv.at[at],
                device_id=device,
                device_id_type=MESH,
            )

        def local(which):
            src, dst = pairs[which]
            at = (number * 2 + which) * SOURCES
            return pltpu.make_async_copy(src.at[slot], dst.at[slot], recv.at[at])

        for step in range(1, SOURCES):
            for which in range(2):
                copy = remote(step, which)
                copy.start()
                copies.append(copy)

        @pl.when(at_home)
        def _():
            for which in range(2):
                local(which).start()

        @pl.when(jnp.logical_not(at_home))
        def _():
            for which in range(2):
                remote(0, which).start()

        def wait_recv():
            @pl.when(at_home)
            def _():
                for which in range(2):
                    local(which).wait()

            @pl.when(jnp.logical_not(at_home))
            def _():
                for which in range(2):
                    remote(0, which).wait_recv()

            for copy in copies:
                copy.wait_recv()

        def wait_send():
            @pl.when(jnp.logical_not(at_home))
            def _():
                for which in range(2):
                    remote(0, which).wait_send()

            for copy in copies:
                copy.wait_send()

        return wait_recv, wait_send

    return holder, sender, start


def pack(tables, source, main, rest):
    send_main, send_rest = tables
    main[...] = dot32(send_main[...], source[...]).astype(jnp.bfloat16).reshape(main.shape)
    total = jnp.zeros((SOURCES * REST_ROWS, REST_WIDTH), jnp.float32)
    for quarter in range(4):
        total += dot32(
            send_rest[quarter], source[:, quarter * REST_WIDTH : (quarter + 1) * REST_WIDTH]
        )
    rest[:, :, :REST_WIDTH] = (
        total.astype(jnp.bfloat16).reshape(SOURCES, REST_ROWS, REST_WIDTH)
    )


def fill_tables(routes_t, send_main, send_rest):
    rows = routes_t.shape[1]
    main_rows = lax.broadcasted_iota(jnp.int32, (SOURCES * MAIN_ROWS, rows), 0)
    rest_rows = lax.broadcasted_iota(jnp.int32, (SOURCES * REST_ROWS, rows), 0)
    places = place_rows([routes_t[c : c + 1, :] for c in range(TOP)], 1)
    send_main[...] = ones_at((main_rows == places[0][0]) | (main_rows == places[1][0]))
    for quarter in range(4):
        send_rest[quarter] = ones_at(
            (rest_rows == places[0][1] + 4 * quarter) | (rest_rows == places[1][1] + 4 * quarter)
        )
    return rest_rows, places


def middle_kernel(
    head_out, tokens, cotangent, c_main_in, c_rest_in, routes, routes_t, scale,
    from_main, to_main, from_rest, to_rest, from_gate, to_gate, lane_mask,
    packed_w, gate_src, up_src, down_src,
    attended, mixed, grad_hidden, grad_branch, router_grad, gain_grad, head_grads,
    gate_grad, up_grad, down_grad,
    gate_w, up_w, down_w, out_w, router_w,
    rows_in, head_send, hidden_one, normed, grad_normed,
    send_main, send_rest, send_gate, place_main, place_rest, place_gate,
    x_main, x_rest, c_main, c_rest, x_main_in, x_rest_in,
    d_main_in, d_rest_in, y_main_in, y_rest_in,
    rows_x, rows_c, gate_pre, up_pre, hidden, grad_gate_pre, grad_up_pre, rows_y, turned,
    weight_sem, out_sem, swap_send, swap_recv, send, recv,
):
    low, wide = jnp.bfloat16, jnp.float32
    dp, ctx = lax.axis_index("dp"), lax.axis_index("ctx")
    rows, width = tokens.shape
    half = rows // 2
    out_at = QUERY_HEAD_COUNT * HEAD_SIZE + 2 * KEY_VALUE_HEADS * HEAD_SIZE
    loads = [
        pltpu.make_async_copy(part, whole, weight_sem.at[n])
        for n, (part, whole) in enumerate(
            (
                (packed_w.at[:, pl.ds(out_at, width)], out_w),
                (packed_w.at[:, pl.ds(out_at + width, 128)], router_w),
                (gate_src, gate_w),
                (up_src, up_w),
                (down_src, down_w),
            )
        )
    ]
    for load in loads:
        load.start()
    z_lo, core = dp % 2, ctx % 2
    expert = ctx // 2 * 2 + z_lo
    holder, sender, start = expert_routes(dp, ctx, send, recv)

    def neighbour(step):
        other = (ctx + step) % SOURCES
        return other, (dp, other)

    barrier = pltpu.get_barrier_semaphore()
    for step in range(1, SOURCES):
        for pick in (neighbour, holder, sender):
            pl.semaphore_signal(barrier, inc=1, device_id=pick(step)[1], device_id_type=MESH)

    @pl.when(z_lo != core)
    def _():
        for pick in (holder, sender):
            pl.semaphore_signal(barrier, inc=1, device_id=pick(0)[1], device_id_type=MESH)

    def swap(number, source, place_in):
        copies = []
        for step in range(1, SOURCES):
            other, device = neighbour(step)
            at = number * SOURCES + step
            copy = pltpu.make_async_remote_copy(
                src_ref=source.at[other],
                dst_ref=place_in.at[ctx],
                send_sem=swap_send.at[at],
                recv_sem=swap_recv.at[at],
                device_id=device,
                device_id_type=MESH,
            )
            copy.start()
            copies.append(copy)
        place_in[ctx] = source[ctx]
        return copies

    def unpack(main_in, rest_in, out, group):
        at = pl.ds(4 * group, 4)
        main = main_in[at].reshape(4 * MAIN_ROWS, -1)
        rest = rest_in[at].reshape(4 * REST_ROWS, -1)
        for quarter in range(4):
            lanes = slice(quarter * REST_WIDTH, (quarter + 1) * REST_WIDTH)
            out[pl.ds(group * 4 * CAPACITY, 4 * CAPACITY), lanes] = (
                dot32(from_main[...], main[:, lanes])
                + dot32(from_rest[quarter], rest[:, :REST_WIDTH])
            ).astype(low)

    def repack(source, main, rest, group):
        at = pl.ds(4 * group, 4)
        block = source[pl.ds(group * 4 * CAPACITY, 4 * CAPACITY), :]
        main[at] = dot32(to_main[...], block).astype(low).reshape(4, MAIN_ROWS, -1)
        total = jnp.zeros((4 * REST_ROWS, REST_WIDTH), wide)
        for quarter in range(4):
            total += dot32(
                to_rest[quarter], block[:, quarter * REST_WIDTH : (quarter + 1) * REST_WIDTH]
            )
        rest[at, :, :REST_WIDTH] = total.astype(low).reshape(4, REST_ROWS, REST_WIDTH)

    pl.semaphore_wait(barrier, 3 * (SOURCES - 1) + 2 * ((z_lo + core) % 2))
    heads_in = swap(0, head_out, rows_in)

    rest_rows, places = fill_tables(routes_t, send_main, send_rest)
    for choice in range(TOP):
        send_gate[choice] = ones_at(rest_rows == places[choice][2])
    main_lanes = lax.broadcasted_iota(jnp.int32, (rows, SOURCES * MAIN_ROWS), 1)
    rest_lanes = lax.broadcasted_iota(jnp.int32, (rows, SOURCES * REST_ROWS), 1)
    lanes = lax.broadcasted_iota(jnp.int32, (rows, 128), 1)
    places = place_rows([routes[:, c : c + 1] for c in range(TOP)], 0)
    gate_lanes = []
    for choice, (main, rest, gate, block) in enumerate(places):
        place_main[choice] = ones_at(main_lanes == main)
        for quarter in range(4):
            place_rest[choice, quarter] = ones_at(rest_lanes == rest + 4 * quarter)
        place_gate[choice] = ones_at(rest_lanes == gate)
        gate_lanes.append(jnp.where((lanes >= 3 * block) & (lanes < 3 * block + 3), 1.0, 0.0))

    for load in loads:
        load.wait()
    for copy in heads_in:
        copy.wait_recv()
    for head in range(KEY_VALUE_HEADS):
        for part in range(2):
            attended[
                part * half : (part + 1) * half, head * HEADS_WIDE : (head + 1) * HEADS_WIDE
            ] = rows_in[2 * head + part]

    @functools.partial(tiles, width)
    def _(at):
        hidden_one[:, at] = tokens[:, at].astype(wide) + across(attended[...], out_w[at, :])

    inverse = lax.rsqrt(jnp.mean(hidden_one[...] * hidden_one[...], axis=1, keepdims=True) + EPSILON)
    normed[...] = (hidden_one[...] * inverse * scale[...]).astype(low)
    logits = dot32(normed[...], router_w[...])
    on_route = [lanes == routes[:, choice : choice + 1] for choice in range(TOP)]
    chosen = [jnp.sum(jnp.where(on, logits, 0.0), axis=1, keepdims=True) for on in on_route]
    highest = jnp.maximum(chosen[0], chosen[1])
    powers = [jnp.exp(value - highest) for value in chosen]
    gates = [power / (powers[0] + powers[1]) for power in powers]

    pack((send_main, send_rest), normed, x_main, x_rest)
    total = jnp.zeros((SOURCES * REST_ROWS, 128), wide)
    for choice in range(TOP):
        carried = in_three(gates[choice], lanes) * gate_lanes[choice]
        total += dot32(send_gate[choice], carried.astype(low))
    x_rest[:, :, REST_WIDTH:] = total.astype(low).reshape(SOURCES, REST_ROWS, 128)
    flights = start(0, holder, ctx, x_main, x_rest, x_main_in, x_rest_in)

    flights[0]()
    for group in range(4):
        unpack(x_main_in, x_rest_in, rows_x, group)

    @functools.partial(tiles, gate_w.shape[1])
    def _(at):
        gate = dot32(rows_x[...], gate_w[:, at])
        up = dot32(rows_x[...], up_w[:, at])
        gate_pre[:, at] = gate
        up_pre[:, at] = up
        hidden[:, at] = (gate / (1.0 + jnp.exp(-gate)) * up).astype(low)

    @functools.partial(tiles, width)
    def _(at):
        rows_y[:, at] = dot32(hidden[...], down_w[:, at]).astype(low)

    for group in range(4):
        repack(rows_y, c_main, c_rest, group)
    flights_y = start(3, sender, expert, c_main, c_rest, y_main_in, y_rest_in)

    flights[1]()
    expert_lanes = lax.broadcasted_iota(jnp.int32, (4 * CAPACITY, 128), 1)
    for group in range(4):
        unpack(c_main_in, c_rest_in, rows_c, group)
        at = pl.ds(group * 4 * CAPACITY, 4 * CAPACITY)
        carried = x_rest_in[pl.ds(4 * group, 4), :, pl.ds(REST_WIDTH, 128)].reshape(4 * REST_ROWS, 128)
        gate = jnp.sum(dot32(from_gate[...], carried) * lane_mask[...], axis=1, keepdims=True)
        grad = rows_c[at, :].astype(wide)
        grad_gate = jnp.sum(grad * rows_y[at, :].astype(wide), axis=1, keepdims=True)
        rows_c[at, :] = (gate * grad).astype(low)
        held = (in_three(grad_gate, expert_lanes) * lane_mask[...]).astype(low)
        x_rest[pl.ds(4 * group, 4), :, pl.ds(REST_WIDTH, 128)] = (
            dot32(to_gate[...], held).astype(low).reshape(4, REST_ROWS, 128)
        )

    @functools.partial(tiles, down_w.shape[0])
    def _(at):
        grad_hidden_rows = across(rows_c[...], down_w[at, :])
        gate = gate_pre[:, at]
        sigmoid = 1.0 / (1.0 + jnp.exp(-gate))
        grad_gate_pre[:, at] = (
            grad_hidden_rows * up_pre[:, at] * sigmoid * (1.0 + gate * (1.0 - sigmoid))
        ).astype(low)
        grad_up_pre[:, at] = (grad_hidden_rows * gate * sigmoid).astype(low)

    @functools.partial(tiles, width)
    def _(at):
        rows_y[:, at] = (
            across(grad_gate_pre[...], gate_w[at, :]) + across(grad_up_pre[...], up_w[at, :])
        ).astype(low)

    for group in range(4):
        repack(rows_y, x_main, x_rest, group)
    flights_d = start(2, sender, expert, x_main, x_rest, d_main_in, d_rest_in)

    turned[...] = rows_x[...].T

    @functools.partial(tiles, gate_w.shape[1])
    def _(at):
        gate_w[:, at] = dot32(turned[...], grad_gate_pre[:, at]).astype(low)
        up_w[:, at] = dot32(turned[...], grad_up_pre[:, at]).astype(low)

    turned[pl.ds(0, hidden.shape[1]), :] = hidden[...].T

    @functools.partial(tiles, width)
    def _(at):
        down_w[:, at] = dot32(turned[pl.ds(0, hidden.shape[1]), :], rows_c[:, at]).astype(low)

    stores = [
        pltpu.make_async_copy(whole, grad, out_sem.at[n])
        for n, (whole, grad) in enumerate(
            ((gate_w, gate_grad), (up_w, up_grad), (down_w, down_grad))
        )
    ]
    for store in stores:
        store.start()

    flights_d[0]()
    main = d_main_in[...].reshape(SOURCES * MAIN_ROWS, -1)
    rest = d_rest_in[...].reshape(SOURCES * REST_ROWS, -1)
    grad_gates = [
        jnp.sum(
            dot32(place_gate[choice], rest[:, REST_WIDTH:]) * gate_lanes[choice],
            axis=1,
            keepdims=True,
        )
        for choice in range(TOP)
    ]
    mean = gates[0] * grad_gates[0] + gates[1] * grad_gates[1]
    grad_logits = jnp.zeros((rows, 128), wide)
    for choice in range(TOP):
        grad_logits += jnp.where(
            on_route[choice], gates[choice] * (grad_gates[choice] - mean), 0.0
        )
    grad_logits = grad_logits.astype(low)
    for quarter in range(4):
        at = slice(quarter * REST_WIDTH, (quarter + 1) * REST_WIDTH)
        grad_normed[:, at] = (
            dot32(place_main[0] + place_main[1], main[:, at])
            + dot32(place_rest[0, quarter] + place_rest[1, quarter], rest[:, :REST_WIDTH])
            + across(grad_logits, router_w[at, :])
        )
    unit = hidden_one[...] * inverse
    grads = grad_normed[...]
    gain_grad[...] = jnp.sum(grads * unit, axis=0, keepdims=True)
    grads = grads * scale[...]
    grads = inverse * (grads - unit * jnp.mean(grads * unit, axis=1, keepdims=True))
    grad_hidden[...] = grads + cotangent[...].astype(wide)
    grad_branch[...] = grad_hidden[...].astype(low)

    @functools.partial(tiles, width)
    def _(at):
        grad_normed[:, at] = dot32(grad_branch[...], out_w[:, at])

    for head in range(KEY_VALUE_HEADS):
        for part in range(2):
            head_send[2 * head + part] = grad_normed[
                part * half : (part + 1) * half, head * HEADS_WIDE : (head + 1) * HEADS_WIDE
            ].astype(low)
    grads_in = swap(1, head_send, head_grads)
    router_grad[...] = dot32(normed[...].T, grad_logits).astype(low)

    flights_y[0]()
    main = y_main_in[...].reshape(SOURCES * MAIN_ROWS, -1)
    rest = y_rest_in[...].reshape(SOURCES * REST_ROWS, -1)
    for quarter in range(4):
        at = slice(quarter * REST_WIDTH, (quarter + 1) * REST_WIDTH)
        total = hidden_one[:, at]
        for choice in range(TOP):
            total += gates[choice] * (
                dot32(place_main[choice], main[:, at])
                + dot32(place_rest[choice, quarter], rest[:, :REST_WIDTH])
            )
        mixed[:, at] = total.astype(low)
    for copy in grads_in:
        copy.wait_recv()
    for copy in heads_in + grads_in:
        copy.wait_send()
    flights_d[1]()
    flights_y[1]()
    for copy in stores:
        copy.wait()


def run_middle(head_out, tokens, cotangent, cotangent_rows, routes, scale, packed, weights):
    rows, width = tokens.shape
    half = rows // 2
    hidden_width = weights[0].shape[-1]
    low, wide = jnp.bfloat16, jnp.float32
    count = SOURCES * CAPACITY
    vmem = pl.BlockSpec(memory_space=pltpu.VMEM)
    anywhere = pl.BlockSpec(memory_space=pltpu.HBM)
    main = pltpu.VMEM((SOURCES, MAIN_ROWS, width), low)
    long_rest = pltpu.VMEM((SOURCES, REST_ROWS, REST_WIDTH + 128), low)
    rest = pltpu.VMEM((SOURCES, REST_ROWS, REST_WIDTH), low)
    heads = pltpu.VMEM((SOURCES, half, HEADS_WIDE), low)
    dma = pltpu.SemaphoreType.DMA
    return pl.pallas_call(
        middle_kernel,
        out_shape=(
            jax.ShapeDtypeStruct((rows, width), low),
            jax.ShapeDtypeStruct((rows, width), low),
            jax.ShapeDtypeStruct((rows, width), wide),
            jax.ShapeDtypeStruct((rows, width), low),
            jax.ShapeDtypeStruct((width, 128), low),
            jax.ShapeDtypeStruct((1, width), wide),
            jax.ShapeDtypeStruct((SOURCES, half, HEADS_WIDE), low),
            jax.ShapeDtypeStruct((width, hidden_width), low),
            jax.ShapeDtypeStruct((width, hidden_width), low),
            jax.ShapeDtypeStruct((hidden_width, width), low),
        ),
        in_specs=[vmem] * 15 + [anywhere] * 4,
        out_specs=[vmem] * 7 + [anywhere] * 3,
        scratch_shapes=[
            pltpu.VMEM((width, hidden_width), low),
            pltpu.VMEM((width, hidden_width), low),
            pltpu.VMEM((hidden_width, width), low),
            pltpu.VMEM((width, width), low),
            pltpu.VMEM((width, 128), low),
            heads,
            heads,
            pltpu.VMEM((rows, width), wide),
            pltpu.VMEM((rows, width), low),
            pltpu.VMEM((rows, width), wide),

            pltpu.VMEM((SOURCES * MAIN_ROWS, rows), low),
            pltpu.VMEM((4, SOURCES * REST_ROWS, rows), low),
            pltpu.VMEM((TOP, SOURCES * REST_ROWS, rows), low),
            pltpu.VMEM((TOP, rows, SOURCES * MAIN_ROWS), low),
            pltpu.VMEM((TOP, 4, rows, SOURCES * REST_ROWS), low),
            pltpu.VMEM((TOP, rows, SOURCES * REST_ROWS), low),
            main, long_rest, main, rest, main, long_rest, main, long_rest, main, rest,
            pltpu.VMEM((count, width), low),
            pltpu.VMEM((count, width), low),
            pltpu.VMEM((count, hidden_width), wide),
            pltpu.VMEM((count, hidden_width), wide),
            pltpu.VMEM((count, hidden_width), low),
            pltpu.VMEM((count, hidden_width), low),
            pltpu.VMEM((count, hidden_width), low),
            pltpu.VMEM((count, width), low),
            pltpu.VMEM((width, count), low),
            dma((5,)), dma((3,)), dma((2 * SOURCES,)), dma((2 * SOURCES,)),
            dma((8 * SOURCES,)), dma((8 * SOURCES,)),
        ],
        compiler_params=pltpu.CompilerParams(
            collective_id=3, has_side_effects=True, vmem_limit_bytes=62 * 2**20
        ),
        cost_estimate=pl.CostEstimate(
            flops=18 * count * width * hidden_width, bytes_accessed=40 * 2**20, transcendentals=0
        ),
        name="run_middle",
    )(
        head_out.reshape(SOURCES, half, HEADS_WIDE), tokens, cotangent, *cotangent_rows, routes, routes.T,
        scale[None, :],
        *unpack_tables(), packed, *weights,
    )


KEY_STEP, QUERY_STEP = 512, 128
BACK_KEY_STEP, BACK_QUERY_STEP = 256, 256


def allowed_block(block, pos, start, key_step):
    keys = lax.broadcasted_iota(jnp.int32, (key_step, pos.shape[1]), 0) + block * key_step
    return (keys <= pos) & (keys >= start)


def attend_kernel(low, high, pos_ref, start_ref, query_ref, kv_ref, kvt_ref, out_ref, outt_ref, log_ref):
    zeros = jnp.zeros((QUERY_STEP, HEAD_SIZE), jnp.bfloat16)

    @pl.loop(0, query_ref.shape[0] // QUERY_STEP)
    def _(tile):
        rows = pl.ds(pl.multiple_of(tile * QUERY_STEP, QUERY_STEP), QUERY_STEP)
        pos, start = pos_ref[:, rows], start_ref[:, rows]
        queries = query_ref[rows, :]
        padded = [
            jnp.concatenate([queries[:, h * HEAD_SIZE : (h + 1) * HEAD_SIZE], zeros], axis=1)
            for h in range(GROUP)
        ]

        def step(block, carry):
            keys = pl.ds(pl.multiple_of(block * KEY_STEP, KEY_STEP), KEY_STEP)
            kv = kv_ref[keys, :]
            values_t = kvt_ref[HEAD_SIZE:, keys]
            allowed = allowed_block(block, pos, start, KEY_STEP)
            new = []
            for h in range(GROUP):
                highest, total, summed = carry[h]
                scores = jnp.where(allowed, across(kv, padded[h]), NEGATIVE)
                new_high = jnp.maximum(highest, jnp.max(scores, axis=0, keepdims=True))
                weights = jnp.exp(scores - new_high)
                shrink = jnp.exp(highest - new_high)
                total = total * shrink + jnp.sum(weights, axis=0, keepdims=True)
                summed = summed * shrink + dot32(values_t, weights.astype(jnp.bfloat16))
                new.append((new_high, total, summed))
            return tuple(new)

        first = tuple(
            (
                jnp.full((1, QUERY_STEP), NEGATIVE, jnp.float32),
                jnp.zeros((1, QUERY_STEP), jnp.float32),
                jnp.zeros((HEAD_SIZE, QUERY_STEP), jnp.float32),
            )
            for _ in range(GROUP)
        )
        last = lax.fori_loop(low[tile], high[tile], step, first)
        pieces = []
        for h in range(GROUP):
            highest, total, summed = last[h]
            log_ref[h : h + 1, rows] = highest + jnp.log(total)
            summed = summed / total
            outt_ref[h, :, rows] = summed
            pieces.append(summed)
        out_ref[rows, :] = jnp.concatenate(pieces, axis=0).T.astype(jnp.bfloat16)


def attend_back_kernel(
    low, high, pos_ref, start_ref, query_ref, kv_ref, kvt_ref, outt_ref, log_ref, grad_ref,
    grad_query_ref, grad_kv_ref, sums,
):
    zeros = jnp.zeros((BACK_QUERY_STEP, HEAD_SIZE), jnp.bfloat16)
    sums[...] = jnp.zeros_like(sums)

    @pl.loop(0, query_ref.shape[0] // BACK_QUERY_STEP)
    def _(tile):
        rows = pl.ds(pl.multiple_of(tile * BACK_QUERY_STEP, BACK_QUERY_STEP), BACK_QUERY_STEP)
        pos, start = pos_ref[:, rows], start_ref[:, rows]
        queries, grads = query_ref[rows, :], grad_ref[rows, :]
        grads_t = grads.astype(jnp.float32).T
        query_pads, grad_pads, deltas, logs = [], [], [], []
        for h in range(GROUP):
            part = slice(h * HEAD_SIZE, (h + 1) * HEAD_SIZE)
            query_pads.append(jnp.concatenate([queries[:, part], zeros], axis=1))
            grad_pads.append(jnp.concatenate([zeros, grads[:, part]], axis=1))
            deltas.append(jnp.sum(grads_t[part, :] * outt_ref[h, :, rows], axis=0, keepdims=True))
            logs.append(log_ref[h : h + 1, rows])

        def step(block, carry):
            keys = pl.ds(pl.multiple_of(block * BACK_KEY_STEP, BACK_KEY_STEP), BACK_KEY_STEP)
            kv = kv_ref[keys, :]
            keys_t = kvt_ref[:HEAD_SIZE, keys]
            allowed = allowed_block(block, pos, start, BACK_KEY_STEP)
            new = []
            total = sums[keys, :]
            for h in range(GROUP):
                scores = jnp.where(allowed, across(kv, query_pads[h]), NEGATIVE)
                probs = jnp.exp(scores - logs[h])
                grad_probs = across(kv, grad_pads[h])
                grad_scores = (probs * (grad_probs - deltas[h])).astype(jnp.bfloat16)
                total += dot32(probs.astype(jnp.bfloat16), grad_pads[h])
                total += dot32(grad_scores, query_pads[h])
                new.append(carry[h] + dot32(keys_t, grad_scores))
            sums[keys, :] = total
            return tuple(new)

        first = tuple(jnp.zeros((HEAD_SIZE, BACK_QUERY_STEP), jnp.float32) for _ in range(GROUP))
        last = lax.fori_loop(low[tile], high[tile], step, first)
        factor = HEAD_SIZE ** (-0.5)
        grad_query_ref[rows, :] = (jnp.concatenate(last, axis=0) * factor).T.astype(jnp.bfloat16)

    grad_kv_ref[...] = sums[...].astype(jnp.bfloat16)


def attend_call(kernel, name, bounds, arrays, out_shape, scratch, matmuls, area):
    vmem = pl.BlockSpec(memory_space=pltpu.VMEM)
    return pl.pallas_call(
        kernel,
        out_shape=out_shape,
        grid_spec=pltpu.PrefetchScalarGridSpec(
            num_scalar_prefetch=2,
            grid=(1,),
            in_specs=[vmem] * len(arrays),
            out_specs=[vmem] * len(out_shape),
            scratch_shapes=scratch,
        ),
        compiler_params=pltpu.CompilerParams(vmem_limit_bytes=32 * 2**20),
        cost_estimate=pl.CostEstimate(
            flops=matmuls * 2 * HEAD_SIZE * area, bytes_accessed=8 * 2**20, transcendentals=area
        ),
        name=name,
    )(*bounds, *arrays)


def shards(
    tokens,
    segments,
    routes,
    gain_attn,
    w_query,
    key_weight,
    value_weight,
    w_out,
    w_router,
    gain_ffn,
    w_gate,
    w_up,
    w_down,
    cotangent,
):
    low = jnp.bfloat16
    wide = jnp.float32
    device_rows, width = tokens.shape
    sequence = segments.shape[0]
    half = device_rows // 2
    core = lax.axis_index("ctx") % 2
    ctx_count = lax.axis_size("ctx")
    slice_rows = w_query.shape[0]
    kv_shards = jnp.stack(
        [
            key_weight.reshape(slice_rows, KEY_VALUE_HEADS, HEAD_SIZE),
            value_weight.reshape(slice_rows, KEY_VALUE_HEADS, HEAD_SIZE),
        ],
        axis=2,
    ).reshape(slice_rows, 2 * KEY_VALUE_HEADS * HEAD_SIZE)
    shard = jnp.concatenate(
        [w_query, kv_shards, w_out, w_router, gain_attn[:, None], gain_ffn[:, None]], axis=1
    )
    shard = jnp.pad(shard, ((0, 0), (0, PACK - shard.shape[1])))
    packed, expert_weights, head_queries, head_kv, scales, *cotangent_rows = gather_weights(
        shard, tokens, cotangent, routes, w_gate[0], w_up[0], w_down[0]
    )
    head_queries = head_queries.reshape(-1, HEADS_WIDE)
    head_kv = head_kv.reshape(sequence, 2 * HEAD_SIZE)
    order = jnp.arange(ctx_count * half, dtype=jnp.int32)
    query_pos = (order // half) * device_rows + core * half + order % half
    first_of = jnp.sum(
        (segments[:, None] < jnp.arange(5, dtype=jnp.int32)[None, :]).astype(jnp.int32), axis=0
    )
    starts = jnp.sum(
        jnp.where(segments[:, None] == jnp.arange(5, dtype=jnp.int32)[None, :], first_of[None, :], 0),
        axis=1,
    )
    query_start = lax.dynamic_slice_in_dim(
        starts.reshape(ctx_count, device_rows), core * half, half, axis=1
    ).reshape(-1)

    def bounds_of(query_step, key_step):
        return (
            query_start.reshape(-1, query_step)[:, 0] // key_step,
            query_pos.reshape(-1, query_step)[:, -1] // key_step + 1,
        )

    mask_rows = (query_pos[None, :], query_start[None, :])

    head_kvt = head_kv.T
    count = head_queries.shape[0]
    area = GROUP * count * sequence // 3
    head_out, head_outt, log_total = attend_call(
        attend_kernel,
        "attend",
        bounds_of(QUERY_STEP, KEY_STEP),
        (*mask_rows, head_queries, head_kv, head_kvt),
        (
            jax.ShapeDtypeStruct((count, HEADS_WIDE), low),
            jax.ShapeDtypeStruct((GROUP, HEAD_SIZE, count), wide),
            jax.ShapeDtypeStruct((GROUP, count), wide),
        ),
        [],
        2,
        area,
    )
    (
        attended, mixed, grad_hidden_one, grad_branch, grad_router_full, grad_gain_two, head_grads,
        *expert_grads,
    ) = run_middle(
        head_out, tokens, cotangent, cotangent_rows, routes, scales[1], packed, expert_weights
    )
    head_grads = head_grads.reshape(-1, HEADS_WIDE)

    head_grad_queries, head_grad_kv = attend_call(
        attend_back_kernel,
        "attend_back",
        bounds_of(BACK_QUERY_STEP, BACK_KEY_STEP),
        (*mask_rows, head_queries, head_kv, head_kvt, head_outt, log_total, head_grads),
        (
            jax.ShapeDtypeStruct((count, HEADS_WIDE), low),
            jax.ShapeDtypeStruct((sequence, 2 * HEAD_SIZE), low),
        ),
        [pltpu.VMEM((sequence, 2 * HEAD_SIZE), wide)],
        5,
        area,
    )
    grad_input, out_share, share, (grad_gate, grad_up, grad_down) = scatter_sum(
        head_grad_queries, head_grad_kv, tokens, scales, grad_hidden_one, grad_branch, attended,
        grad_router_full, grad_gain_two, packed, expert_grads,
    )
    share, out_share = share.astype(wide), out_share.astype(wide)
    kv_share = share[:, 1536:2560].reshape(slice_rows, KEY_VALUE_HEADS, 2, HEAD_SIZE)
    return (
        mixed,
        grad_input,
        share[:, 2576],
        share[:, :1536],
        kv_share[:, :, 0].reshape(slice_rows, -1),
        kv_share[:, :, 1].reshape(slice_rows, -1),
        out_share,
        share[:, 2560:2576],
        share[:, 2577],
        grad_gate[None],
        grad_up[None],
        grad_down[None],
    )


def solution(mesh):
    in_specs = (
        P(("dp", "ctx"), None),
        P("dp"),
        P(("dp", "ctx"), None),
        P(("dp", "ctx")),
        P(("dp", "ctx"), None),
        P(("dp", "ctx"), None),
        P(("dp", "ctx"), None),
        P(("dp", "ctx"), None),
        P(("dp", "ctx"), None),
        P(("dp", "ctx")),
        P("ctx", "dp", None),
        P("ctx", "dp", None),
        P("ctx", "dp", None),
        P(("dp", "ctx"), None),
    )
    out_specs = (
        P(("dp", "ctx"), None),
        P(("dp", "ctx"), None),
        P(("dp", "ctx")),
        P(("dp", "ctx"), None),
        P(("dp", "ctx"), None),
        P(("dp", "ctx"), None),
        P(("dp", "ctx"), None),
        P(("dp", "ctx"), None),
        P(("dp", "ctx")),
        P("ctx", "dp", None),
        P("ctx", "dp", None),
        P("ctx", "dp", None),
    )
    return jax.shard_map(shards, mesh=mesh, in_specs=in_specs, out_specs=out_specs, check_vma=False)
```

```python
import functools

import jax
import jax.numpy as jnp
import numpy as np
from jax import lax
from jax.experimental import pallas as pl
from jax.experimental.pallas import tpu as pltpu
from jax.sharding import PartitionSpec as P

QUERY_HEAD_COUNT = 24
KEY_VALUE_HEADS = 8
HEAD_SIZE = 64
TOP = 2

EPSILON = 1e-06
NEGATIVE = -1e30
SOURCES = 16
GROUP = QUERY_HEAD_COUNT // KEY_VALUE_HEADS
HEADS_WIDE = GROUP * HEAD_SIZE
MESH = pl.DeviceIdType.MESH

PACK = 4608
HALF = PACK // 2
QUARTER = PACK // 4
RING_ORDERS = (("x", "y", "z"), ("y", "z", "x"), ("z", "x", "y"))


def place():
    dp = lax.axis_index("dp")
    ctx = lax.axis_index("ctx")
    return {"y": dp // 2, "z": (ctx // 8) * 2 + dp % 2, "x": (ctx // 2) % 4, "core": ctx % 2}


def device_of(spot):
    z = spot["z"]
    return (spot["y"] * 2 + z % 2, (z // 2) * 8 + spot["x"] * 2 + spot["core"])


def moved(spot, axis, step):
    other = dict(spot)
    if axis == "core":
        other["core"] = 1 - spot["core"]
    else:
        other[axis] = (spot[axis] + step) % 4
    return other


def member(spot, step):
    index = (spot["x"] % 2) * 2 + spot["core"]
    target = (index // 2 + step // 2) % 2 * 2 + (index % 2 + step % 2) % 2
    other = dict(spot)
    other["x"] = (spot["x"] // 2) * 2 + target // 2
    other["core"] = target % 2
    return other, target


def partner(spot):
    other = dict(spot)
    other["z"] = spot["z"] // 2 * 2 + (spot["z"] + 1) % 2
    other["core"] = (spot["core"] + 1) % 2
    return other


def others_of(ctx):
    return [(step, (ctx + step) % SOURCES) for step in range(1, SOURCES)]


def meet(spot, heads, picks=()):
    barrier = pltpu.get_barrier_semaphore()
    others = [partner(spot)] + [moved(spot, "y", step) for step in (1, 2, 3)]
    others += [moved(spot, "z", step) for step in (1, 3)]
    others = [device_of(other) for other in others]
    others += [(lax.axis_index("dp"), other) for _, other in heads]
    for other in others:
        pl.semaphore_signal(barrier, inc=1, device_id=other, device_id_type=MESH)
    for pick in picks:
        for step in range(1, SOURCES):
            pl.semaphore_signal(barrier, inc=1, device_id=pick(step)[1], device_id_type=MESH)

    if picks:

        @pl.when(spot["z"] % 2 != spot["core"])
        def _():
            for pick in picks:
                pl.semaphore_signal(barrier, inc=1, device_id=pick(0)[1], device_id_type=MESH)

    away = (spot["z"] + spot["core"]) % 2
    amount = len(others) + len(picks) * (SOURCES - 1)
    pl.semaphore_wait(barrier, amount + len(picks) * away if picks else amount)


def region(spot, known, part, base):
    def pick(axis, value, size):
        return pl.ds(0, size) if axis in known else pl.ds(value, 1)

    z = spot["z"]
    if "x" in known:
        columns = pl.ds(base, HALF)
    else:
        columns = pl.ds(pl.multiple_of(base + (spot["x"] % 2) * QUARTER, 128), QUARTER)
    return (
        pick("y", spot["y"], 4),
        pick("z", z % 2, 2),
        pick("z", z // 2, 2),
        pick("x", spot["x"] // 2, 2),
        pl.ds(part * 16, 16),
        columns,
    )


def expert_rows(ref, spot, core, half=None):
    rows = ref.shape[0] // 8
    first = (spot["y"] * 2 + core) * rows
    if half is not None:
        rows //= 2
        first += half * rows
    return ref.at[pl.ds(pl.multiple_of(first, 32), rows)]


def half_region(where, axis, half):
    if axis == "y":
        return where[:1] + (pl.ds(half, 1),) + where[2:]
    return (pl.ds(2 * half, 2),) + where[1:]


def relay(ring, numbers, send, recv, whole, half):
    spot, axis = ring

    def copy(ref, step, number):
        return pltpu.make_async_remote_copy(
            src_ref=ref,
            dst_ref=ref,
            send_sem=send.at[numbers + number],
            recv_sem=recv.at[numbers + number],
            device_id=device_of(moved(spot, axis, step)),
            device_id_type=MESH,
        )

    first = [copy(whole(spot), 1, 0), copy(whole(spot), 3, 1)]
    second = [copy(half(moved(spot, axis, 3), 0), 1, 2), copy(half(moved(spot, axis, 1), 1), 3, 3)]
    return first, second


def gather_kernel(
    shard, merge, tokens, cotangent, routes_t, own_gate, own_up, own_down,
    out, gate_out, up_out, down_out, head_rows, head_kv, scales, c_main_in, c_rest_in,
    pieces, joined, qkv_w, rest_w, normed, qkv, packed, packed_kv,
    send0, recv0, send, recv, send_core, recv_core, local,
    swap_send, swap_recv, swap_local, line_send, line_recv, mate_send, mate_recv, ring_send, ring_recv,
    head_send, head_recv, head_local,
    send_main, send_rest, c_main, c_rest, route_send, route_recv,
):
    spot = place()
    dp, ctx = lax.axis_index("dp"), lax.axis_index("ctx")
    holder, sender, start = expert_routes(dp, ctx, route_send, route_recv)
    meet(spot, others_of(ctx), (holder, sender))
    mate = moved(spot, "core", 1)
    stays = spot["core"] == spot["z"] % 2
    experts = ((own_gate, gate_out), (own_up, up_out), (own_down, down_out))

    def swaps():
        return [
            pltpu.make_async_remote_copy(
                src_ref=own,
                dst_ref=expert_rows(whole, spot, spot["z"] % 2),
                send_sem=swap_send.at[n],
                recv_sem=swap_recv.at[n],
                device_id=device_of(partner(spot)),
                device_id_type=MESH,
            )
            for n, (own, whole) in enumerate(experts)
        ]

    def stays_here():
        return [
            pltpu.make_async_copy(own, expert_rows(whole, spot, spot["core"]), swap_local.at[n])
            for n, (own, whole) in enumerate(experts)
        ]

    def line(n):
        whole = experts[n][1]
        return relay(
            (spot, "y"),
            4 * n,
            line_send,
            line_recv,
            lambda at: expert_rows(whole, at, spot["core"]),
            lambda at, half: expert_rows(whole, at, spot["core"], half),
        )

    def to_mates(step):
        source = moved(spot, "y", 4 - step)
        return [
            pltpu.make_async_remote_copy(
                src_ref=expert_rows(whole, source, spot["core"]),
                dst_ref=expert_rows(whole, source, spot["core"]),
                send_sem=mate_send.at[3 * step + n],
                recv_sem=mate_recv.at[3 * step + n],
                device_id=device_of(mate),
                device_id_type=MESH,
            )
            for n, (own, whole) in enumerate(experts)
        ]

    def start_all(copies):
        for copy in copies:
            copy.start()

    @pl.when(stays)
    def _():
        start_all(stays_here())

    @pl.when(jnp.logical_not(stays))
    def _():
        start_all(swaps())

    index = (spot["x"] % 2) * 2 + spot["core"]
    quarter = spot["core"] * 2 + spot["x"] % 2
    copies = []
    for step in (1, 2, 3):
        other, target = member(spot, step)
        goal = other["core"] * 2 + other["x"] % 2
        copy = pltpu.make_async_remote_copy(
            src_ref=shard.at[:, pl.ds(pl.multiple_of(goal * QUARTER, 128), QUARTER)],
            dst_ref=pieces.at[index],
            send_sem=send0.at[step - 1],
            recv_sem=recv0.at[step - 1],
            device_id=device_of(other),
            device_id_type=MESH,
        )
        copy.start()
        copies.append(copy)
    pieces[index] = shard[:, pl.ds(pl.multiple_of(quarter * QUARTER, 128), QUARTER)]
    fill_tables(routes_t, send_main, send_rest)
    pack((send_main, send_rest), cotangent, c_main, c_rest)
    for copy in copies:
        copy.wait()
    joined[...] = jnp.dot(
        merge[...], pieces[...].reshape(64, QUARTER), preferred_element_type=jnp.float32
    ).astype(jnp.bfloat16)
    base = pl.multiple_of(spot["core"] * HALF, 128)
    mine = region(spot, "", 0, base)
    own = pltpu.make_async_copy(
        joined,
        out.at[spot["y"], spot["z"] % 2, spot["z"] // 2, spot["x"] // 2, :, mine[5]],
        local,
    )
    own.start()
    own.wait()
    core_copies = []

    def to_mate(number, where):
        copy = pltpu.make_async_remote_copy(
            src_ref=out.at[where],
            dst_ref=out.at[where],
            send_sem=send_core.at[number],
            recv_sem=recv_core.at[number],
            device_id=device_of(mate),
            device_id_type=MESH,
        )
        copy.start()
        core_copies.append(copy)

    flights, relays, finals = {}, [], []
    for stage in range(3):
        for part, order in enumerate(RING_ORDERS):
            axis, known = order[stage], order[:stage]
            if stage > 0:
                for copy in flights[part]:
                    copy.wait_recv()
            where = region(spot, known, part, base)
            if stage == 2:
                ring = relay(
                    (spot, axis),
                    4 * part,
                    ring_send,
                    ring_recv,
                    lambda at, known=known, part=part: out.at[region(at, known, part, base)],
                    lambda at, half, known=known, part=part, axis=axis: out.at[
                        half_region(region(at, known, part, base), axis, half)
                    ],
                )
                start_all(ring[0])
                relays.append(ring)
                finals.append((axis, known))
                to_mate(part * 4, where)
                continue
            started = []
            for step in (1, 3, 2):
                number = (stage * 3 + part) * 3 + step - 1
                copy = pltpu.make_async_remote_copy(
                    src_ref=out.at[where],
                    dst_ref=out.at[where],
                    send_sem=send.at[number],
                    recv_sem=recv.at[number],
                    device_id=device_of(moved(spot, axis, step)),
                    device_id_type=MESH,
                )
                copy.start()
                started.append(copy)
            flights[part] = started
            copies += started
        if stage == 1:

            @pl.when(stays)
            def _():
                for copy in stays_here():
                    copy.wait()

            @pl.when(jnp.logical_not(stays))
            def _():
                for copy in swaps():
                    copy.wait()


    mates = {step: to_mates(step) for step in (1, 3, 2)}

    def pass_on(ring):
        first, second = ring
        for number in range(2):
            first[number].wait_recv()
            second[number].start()

    residual = tokens[...].astype(jnp.float32)
    inverse = lax.rsqrt(jnp.mean(residual * residual, axis=1, keepdims=True) + EPSILON)
    for ring in relays:
        pass_on(ring)
    lines = [line(n) for n in range(3)]
    for first, _ in lines:
        start_all(first)
    own_mates = to_mates(0)
    flights = start(0, holder, ctx, c_main, c_rest, c_main_in, c_rest_in)
    for part, (axis, _) in enumerate(finals):
        for step in (1, 3):
            to_mate(part * 4 + step, region(moved(spot, axis, 4 - step), RING_ORDERS[part][:2], part, base))
    for part, (_, second) in enumerate(relays):
        for copy in second:
            copy.wait_recv()
        axis = RING_ORDERS[part][2]
        to_mate(part * 4 + 2, region(moved(spot, axis, 2), RING_ORDERS[part][:2], part, base))
    for copy in core_copies:
        copy.wait_recv()
    kv_at = QUERY_HEAD_COUNT * HEAD_SIZE
    qkv_width = qkv.shape[1]
    loads = [
        pltpu.make_async_copy(
            out.at[:, :, :, :, :, pl.ds(PACK - 512, 128)], rest_w, head_local.at[2]
        ),
        pltpu.make_async_copy(out.at[:, :, :, :, :, pl.ds(0, qkv_width)], qkv_w, head_local.at[3]),
    ]
    for load in loads:
        load.start()
    loads[0].wait()
    gains = rest_w[...].reshape(1536, 128).astype(jnp.float32).T
    scales[...] = gains[16:24, :]
    normed[...] = (residual * inverse * gains[16:17, :]).astype(jnp.bfloat16)
    loads[1].wait()
    factor = HEAD_SIZE ** (-0.5)

    @pl.loop(0, qkv_width // 256)
    def _(n):
        at = pl.ds(pl.multiple_of(n * 256, 256), 256)
        rows = jnp.dot(
            normed[...], qkv_w[:, :, :, :, :, at].reshape(1536, 256), preferred_element_type=jnp.float32
        )
        qkv[:, at] = (rows * jnp.where(n < kv_at // 256, factor, 1.0)).astype(jnp.bfloat16)

    half = tokens.shape[0] // 2
    for head in range(KEY_VALUE_HEADS):
        for core in range(2):
            packed[2 * head + core] = qkv[
                core * half : (core + 1) * half, head * HEADS_WIDE : (head + 1) * HEADS_WIDE
            ]

    for head in range(KEY_VALUE_HEADS):
        for which in range(2):
            start = kv_at + (which * KEY_VALUE_HEADS + head) * HEAD_SIZE
            packed_kv[head, :, which * HEAD_SIZE : (which + 1) * HEAD_SIZE] = qkv[
                :, start : start + HEAD_SIZE
            ]

    def kv_of(other):
        return packed_kv.at[other // 2]

    own_heads = [
        pltpu.make_async_copy(packed.at[ctx], head_rows.at[ctx], head_local.at[0]),
        pltpu.make_async_copy(kv_of(ctx), head_kv.at[ctx], head_local.at[1]),
    ]
    for copy in own_heads:
        copy.start()
    head_copies = []
    for step, other in others_of(ctx):
        for source, place_in, first in (
            (kv_of(other), head_kv.at[ctx], SOURCES),
            (packed.at[other], head_rows.at[ctx], 0),
        ):
            copy = pltpu.make_async_remote_copy(
                src_ref=source,
                dst_ref=place_in,
                send_sem=head_send.at[first + step],
                recv_sem=head_recv.at[first + step],
                device_id=(dp, other),
                device_id_type=MESH,
            )
            copy.start()
            head_copies.append(copy)
    start_all(own_mates)
    for n, ring in enumerate(lines):
        pass_on(ring)
        mates[1][n].start()
        mates[3][n].start()
    for n, (_, second) in enumerate(lines):
        for copy in second:
            copy.wait_recv()
        mates[2][n].start()
    line_copies = [copy for first, second in lines + relays for copy in first + second]
    for copy in own_heads + head_copies:
        copy.wait()
    flights[0]()
    flights[1]()
    for copy in copies[3:] + line_copies:
        copy.wait_send()
    for copy in core_copies:
        copy.wait_send()
    for copy in own_mates + mates[1] + mates[2] + mates[3]:
        copy.wait()


def gather_weights(shard, tokens, cotangent, routes, gate, up, down):
    shard = jnp.pad(shard, ((0, 4), (0, 0)))
    target, source = np.arange(48)[:, None], np.arange(64)[None, :]
    merge = jnp.asarray(
        (target // 12 == source // 16) & (target % 12 == source % 16), jnp.bfloat16
    )
    vmem = pl.BlockSpec(memory_space=pltpu.VMEM)
    anywhere = pl.BlockSpec(memory_space=pltpu.HBM)
    low = jnp.bfloat16
    rows, width = tokens.shape
    qkv_width = QUERY_HEAD_COUNT * HEAD_SIZE + 2 * KEY_VALUE_HEADS * HEAD_SIZE
    experts = [
        jax.ShapeDtypeStruct((8 * part.shape[0], part.shape[1]), low) for part in (gate, up, down)
    ]
    dma = pltpu.SemaphoreType.DMA
    packed, *rest = pl.pallas_call(
        gather_kernel,
        out_shape=[jax.ShapeDtypeStruct((4, 2, 2, 2, 48, PACK), low)]
        + experts
        + [
            jax.ShapeDtypeStruct((SOURCES, rows // 2, HEADS_WIDE), low),
            jax.ShapeDtypeStruct((SOURCES, rows, 2 * HEAD_SIZE), low),
            jax.ShapeDtypeStruct((8, width), jnp.float32),
            jax.ShapeDtypeStruct((SOURCES, MAIN_ROWS, width), low),
            jax.ShapeDtypeStruct((SOURCES, REST_ROWS, REST_WIDTH), low),
        ],
        in_specs=[vmem] * 5 + [anywhere] * 3,
        out_specs=[anywhere] * 4 + [vmem] * 5,
        scratch_shapes=[
            pltpu.VMEM((4, 16, QUARTER), low),
            pltpu.VMEM((48, QUARTER), low),
            pltpu.VMEM((4, 2, 2, 2, 48, qkv_width), low),
            pltpu.VMEM((4, 2, 2, 2, 48, 128), low),
            pltpu.VMEM((rows, width), low),
            pltpu.VMEM((rows, qkv_width), low),
            pltpu.VMEM((SOURCES, rows // 2, HEADS_WIDE), low),
            pltpu.VMEM((KEY_VALUE_HEADS, rows, 2 * HEAD_SIZE), low),
            dma((3,)), dma((3,)), dma((18,)), dma((18,)), dma((12,)), dma((12,)), dma,
            dma((3,)), dma((3,)), dma((3,)), dma((12,)), dma((12,)), dma((12,)), dma((12,)),
            dma((12,)), dma((12,)),
            dma((2 * SOURCES,)), dma((2 * SOURCES,)), dma((4,)),
            pltpu.VMEM((SOURCES * MAIN_ROWS, rows), low),
            pltpu.VMEM((4, SOURCES * REST_ROWS, rows), low),
            pltpu.VMEM((SOURCES, MAIN_ROWS, width), low),
            pltpu.VMEM((SOURCES, REST_ROWS, REST_WIDTH), low),
            dma((2 * SOURCES,)), dma((2 * SOURCES,)),
        ],
        compiler_params=pltpu.CompilerParams(
            collective_id=1, has_side_effects=True, vmem_limit_bytes=62 * 2**20
        ),
        cost_estimate=pl.CostEstimate(
            flops=2 * rows * width * qkv_width, bytes_accessed=40 * 2**20, transcendentals=0
        ),
        name="gather_weights",
    )(shard, merge, tokens, cotangent, routes.T, gate, up, down)
    return packed.reshape(1536, PACK), rest[:3], *rest[3:]


EARLY = 1536
EARLY_ORDERS = (("y", "z", "x"), ("y", "x", "z"), ("y", "z", "x"))
LATE_ORDERS = (("y", "z", "x"), ("y", "x", "z"), ("y", "x", "z"))


def cut(spot, known, part, half):
    z = spot["z"]

    def pick(axis, value, size):
        return pl.ds(0, size) if axis in known else pl.ds(value, 1)

    columns = pl.ds(0, half)
    if "x" not in known:
        columns = pl.ds(pl.multiple_of((spot["x"] % 2) * (half // 2), 128), half // 2)
    return (
        pick("y", spot["y"], 4),
        pick("z", z % 2, 2),
        pick("z", z // 2, 2),
        pick("x", spot["x"] // 2, 2),
        pl.ds(part * 16, 16),
        columns,
    )


def landing_shape(known, half):
    return (
        4 if "y" in known else 1,
        2 if "z" in known else 1,
        2 if "z" in known else 1,
        2 if "x" in known else 1,
        16,
        half if "x" in known else half // 2,
    )


class Scatter:
    def __init__(self, orders, spot, split, grads, total, done, packed, out, sems, landing):
        self.spot, self.split, self.grads, self.total, self.out = spot, split, grads, total, out
        self.done, self.packed = done, packed
        self.orders = orders
        self.send_core, self.recv_core, self.send, self.recv, self.send_last, self.recv_last = sems
        self.landing = (landing[:3], landing[3:6], landing[6:9])
        self.half = total.shape[-1]
        self.base = pl.multiple_of(spot["core"] * self.half, 128)
        self.pending, self.copies = [], []

    def start(self):
        mate = moved(self.spot, "core", 1)
        mate_base = pl.multiple_of(mate["core"] * self.half, 128)
        for part in range(3):
            rows = pl.ds(part * 16, 16)
            copy = pltpu.make_async_remote_copy(
                src_ref=self.grads.at[:, :, :, :, rows, pl.ds(mate_base, self.half)],
                dst_ref=self.total.at[:, :, :, :, rows, :],
                send_sem=self.send_core.at[part],
                recv_sem=self.recv_core.at[part],
                device_id=device_of(mate),
                device_id_type=MESH,
            )
            copy.start()
            self.copies.append(copy)

    def first(self):
        cores = list(self.copies)
        for part in range(3):
            rows = pl.ds(part * 16, 16)
            cores[part].wait_recv()

            @pl.loop(0, 32)
            def _(block):
                at = (block // 8, (block // 4) % 2, (block // 2) % 2, block % 2, rows)
                self.total[at] = (
                    self.grads[at + (pl.ds(self.base, self.half),)].astype(jnp.float32)
                    + self.total[at].astype(jnp.float32)
                ).astype(jnp.bfloat16)

            self.pending.append(self.ring(part, 0))

    def ring(self, part, stage):
        axis, known = self.orders[part][2 - stage], self.orders[part][: 2 - stage]
        started = []
        for step in (1, 3, 2):
            other = moved(self.spot, axis, step)
            number = (stage * 3 + part) * 3 + step - 1
            copy = pltpu.make_async_remote_copy(
                src_ref=self.total.at[cut(other, known, part, self.half)],
                dst_ref=self.landing[stage][part].at[step - 1],
                send_sem=self.send.at[number],
                recv_sem=self.recv.at[number],
                device_id=device_of(other),
                device_id_type=MESH,
            )
            copy.start()
            started.append(copy)
        self.copies += started
        return started

    def next(self, stage):
        for part in range(3):
            known = self.orders[part][: 2 - stage]
            for copy in self.pending[part]:
                copy.wait_recv()
            self.add(known, part, self.landing[stage][part])
            if stage < 2:
                self.pending[part] = self.ring(part, stage + 1)

    def add(self, known, part, landing):
        spot = self.spot
        shape = landing_shape(known, self.half)
        columns = cut(spot, known, part, self.half)[5]

        def body(block):
            a, b, c, d = (
                block // (shape[1] * shape[2] * shape[3]),
                (block // (shape[2] * shape[3])) % shape[1],
                (block // shape[3]) % shape[2],
                block % shape[3],
            )
            at = (
                a + (0 if "y" in known else spot["y"]),
                b + (0 if "z" in known else spot["z"] % 2),
                c + (0 if "z" in known else spot["z"] // 2),
                d + (0 if "x" in known else spot["x"] // 2),
                pl.ds(part * 16, 16),
                columns,
            )
            summed = self.total[at].astype(jnp.float32)
            for step in range(3):
                summed += landing[step, a, b, c, d].astype(jnp.float32)
            self.total[at] = summed.astype(jnp.bfloat16)

        count = shape[0] * shape[1] * shape[2] * shape[3]
        if count == 1:
            body(0)
        else:
            pl.loop(0, count)(body)

    def finish(self):
        spot = self.spot
        quarter = self.half // 2
        index = (spot["x"] % 2) * 2 + spot["core"]
        place_in = spot["core"] * 2 + spot["x"] % 2
        mine = cut(spot, "", 0, self.half)
        self.done[...] = self.total[
            spot["y"], spot["z"] % 2, spot["z"] // 2, spot["x"] // 2, :, mine[5]
        ]
        self.packed[...] = (
            jnp.dot(self.split[...], self.done[...], preferred_element_type=jnp.float32)
            .astype(jnp.bfloat16)
            .reshape(4, 16, quarter)
        )
        columns = pl.ds(pl.multiple_of(place_in * quarter, 128), quarter)
        self.last = []
        for step in (1, 2, 3):
            other, target = member(spot, step)
            copy = pltpu.make_async_remote_copy(
                src_ref=self.packed.at[target],
                dst_ref=self.out.at[:, columns],
                send_sem=self.send_last.at[step - 1],
                recv_sem=self.recv_last.at[step - 1],
                device_id=device_of(other),
                device_id_type=MESH,
            )
            copy.start()
            self.last.append(copy)
        self.out[:, columns] = self.packed[index]

    def end(self):
        for copy in self.last:
            copy.wait()
        for copy in self.copies:
            copy.wait_send()


def scatter_kernel(
    head_rows, head_kv, tokens, scales, grad_hidden, branch, attended, router_grad, gain_grad, split,
    packed_w, grad_gate, grad_up, grad_down,
    grad_input, out, late_out, gate_out, up_out, down_out,
    rows_in, kv_in, grad_qkv, grad_normed, normed,
    mate_send, mate_recv, own_sem, line_send, line_recv, swap_send, swap_recv,
    head_send, head_recv, weight_sem,
    *buffers,
):
    spot = place()
    dp, ctx = lax.axis_index("dp"), lax.axis_index("ctx")
    held, mates, lines, results, arrived = (buffers[3 * n : 3 * n + 3] for n in range(5))
    early = Scatter(EARLY_ORDERS, spot, split, *buffers[15:19], out, buffers[19:25], buffers[25:34])
    late = Scatter(LATE_ORDERS, spot, split, *buffers[34:38], late_out, buffers[38:44], buffers[44:])
    wholes, finals = (grad_gate, grad_up, grad_down), (gate_out, up_out, down_out)
    mate = moved(spot, "core", 1)
    qkv_width = grad_qkv.shape[1]
    load = pltpu.make_async_copy(
        packed_w.at[:, :, :, :, :, pl.ds(0, qkv_width)],
        late.grads.at[:, :, :, :, :, pl.ds(0, qkv_width)],
        weight_sem,
    )
    load.start()
    own_copies, mate_copies = [], []
    for n, whole in enumerate(wholes):
        for y in range(4):
            rows = whole.shape[0] // 8

            def part(core, whole=whole, y=y, rows=rows):
                return whole.at[pl.ds(pl.multiple_of((2 * y + core) * rows, 64), rows)]

            own = pltpu.make_async_copy(part(spot["core"]), held[n].at[y], own_sem.at[4 * n + y])
            own.start()
            own_copies.append(own)
            mate_copies.append(
                pltpu.make_async_remote_copy(
                    src_ref=part(mate["core"]),
                    dst_ref=mates[n].at[y],
                    send_sem=mate_send.at[4 * n + y],
                    recv_sem=mate_recv.at[4 * n + y],
                    device_id=device_of(mate),
                    device_id_type=MESH,
                )
            )
    meet(spot, others_of(ctx))
    for copy in mate_copies:
        copy.start()
    head_copies = []
    for step, other in others_of(ctx):
        for source, place_in, first in ((head_kv, kv_in, SOURCES), (head_rows, rows_in, 0)):
            copy = pltpu.make_async_remote_copy(
                src_ref=source.at[other],
                dst_ref=place_in.at[ctx],
                send_sem=head_send.at[first + step],
                recv_sem=head_recv.at[first + step],
                device_id=(dp, other),
                device_id_type=MESH,
            )
            copy.start()
            head_copies.append(copy)
    rows_in[ctx] = head_rows[ctx]
    kv_in[ctx] = head_kv[ctx]

    tile = 512
    grads_shape = (4, 2, 2, 2, 48, tile)

    def fill(turned, right, grads):
        @pl.loop(0, right.shape[1] // tile)
        def _(n):
            at = pl.ds(pl.multiple_of(n * tile, tile), tile)
            grads[:, :, :, :, :, at] = (
                jnp.dot(turned, right[:, at], preferred_element_type=jnp.float32)
                .astype(jnp.bfloat16)
                .reshape(grads_shape)
            )

    fill(branch[...].T, attended, early.grads)
    early.start()

    line_copies = []
    for n in range(3):
        for copy in mate_copies[4 * n : 4 * n + 4]:
            copy.wait_recv()
        for copy in own_copies[4 * n : 4 * n + 4]:
            copy.wait()

        @pl.loop(0, 4)
        def _(y, n=n):
            held[n][y] = (
                held[n][y].astype(jnp.float32) + mates[n][y].astype(jnp.float32)
            ).astype(jnp.bfloat16)

        for step in (1, 3, 2):
            other = moved(spot, "y", step)
            copy = pltpu.make_async_remote_copy(
                src_ref=held[n].at[other["y"]],
                dst_ref=lines[n].at[step - 1],
                send_sem=line_send.at[3 * n + step - 1],
                recv_sem=line_recv.at[3 * n + step - 1],
                device_id=device_of(other),
                device_id_type=MESH,
            )
            copy.start()
            line_copies.append(copy)

    early.first()

    half = tokens.shape[0] // 2
    residual = tokens[...].astype(jnp.float32)
    inverse = lax.rsqrt(jnp.mean(residual * residual, axis=1, keepdims=True) + EPSILON)
    unit = residual * inverse
    scale = scales[0:1, :]
    normed[...] = (unit * scale).astype(jnp.bfloat16)
    for copy in head_copies:
        copy.wait_recv()
    for head in range(KEY_VALUE_HEADS):
        for core in range(2):
            grad_qkv[
                core * half : (core + 1) * half, head * HEADS_WIDE : (head + 1) * HEADS_WIDE
            ] = rows_in[2 * head + core]
        kv_grad = (
            kv_in[2 * head].astype(jnp.float32) + kv_in[2 * head + 1].astype(jnp.float32)
        ).astype(jnp.bfloat16)
        for which in range(2):
            start = QUERY_HEAD_COUNT * HEAD_SIZE + (which * KEY_VALUE_HEADS + head) * HEAD_SIZE
            grad_qkv[:, start : start + HEAD_SIZE] = kv_grad[
                :, which * HEAD_SIZE : (which + 1) * HEAD_SIZE
            ]
    load.wait()
    grad_normed[...] = jnp.zeros_like(grad_normed)

    @pl.loop(0, qkv_width // tile)
    def _(n):
        at = pl.ds(pl.multiple_of(n * tile, tile), tile)
        grad_normed[...] += contract_cols(
            grad_qkv[:, at], late.grads[:, :, :, :, :, at].reshape(1536, tile)
        )

    fill(normed[...].T, grad_qkv, late.grads)
    gain_column = jnp.sum(grad_normed[...] * unit, axis=0, keepdims=True)
    lanes = lax.broadcasted_iota(jnp.int32, (1536, 128), 1)
    first_column = jnp.broadcast_to(gain_column, (128, 1536)).T
    second_column = jnp.broadcast_to(gain_grad[...], (128, 1536)).T
    rest = jnp.where(
        lanes < 16,
        router_grad[...].astype(jnp.float32),
        jnp.where(lanes == 16, first_column, jnp.where(lanes == 17, second_column, 0.0)),
    )
    at = qkv_width
    late.grads[:, :, :, :, :, at : at + 128] = rest.astype(jnp.bfloat16).reshape(4, 2, 2, 2, 48, 128)
    late.grads[:, :, :, :, :, at + 128 :] = jnp.zeros(
        (4, 2, 2, 2, 48, late.grads.shape[-1] - at - 128), jnp.bfloat16
    )
    late.start()
    grads_here = grad_normed[...] * scale
    grads_here = inverse * (
        grads_here - unit * jnp.mean(grads_here * unit, axis=1, keepdims=True)
    )
    grad_input[...] = (grads_here + grad_hidden[...]).astype(jnp.bfloat16)
    late.first()
    early.next(0)
    early.next(1)
    early.next(2)
    early.finish()
    late.next(0)
    sum_lines(spot, held, lines, line_copies, results)
    swap_results(spot, results, arrived, swap_send, swap_recv, True)
    late.next(1)
    late.next(2)
    late.finish()
    swap_results(spot, results, arrived, swap_send, swap_recv, False)
    stays = spot["core"] == spot["z"] % 2

    @pl.when(stays)
    def _():
        for result, final in zip(results, finals):
            final[...] = result[...]

    @pl.when(jnp.logical_not(stays))
    def _():
        for result, final in zip(arrived, finals):
            final[...] = result[...]

    early.end()
    late.end()
    for copy in mate_copies + head_copies + line_copies:
        copy.wait_send()


def sum_lines(spot, held, lines, line_copies, results):
    for copy in line_copies:
        copy.wait_recv()
    for mine, line, result in zip(held, lines, results):
        total = mine[spot["y"]].astype(jnp.float32)
        for step in range(3):
            total += line[step].astype(jnp.float32)
        result[...] = total.astype(jnp.bfloat16)


def swap_results(spot, results, arrived, send, recv, start):
    @pl.when(spot["core"] != spot["z"] % 2)
    def _():
        for n, (result, place_in) in enumerate(zip(results, arrived)):
            copy = pltpu.make_async_remote_copy(
                src_ref=result,
                dst_ref=place_in,
                send_sem=send.at[n],
                recv_sem=recv.at[n],
                device_id=device_of(partner(spot)),
                device_id_type=MESH,
            )
            if start:
                copy.start()
            else:
                copy.wait()


def scatter_sum(
    head_rows, head_kv, tokens, scales, grad_hidden, branch, attended, router_grad, gain_grad, packed,
    expert_grads,
):
    source, target = np.arange(48)[None, :], np.arange(64)[:, None]
    split = jnp.asarray(
        (source // 12 == target // 16) & (source % 12 == target % 16), jnp.bfloat16
    )
    low = jnp.bfloat16
    dma = pltpu.SemaphoreType.DMA
    blocks = [(part.shape[0] // 8, part.shape[1]) for part in expert_grads]
    buffers = [pltpu.VMEM((4,) + block, low) for block in blocks] * 2
    buffers += [pltpu.VMEM((3,) + block, low) for block in blocks]
    buffers += [pltpu.VMEM(block, low) for block in blocks] * 2
    for columns, orders in ((EARLY, EARLY_ORDERS), (PACK - EARLY, LATE_ORDERS)):
        buffers += [
            pltpu.VMEM((4, 2, 2, 2, 48, columns), low),
            pltpu.VMEM((4, 2, 2, 2, 48, columns // 2), low),
            pltpu.VMEM((48, columns // 4), low),
            pltpu.VMEM((4, 16, columns // 4), low),
            dma((3,)), dma((3,)), dma((27,)), dma((27,)), dma((3,)), dma((3,)),
        ]
        buffers += [
            pltpu.VMEM((3,) + landing_shape(order[: 2 - stage], columns // 2), low)
            for stage in range(3)
            for order in orders
        ]
    vmem = pl.BlockSpec(memory_space=pltpu.VMEM)
    anywhere = pl.BlockSpec(memory_space=pltpu.HBM)
    rows, width = tokens.shape
    head_rows = head_rows.reshape(SOURCES, rows // 2, HEADS_WIDE)
    head_kv = head_kv.reshape(SOURCES, rows, 2 * HEAD_SIZE)
    qkv_width = QUERY_HEAD_COUNT * HEAD_SIZE + 2 * KEY_VALUE_HEADS * HEAD_SIZE
    grad_input, out, late_out, *finals = pl.pallas_call(
        scatter_kernel,
        out_shape=[jax.ShapeDtypeStruct((rows, width), low)]
        + [jax.ShapeDtypeStruct((16, columns), low) for columns in (EARLY, PACK - EARLY)]
        + [jax.ShapeDtypeStruct(block, low) for block in blocks],
        in_specs=[vmem] * 10 + [anywhere] * 4,
        out_specs=[vmem] * 6,
        scratch_shapes=[
            pltpu.VMEM(head_rows.shape, low),
            pltpu.VMEM(head_kv.shape, low),
            pltpu.VMEM((rows, qkv_width), low),
            pltpu.VMEM((rows, width), jnp.float32),
            pltpu.VMEM((rows, width), low),
            dma((12,)), dma((12,)), dma((12,)), dma((9,)), dma((9,)), dma((3,)), dma((3,)),
            dma((2 * SOURCES,)), dma((2 * SOURCES,)), dma,
        ]
        + buffers,
        compiler_params=pltpu.CompilerParams(
            collective_id=2, has_side_effects=True, vmem_limit_bytes=62 * 2**20
        ),
        cost_estimate=pl.CostEstimate(
            flops=2 * rows * width * 6656, bytes_accessed=28 * 2**20, transcendentals=0
        ),
        name="scatter_sum",
    )(
        head_rows, head_kv, tokens, scales, grad_hidden, branch, attended, router_grad, gain_grad, split,
        packed.reshape(4, 2, 2, 2, 48, PACK), *expert_grads,
    )
    return grad_input, out[:12], late_out[:12], [final.astype(jnp.float32) for final in finals]


def contract_cols(left, right):
    return lax.dot_general(
        left, right, (((1,), (1,)), ((), ())), preferred_element_type=jnp.float32
    )


MAIN_ROWS = 32
REST_ROWS = 16
REST_WIDTH = 384
CAPACITY = 36
TILE = 512


def across(left, right):
    return lax.dot_general(
        left, right, (((1,), (1,)), ((), ())), preferred_element_type=jnp.float32
    )


def dot32(left, right):
    return jnp.dot(left, right, preferred_element_type=jnp.float32)


def tiles(extent, body):
    pl.loop(0, extent // TILE)(lambda n: body(pl.ds(pl.multiple_of(n * TILE, TILE), TILE)))


def ones_at(condition):
    return jnp.where(condition, 1.0, 0.0).astype(jnp.bfloat16)


def in_three(column, lanes):
    first = column.astype(jnp.bfloat16).astype(jnp.float32)
    second = (column - first).astype(jnp.bfloat16).astype(jnp.float32)
    third = column - first - second
    return jnp.where(lanes % 3 == 0, first, jnp.where(lanes % 3 == 1, second, third))


def unpack_tables():
    row = np.arange(4 * CAPACITY)[:, None]
    device, slot = row // CAPACITY, row % CAPACITY
    main = np.arange(4 * MAIN_ROWS)[None, :]
    from_main = (device == main // MAIN_ROWS) & (slot == main % MAIN_ROWS)
    rest = np.arange(4 * REST_ROWS)[None, :]
    from_rest = np.stack(
        [
            (device == rest // REST_ROWS)
            & ((rest // 4) % 4 == quarter)
            & (slot == MAIN_ROWS + rest % 4)
            for quarter in range(4)
        ]
    )
    from_gate = (device == rest // REST_ROWS) & (slot % REST_ROWS == rest % REST_ROWS)
    lane_mask = np.arange(128)[None, :] // 3 == slot // REST_ROWS
    return [
        jnp.asarray(table, jnp.bfloat16)
        for table in (from_main, from_main.T, from_rest, from_rest.transpose(0, 2, 1), from_gate, from_gate.T)
    ] + [jnp.asarray(lane_mask, jnp.float32)]


def place_rows(routes, axis):
    rows = routes[0].shape[axis]
    experts = lax.broadcasted_iota(jnp.int32, (rows, 128) if axis == 0 else (128, rows), 1 - axis)
    picked = [jnp.where(route == experts, 1.0, 0.0) for route in routes]
    both = (picked[0] + picked[1]).astype(jnp.bfloat16)
    first = lax.broadcasted_iota(jnp.int32, (rows, rows), 0)
    second = lax.broadcasted_iota(jnp.int32, (rows, rows), 1)
    if axis == 0:
        earlier = dot32(ones_at(second < first), both)
    else:
        earlier = dot32(both, ones_at(first < second))
    places = []
    for route, pick in zip(routes, picked):
        slot = jnp.sum(pick * earlier, axis=1 - axis, keepdims=True).astype(jnp.int32)
        whole = slot < MAIN_ROWS
        main = jnp.where(whole, route * MAIN_ROWS + slot, -1)
        rest = jnp.where(whole, -64, route * REST_ROWS + slot - MAIN_ROWS)
        block = jnp.where(slot < REST_ROWS, 0, jnp.where(whole, 1, 2))
        places.append((main, rest, route * REST_ROWS + slot - REST_ROWS * block, block))
    return places


def expert_routes(dp, ctx, send, recv):
    y, z_lo, core = dp // 2, dp % 2, ctx % 2
    expert = ctx // 2 * 2 + z_lo
    at_home = z_lo == core

    def holder(step):
        other = (ctx + step) % SOURCES
        return other, (2 * y + other % 2, other // 2 * 2 + z_lo)

    def sender(step):
        other = (expert + step) % SOURCES
        return other, (2 * y + core, other)

    def start(number, pick, slot, main, rest, main_in, rest_in):
        copies = []
        pairs = ((main, main_in), (rest, rest_in))

        def remote(step, which):
            other, device = pick(step)
            src, dst = pairs[which]
            at = (number * 2 + which) * SOURCES + step
            return pltpu.make_async_remote_copy(
                src_ref=src.at[other],
                dst_ref=dst.at[slot],
                send_sem=send.at[at],
                recv_sem=recv.at[at],
                device_id=device,
                device_id_type=MESH,
            )

        def local(which):
            src, dst = pairs[which]
            at = (number * 2 + which) * SOURCES
            return pltpu.make_async_copy(src.at[slot], dst.at[slot], recv.at[at])

        for step in range(1, SOURCES):
            for which in range(2):
                copy = remote(step, which)
                copy.start()
                copies.append(copy)

        @pl.when(at_home)
        def _():
            for which in range(2):
                local(which).start()

        @pl.when(jnp.logical_not(at_home))
        def _():
            for which in range(2):
                remote(0, which).start()

        def wait_recv():
            @pl.when(at_home)
            def _():
                for which in range(2):
                    local(which).wait()

            @pl.when(jnp.logical_not(at_home))
            def _():
                for which in range(2):
                    remote(0, which).wait_recv()

            for copy in copies:
                copy.wait_recv()

        def wait_send():
            @pl.when(jnp.logical_not(at_home))
            def _():
                for which in range(2):
                    remote(0, which).wait_send()

            for copy in copies:
                copy.wait_send()

        return wait_recv, wait_send

    return holder, sender, start


def pack(tables, source, main, rest):
    send_main, send_rest = tables
    main[...] = dot32(send_main[...], source[...]).astype(jnp.bfloat16).reshape(main.shape)
    total = jnp.zeros((SOURCES * REST_ROWS, REST_WIDTH), jnp.float32)
    for quarter in range(4):
        total += dot32(
            send_rest[quarter], source[:, quarter * REST_WIDTH : (quarter + 1) * REST_WIDTH]
        )
    rest[:, :, :REST_WIDTH] = (
        total.astype(jnp.bfloat16).reshape(SOURCES, REST_ROWS, REST_WIDTH)
    )


def fill_tables(routes_t, send_main, send_rest):
    rows = routes_t.shape[1]
    main_rows = lax.broadcasted_iota(jnp.int32, (SOURCES * MAIN_ROWS, rows), 0)
    rest_rows = lax.broadcasted_iota(jnp.int32, (SOURCES * REST_ROWS, rows), 0)
    places = place_rows([routes_t[c : c + 1, :] for c in range(TOP)], 1)
    send_main[...] = ones_at((main_rows == places[0][0]) | (main_rows == places[1][0]))
    for quarter in range(4):
        send_rest[quarter] = ones_at(
            (rest_rows == places[0][1] + 4 * quarter) | (rest_rows == places[1][1] + 4 * quarter)
        )
    return rest_rows, places


def middle_kernel(
    head_out, tokens, cotangent, c_main_in, c_rest_in, routes, routes_t, scale,
    from_main, to_main, from_rest, to_rest, from_gate, to_gate, lane_mask,
    packed_w, gate_src, up_src, down_src,
    attended, mixed, grad_hidden, grad_branch, router_grad, gain_grad, head_grads,
    gate_grad, up_grad, down_grad,
    gate_w, up_w, down_w, out_w, router_w,
    rows_in, head_send, hidden_one, normed, grad_normed,
    send_main, send_rest, send_gate, place_main, place_rest, place_gate,
    x_main, x_rest, c_main, c_rest, x_main_in, x_rest_in,
    d_main_in, d_rest_in, y_main_in, y_rest_in,
    rows_x, rows_c, gate_pre, up_pre, hidden, grad_gate_pre, grad_up_pre, rows_y, turned,
    weight_sem, out_sem, swap_send, swap_recv, send, recv,
):
    low, wide = jnp.bfloat16, jnp.float32
    dp, ctx = lax.axis_index("dp"), lax.axis_index("ctx")
    rows, width = tokens.shape
    half = rows // 2
    out_at = QUERY_HEAD_COUNT * HEAD_SIZE + 2 * KEY_VALUE_HEADS * HEAD_SIZE
    loads = [
        pltpu.make_async_copy(part, whole, weight_sem.at[n])
        for n, (part, whole) in enumerate(
            (
                (packed_w.at[:, pl.ds(out_at, width)], out_w),
                (packed_w.at[:, pl.ds(out_at + width, 128)], router_w),
                (gate_src, gate_w),
                (up_src, up_w),
                (down_src, down_w),
            )
        )
    ]
    for load in loads:
        load.start()
    z_lo, core = dp % 2, ctx % 2
    expert = ctx // 2 * 2 + z_lo
    holder, sender, start = expert_routes(dp, ctx, send, recv)

    def neighbour(step):
        other = (ctx + step) % SOURCES
        return other, (dp, other)

    barrier = pltpu.get_barrier_semaphore()
    for step in range(1, SOURCES):
        for pick in (neighbour, holder, sender):
            pl.semaphore_signal(barrier, inc=1, device_id=pick(step)[1], device_id_type=MESH)

    @pl.when(z_lo != core)
    def _():
        for pick in (holder, sender):
            pl.semaphore_signal(barrier, inc=1, device_id=pick(0)[1], device_id_type=MESH)

    def swap(number, source, place_in):
        copies = []
        for step in range(1, SOURCES):
            other, device = neighbour(step)
            at = number * SOURCES + step
            copy = pltpu.make_async_remote_copy(
                src_ref=source.at[other],
                dst_ref=place_in.at[ctx],
                send_sem=swap_send.at[at],
                recv_sem=swap_recv.at[at],
                device_id=device,
                device_id_type=MESH,
            )
            copy.start()
            copies.append(copy)
        place_in[ctx] = source[ctx]
        return copies

    def unpack(main_in, rest_in, out, group):
        at = pl.ds(4 * group, 4)
        main = main_in[at].reshape(4 * MAIN_ROWS, -1)
        rest = rest_in[at].reshape(4 * REST_ROWS, -1)
        for quarter in range(4):
            lanes = slice(quarter * REST_WIDTH, (quarter + 1) * REST_WIDTH)
            out[pl.ds(group * 4 * CAPACITY, 4 * CAPACITY), lanes] = (
                dot32(from_main[...], main[:, lanes])
                + dot32(from_rest[quarter], rest[:, :REST_WIDTH])
            ).astype(low)

    def repack(source, main, rest, group):
        at = pl.ds(4 * group, 4)
        block = source[pl.ds(group * 4 * CAPACITY, 4 * CAPACITY), :]
        main[at] = dot32(to_main[...], block).astype(low).reshape(4, MAIN_ROWS, -1)
        total = jnp.zeros((4 * REST_ROWS, REST_WIDTH), wide)
        for quarter in range(4):
            total += dot32(
                to_rest[quarter], block[:, quarter * REST_WIDTH : (quarter + 1) * REST_WIDTH]
            )
        rest[at, :, :REST_WIDTH] = total.astype(low).reshape(4, REST_ROWS, REST_WIDTH)

    pl.semaphore_wait(barrier, 3 * (SOURCES - 1) + 2 * ((z_lo + core) % 2))
    heads_in = swap(0, head_out, rows_in)

    rest_rows, places = fill_tables(routes_t, send_main, send_rest)
    for choice in range(TOP):
        send_gate[choice] = ones_at(rest_rows == places[choice][2])
    main_lanes = lax.broadcasted_iota(jnp.int32, (rows, SOURCES * MAIN_ROWS), 1)
    rest_lanes = lax.broadcasted_iota(jnp.int32, (rows, SOURCES * REST_ROWS), 1)
    lanes = lax.broadcasted_iota(jnp.int32, (rows, 128), 1)
    places = place_rows([routes[:, c : c + 1] for c in range(TOP)], 0)
    gate_lanes = []
    for choice, (main, rest, gate, block) in enumerate(places):
        place_main[choice] = ones_at(main_lanes == main)
        for quarter in range(4):
            place_rest[choice, quarter] = ones_at(rest_lanes == rest + 4 * quarter)
        place_gate[choice] = ones_at(rest_lanes == gate)
        gate_lanes.append(jnp.where((lanes >= 3 * block) & (lanes < 3 * block + 3), 1.0, 0.0))

    for load in loads:
        load.wait()
    for copy in heads_in:
        copy.wait_recv()
    for head in range(KEY_VALUE_HEADS):
        for part in range(2):
            attended[
                part * half : (part + 1) * half, head * HEADS_WIDE : (head + 1) * HEADS_WIDE
            ] = rows_in[2 * head + part]

    @functools.partial(tiles, width)
    def _(at):
        hidden_one[:, at] = tokens[:, at].astype(wide) + across(attended[...], out_w[at, :])

    inverse = lax.rsqrt(jnp.mean(hidden_one[...] * hidden_one[...], axis=1, keepdims=True) + EPSILON)
    normed[...] = (hidden_one[...] * inverse * scale[...]).astype(low)
    logits = dot32(normed[...], router_w[...])
    on_route = [lanes == routes[:, choice : choice + 1] for choice in range(TOP)]
    chosen = [jnp.sum(jnp.where(on, logits, 0.0), axis=1, keepdims=True) for on in on_route]
    highest = jnp.maximum(chosen[0], chosen[1])
    powers = [jnp.exp(value - highest) for value in chosen]
    gates = [power / (powers[0] + powers[1]) for power in powers]

    pack((send_main, send_rest), normed, x_main, x_rest)
    total = jnp.zeros((SOURCES * REST_ROWS, 128), wide)
    for choice in range(TOP):
        carried = in_three(gates[choice], lanes) * gate_lanes[choice]
        total += dot32(send_gate[choice], carried.astype(low))
    x_rest[:, :, REST_WIDTH:] = total.astype(low).reshape(SOURCES, REST_ROWS, 128)
    flights = start(0, holder, ctx, x_main, x_rest, x_main_in, x_rest_in)

    flights[0]()
    for group in range(4):
        unpack(x_main_in, x_rest_in, rows_x, group)

    @functools.partial(tiles, gate_w.shape[1])
    def _(at):
        gate = dot32(rows_x[...], gate_w[:, at])
        up = dot32(rows_x[...], up_w[:, at])
        gate_pre[:, at] = gate
        up_pre[:, at] = up
        hidden[:, at] = (gate / (1.0 + jnp.exp(-gate)) * up).astype(low)

    @functools.partial(tiles, width)
    def _(at):
        rows_y[:, at] = dot32(hidden[...], down_w[:, at]).astype(low)

    for group in range(4):
        repack(rows_y, c_main, c_rest, group)
    flights_y = start(3, sender, expert, c_main, c_rest, y_main_in, y_rest_in)

    flights[1]()
    expert_lanes = lax.broadcasted_iota(jnp.int32, (4 * CAPACITY, 128), 1)
    for group in range(4):
        unpack(c_main_in, c_rest_in, rows_c, group)
        at = pl.ds(group * 4 * CAPACITY, 4 * CAPACITY)
        carried = x_rest_in[pl.ds(4 * group, 4), :, pl.ds(REST_WIDTH, 128)].reshape(4 * REST_ROWS, 128)
        gate = jnp.sum(dot32(from_gate[...], carried) * lane_mask[...], axis=1, keepdims=True)
        grad = rows_c[at, :].astype(wide)
        grad_gate = jnp.sum(grad * rows_y[at, :].astype(wide), axis=1, keepdims=True)
        rows_c[at, :] = (gate * grad).astype(low)
        held = (in_three(grad_gate, expert_lanes) * lane_mask[...]).astype(low)
        x_rest[pl.ds(4 * group, 4), :, pl.ds(REST_WIDTH, 128)] = (
            dot32(to_gate[...], held).astype(low).reshape(4, REST_ROWS, 128)
        )

    @functools.partial(tiles, down_w.shape[0])
    def _(at):
        grad_hidden_rows = across(rows_c[...], down_w[at, :])
        gate = gate_pre[:, at]
        sigmoid = 1.0 / (1.0 + jnp.exp(-gate))
        grad_gate_pre[:, at] = (
            grad_hidden_rows * up_pre[:, at] * sigmoid * (1.0 + gate * (1.0 - sigmoid))
        ).astype(low)
        grad_up_pre[:, at] = (grad_hidden_rows * gate * sigmoid).astype(low)

    @functools.partial(tiles, width)
    def _(at):
        rows_y[:, at] = (
            across(grad_gate_pre[...], gate_w[at, :]) + across(grad_up_pre[...], up_w[at, :])
        ).astype(low)

    for group in range(4):
        repack(rows_y, x_main, x_rest, group)
    flights_d = start(2, sender, expert, x_main, x_rest, d_main_in, d_rest_in)

    turned[...] = rows_x[...].T

    @functools.partial(tiles, gate_w.shape[1])
    def _(at):
        gate_w[:, at] = dot32(turned[...], grad_gate_pre[:, at]).astype(low)
        up_w[:, at] = dot32(turned[...], grad_up_pre[:, at]).astype(low)

    turned[pl.ds(0, hidden.shape[1]), :] = hidden[...].T

    @functools.partial(tiles, width)
    def _(at):
        down_w[:, at] = dot32(turned[pl.ds(0, hidden.shape[1]), :], rows_c[:, at]).astype(low)

    stores = [
        pltpu.make_async_copy(whole, grad, out_sem.at[n])
        for n, (whole, grad) in enumerate(
            ((gate_w, gate_grad), (up_w, up_grad), (down_w, down_grad))
        )
    ]
    for store in stores:
        store.start()

    flights_d[0]()
    main = d_main_in[...].reshape(SOURCES * MAIN_ROWS, -1)
    rest = d_rest_in[...].reshape(SOURCES * REST_ROWS, -1)
    grad_gates = [
        jnp.sum(
            dot32(place_gate[choice], rest[:, REST_WIDTH:]) * gate_lanes[choice],
            axis=1,
            keepdims=True,
        )
        for choice in range(TOP)
    ]
    mean = gates[0] * grad_gates[0] + gates[1] * grad_gates[1]
    grad_logits = jnp.zeros((rows, 128), wide)
    for choice in range(TOP):
        grad_logits += jnp.where(
            on_route[choice], gates[choice] * (grad_gates[choice] - mean), 0.0
        )
    grad_logits = grad_logits.astype(low)
    for quarter in range(4):
        at = slice(quarter * REST_WIDTH, (quarter + 1) * REST_WIDTH)
        grad_normed[:, at] = (
            dot32(place_main[0] + place_main[1], main[:, at])
            + dot32(place_rest[0, quarter] + place_rest[1, quarter], rest[:, :REST_WIDTH])
            + across(grad_logits, router_w[at, :])
        )
    unit = hidden_one[...] * inverse
    grads = grad_normed[...]
    gain_grad[...] = jnp.sum(grads * unit, axis=0, keepdims=True)
    grads = grads * scale[...]
    grads = inverse * (grads - unit * jnp.mean(grads * unit, axis=1, keepdims=True))
    grad_hidden[...] = grads + cotangent[...].astype(wide)
    grad_branch[...] = grad_hidden[...].astype(low)

    @functools.partial(tiles, width)
    def _(at):
        grad_normed[:, at] = dot32(grad_branch[...], out_w[:, at])

    for head in range(KEY_VALUE_HEADS):
        for part in range(2):
            head_send[2 * head + part] = grad_normed[
                part * half : (part + 1) * half, head * HEADS_WIDE : (head + 1) * HEADS_WIDE
            ].astype(low)
    grads_in = swap(1, head_send, head_grads)
    router_grad[...] = dot32(normed[...].T, grad_logits).astype(low)

    flights_y[0]()
    main = y_main_in[...].reshape(SOURCES * MAIN_ROWS, -1)
    rest = y_rest_in[...].reshape(SOURCES * REST_ROWS, -1)
    for quarter in range(4):
        at = slice(quarter * REST_WIDTH, (quarter + 1) * REST_WIDTH)
        total = hidden_one[:, at]
        for choice in range(TOP):
            total += gates[choice] * (
                dot32(place_main[choice], main[:, at])
                + dot32(place_rest[choice, quarter], rest[:, :REST_WIDTH])
            )
        mixed[:, at] = total.astype(low)
    for copy in grads_in:
        copy.wait_recv()
    for copy in heads_in + grads_in:
        copy.wait_send()
    flights_d[1]()
    flights_y[1]()
    for copy in stores:
        copy.wait()


def run_middle(head_out, tokens, cotangent, cotangent_rows, routes, scale, packed, weights):
    rows, width = tokens.shape
    half = rows // 2
    hidden_width = weights[0].shape[-1]
    low, wide = jnp.bfloat16, jnp.float32
    count = SOURCES * CAPACITY
    vmem = pl.BlockSpec(memory_space=pltpu.VMEM)
    anywhere = pl.BlockSpec(memory_space=pltpu.HBM)
    main = pltpu.VMEM((SOURCES, MAIN_ROWS, width), low)
    long_rest = pltpu.VMEM((SOURCES, REST_ROWS, REST_WIDTH + 128), low)
    rest = pltpu.VMEM((SOURCES, REST_ROWS, REST_WIDTH), low)
    heads = pltpu.VMEM((SOURCES, half, HEADS_WIDE), low)
    dma = pltpu.SemaphoreType.DMA
    return pl.pallas_call(
        middle_kernel,
        out_shape=(
            jax.ShapeDtypeStruct((rows, width), low),
            jax.ShapeDtypeStruct((rows, width), low),
            jax.ShapeDtypeStruct((rows, width), wide),
            jax.ShapeDtypeStruct((rows, width), low),
            jax.ShapeDtypeStruct((width, 128), low),
            jax.ShapeDtypeStruct((1, width), wide),
            jax.ShapeDtypeStruct((SOURCES, half, HEADS_WIDE), low),
            jax.ShapeDtypeStruct((width, hidden_width), low),
            jax.ShapeDtypeStruct((width, hidden_width), low),
            jax.ShapeDtypeStruct((hidden_width, width), low),
        ),
        in_specs=[vmem] * 15 + [anywhere] * 4,
        out_specs=[vmem] * 7 + [anywhere] * 3,
        scratch_shapes=[
            pltpu.VMEM((width, hidden_width), low),
            pltpu.VMEM((width, hidden_width), low),
            pltpu.VMEM((hidden_width, width), low),
            pltpu.VMEM((width, width), low),
            pltpu.VMEM((width, 128), low),
            heads,
            heads,
            pltpu.VMEM((rows, width), wide),
            pltpu.VMEM((rows, width), low),
            pltpu.VMEM((rows, width), wide),

            pltpu.VMEM((SOURCES * MAIN_ROWS, rows), low),
            pltpu.VMEM((4, SOURCES * REST_ROWS, rows), low),
            pltpu.VMEM((TOP, SOURCES * REST_ROWS, rows), low),
            pltpu.VMEM((TOP, rows, SOURCES * MAIN_ROWS), low),
            pltpu.VMEM((TOP, 4, rows, SOURCES * REST_ROWS), low),
            pltpu.VMEM((TOP, rows, SOURCES * REST_ROWS), low),
            main, long_rest, main, rest, main, long_rest, main, long_rest, main, rest,
            pltpu.VMEM((count, width), low),
            pltpu.VMEM((count, width), low),
            pltpu.VMEM((count, hidden_width), wide),
            pltpu.VMEM((count, hidden_width), wide),
            pltpu.VMEM((count, hidden_width), low),
            pltpu.VMEM((count, hidden_width), low),
            pltpu.VMEM((count, hidden_width), low),
            pltpu.VMEM((count, width), low),
            pltpu.VMEM((width, count), low),
            dma((5,)), dma((3,)), dma((2 * SOURCES,)), dma((2 * SOURCES,)),
            dma((8 * SOURCES,)), dma((8 * SOURCES,)),
        ],
        compiler_params=pltpu.CompilerParams(
            collective_id=3, has_side_effects=True, vmem_limit_bytes=62 * 2**20
        ),
        cost_estimate=pl.CostEstimate(
            flops=18 * count * width * hidden_width, bytes_accessed=40 * 2**20, transcendentals=0
        ),
        name="run_middle",
    )(
        head_out.reshape(SOURCES, half, HEADS_WIDE), tokens, cotangent, *cotangent_rows, routes, routes.T,
        scale[None, :],
        *unpack_tables(), packed, *weights,
    )


KEY_STEP, QUERY_STEP = 512, 128
BACK_KEY_STEP, BACK_QUERY_STEP = 256, 256


def allowed_block(block, pos, start, key_step):
    keys = lax.broadcasted_iota(jnp.int32, (key_step, pos.shape[1]), 0) + block * key_step
    return (keys <= pos) & (keys >= start)


def attend_kernel(low, high, pos_ref, start_ref, query_ref, kv_ref, kvt_ref, out_ref, outt_ref, log_ref):
    zeros = jnp.zeros((QUERY_STEP, HEAD_SIZE), jnp.bfloat16)

    @pl.loop(0, query_ref.shape[0] // QUERY_STEP)
    def _(tile):
        rows = pl.ds(pl.multiple_of(tile * QUERY_STEP, QUERY_STEP), QUERY_STEP)
        pos, start = pos_ref[:, rows], start_ref[:, rows]
        queries = query_ref[rows, :]
        padded = [
            jnp.concatenate([queries[:, h * HEAD_SIZE : (h + 1) * HEAD_SIZE], zeros], axis=1)
            for h in range(GROUP)
        ]

        def step(block, carry):
            keys = pl.ds(pl.multiple_of(block * KEY_STEP, KEY_STEP), KEY_STEP)
            kv = kv_ref[keys, :]
            values_t = kvt_ref[HEAD_SIZE:, keys]
            allowed = allowed_block(block, pos, start, KEY_STEP)
            new = []
            for h in range(GROUP):
                highest, total, summed = carry[h]
                scores = jnp.where(allowed, across(kv, padded[h]), NEGATIVE)
                new_high = jnp.maximum(highest, jnp.max(scores, axis=0, keepdims=True))
                weights = jnp.exp(scores - new_high)
                shrink = jnp.exp(highest - new_high)
                total = total * shrink + jnp.sum(weights, axis=0, keepdims=True)
                summed = summed * shrink + dot32(values_t, weights.astype(jnp.bfloat16))
                new.append((new_high, total, summed))
            return tuple(new)

        first = tuple(
            (
                jnp.full((1, QUERY_STEP), NEGATIVE, jnp.float32),
                jnp.zeros((1, QUERY_STEP), jnp.float32),
                jnp.zeros((HEAD_SIZE, QUERY_STEP), jnp.float32),
            )
            for _ in range(GROUP)
        )
        last = lax.fori_loop(low[tile], high[tile], step, first)
        pieces = []
        for h in range(GROUP):
            highest, total, summed = last[h]
            log_ref[h : h + 1, rows] = highest + jnp.log(total)
            summed = summed / total
            outt_ref[h, :, rows] = summed
            pieces.append(summed)
        out_ref[rows, :] = jnp.concatenate(pieces, axis=0).T.astype(jnp.bfloat16)


def attend_back_kernel(
    low, high, pos_ref, start_ref, query_ref, kv_ref, kvt_ref, outt_ref, log_ref, grad_ref,
    grad_query_ref, grad_kv_ref, sums,
):
    zeros = jnp.zeros((BACK_QUERY_STEP, HEAD_SIZE), jnp.bfloat16)
    sums[...] = jnp.zeros_like(sums)

    @pl.loop(0, query_ref.shape[0] // BACK_QUERY_STEP)
    def _(tile):
        rows = pl.ds(pl.multiple_of(tile * BACK_QUERY_STEP, BACK_QUERY_STEP), BACK_QUERY_STEP)
        pos, start = pos_ref[:, rows], start_ref[:, rows]
        queries, grads = query_ref[rows, :], grad_ref[rows, :]
        grads_t = grads.astype(jnp.float32).T
        query_pads, grad_pads, deltas, logs = [], [], [], []
        for h in range(GROUP):
            part = slice(h * HEAD_SIZE, (h + 1) * HEAD_SIZE)
            query_pads.append(jnp.concatenate([queries[:, part], zeros], axis=1))
            grad_pads.append(jnp.concatenate([zeros, grads[:, part]], axis=1))
            deltas.append(jnp.sum(grads_t[part, :] * outt_ref[h, :, rows], axis=0, keepdims=True))
            logs.append(log_ref[h : h + 1, rows])

        def step(block, carry):
            keys = pl.ds(pl.multiple_of(block * BACK_KEY_STEP, BACK_KEY_STEP), BACK_KEY_STEP)
            kv = kv_ref[keys, :]
            keys_t = kvt_ref[:HEAD_SIZE, keys]
            allowed = allowed_block(block, pos, start, BACK_KEY_STEP)
            new = []
            total = sums[keys, :]
            for h in range(GROUP):
                scores = jnp.where(allowed, across(kv, query_pads[h]), NEGATIVE)
                probs = jnp.exp(scores - logs[h])
                grad_probs = across(kv, grad_pads[h])
                grad_scores = (probs * (grad_probs - deltas[h])).astype(jnp.bfloat16)
                total += dot32(probs.astype(jnp.bfloat16), grad_pads[h])
                total += dot32(grad_scores, query_pads[h])
                new.append(carry[h] + dot32(keys_t, grad_scores))
            sums[keys, :] = total
            return tuple(new)

        first = tuple(jnp.zeros((HEAD_SIZE, BACK_QUERY_STEP), jnp.float32) for _ in range(GROUP))
        last = lax.fori_loop(low[tile], high[tile], step, first)
        factor = HEAD_SIZE ** (-0.5)
        grad_query_ref[rows, :] = (jnp.concatenate(last, axis=0) * factor).T.astype(jnp.bfloat16)

    grad_kv_ref[...] = sums[...].astype(jnp.bfloat16)


def attend_call(kernel, name, bounds, arrays, out_shape, scratch, matmuls, area):
    vmem = pl.BlockSpec(memory_space=pltpu.VMEM)
    return pl.pallas_call(
        kernel,
        out_shape=out_shape,
        grid_spec=pltpu.PrefetchScalarGridSpec(
            num_scalar_prefetch=2,
            grid=(1,),
            in_specs=[vmem] * len(arrays),
            out_specs=[vmem] * len(out_shape),
            scratch_shapes=scratch,
        ),
        compiler_params=pltpu.CompilerParams(vmem_limit_bytes=32 * 2**20),
        cost_estimate=pl.CostEstimate(
            flops=matmuls * 2 * HEAD_SIZE * area, bytes_accessed=8 * 2**20, transcendentals=area
        ),
        name=name,
    )(*bounds, *arrays)


def shards(
    tokens,
    segments,
    routes,
    gain_attn,
    w_query,
    key_weight,
    value_weight,
    w_out,
    w_router,
    gain_ffn,
    w_gate,
    w_up,
    w_down,
    cotangent,
):
    low = jnp.bfloat16
    wide = jnp.float32
    device_rows, width = tokens.shape
    sequence = segments.shape[0]
    half = device_rows // 2
    core = lax.axis_index("ctx") % 2
    ctx_count = lax.axis_size("ctx")
    shard = jnp.concatenate(
        [w_query, key_weight, value_weight, w_out, w_router, gain_attn[:, None], gain_ffn[:, None]], axis=1
    )
    shard = jnp.pad(shard, ((0, 0), (0, PACK - shard.shape[1])))
    packed, expert_weights, head_queries, head_kv, scales, *cotangent_rows = gather_weights(
        shard, tokens, cotangent, routes, w_gate[0], w_up[0], w_down[0]
    )
    head_queries = head_queries.reshape(-1, HEADS_WIDE)
    head_kv = head_kv.reshape(sequence, 2 * HEAD_SIZE)
    order = jnp.arange(ctx_count * half, dtype=jnp.int32)
    query_pos = (order // half) * device_rows + core * half + order % half
    first_of = jnp.sum(
        (segments[:, None] < jnp.arange(5, dtype=jnp.int32)[None, :]).astype(jnp.int32), axis=0
    )
    starts = jnp.sum(
        jnp.where(segments[:, None] == jnp.arange(5, dtype=jnp.int32)[None, :], first_of[None, :], 0),
        axis=1,
    )
    query_start = lax.dynamic_slice_in_dim(
        starts.reshape(ctx_count, device_rows), core * half, half, axis=1
    ).reshape(-1)

    def bounds_of(query_step, key_step):
        return (
            query_start.reshape(-1, query_step)[:, 0] // key_step,
            query_pos.reshape(-1, query_step)[:, -1] // key_step + 1,
        )

    mask_rows = (query_pos[None, :], query_start[None, :])

    head_kvt = head_kv.T
    count = head_queries.shape[0]
    area = GROUP * count * sequence // 3
    head_out, head_outt, log_total = attend_call(
        attend_kernel,
        "attend",
        bounds_of(QUERY_STEP, KEY_STEP),
        (*mask_rows, head_queries, head_kv, head_kvt),
        (
            jax.ShapeDtypeStruct((count, HEADS_WIDE), low),
            jax.ShapeDtypeStruct((GROUP, HEAD_SIZE, count), wide),
            jax.ShapeDtypeStruct((GROUP, count), wide),
        ),
        [],
        2,
        area,
    )
    (
        attended, mixed, grad_hidden_one, grad_branch, grad_router_full, grad_gain_two, head_grads,
        *expert_grads,
    ) = run_middle(
        head_out, tokens, cotangent, cotangent_rows, routes, scales[1], packed, expert_weights
    )
    head_grads = head_grads.reshape(-1, HEADS_WIDE)

    head_grad_queries, head_grad_kv = attend_call(
        attend_back_kernel,
        "attend_back",
        bounds_of(BACK_QUERY_STEP, BACK_KEY_STEP),
        (*mask_rows, head_queries, head_kv, head_kvt, head_outt, log_total, head_grads),
        (
            jax.ShapeDtypeStruct((count, HEADS_WIDE), low),
            jax.ShapeDtypeStruct((sequence, 2 * HEAD_SIZE), low),
        ),
        [pltpu.VMEM((sequence, 2 * HEAD_SIZE), wide)],
        5,
        area,
    )
    grad_input, out_share, share, (grad_gate, grad_up, grad_down) = scatter_sum(
        head_grad_queries, head_grad_kv, tokens, scales, grad_hidden_one, grad_branch, attended,
        grad_router_full, grad_gain_two, packed, expert_grads,
    )
    share, out_share = share.astype(wide), out_share.astype(wide)
    return (
        mixed,
        grad_input,
        share[:, 2576],
        share[:, :1536],
        share[:, 1536:2048],
        share[:, 2048:2560],
        out_share,
        share[:, 2560:2576],
        share[:, 2577],
        grad_gate[None],
        grad_up[None],
        grad_down[None],
    )


def solution(mesh):
    in_specs = (
        P(("dp", "ctx"), None),
        P("dp"),
        P(("dp", "ctx"), None),
        P(("dp", "ctx")),
        P(("dp", "ctx"), None),
        P(("dp", "ctx"), None),
        P(("dp", "ctx"), None),
        P(("dp", "ctx"), None),
        P(("dp", "ctx"), None),
        P(("dp", "ctx")),
        P("ctx", "dp", None),
        P("ctx", "dp", None),
        P("ctx", "dp", None),
        P(("dp", "ctx"), None),
    )
    out_specs = (
        P(("dp", "ctx"), None),
        P(("dp", "ctx"), None),
        P(("dp", "ctx")),
        P(("dp", "ctx"), None),
        P(("dp", "ctx"), None),
        P(("dp", "ctx"), None),
        P(("dp", "ctx"), None),
        P(("dp", "ctx"), None),
        P(("dp", "ctx")),
        P("ctx", "dp", None),
        P("ctx", "dp", None),
        P("ctx", "dp", None),
    )
    return jax.shard_map(shards, mesh=mesh, in_specs=in_specs, out_specs=out_specs, check_vma=False)
```
